256 devices in a mesh: dp: 128 (over y, x, z), mp: 2 (over core).
Axes of the slice: x: 4, y: 4, z: 8, core: 2. Of those that a mesh axis runs over, the one named last changes fastest.
Arguments:
- query_states: bfloat16 [4096, 4096], P('dp')
- passage_states: bfloat16 [32768, 4096], P('dp')
- head_weight: bfloat16 [4096, 2048], P(None, 'mp'), may hold values from -0.09375 to 0.09375
- positives: int32 [4096], P('dp'), may hold values from 0 to 32767, as said below
- negatives: int32 [4096, 8], P('dp'), may hold values from 0 to 32767, as said below
- search_cost_incoming_slope: float32 [4096], P('dp'), may hold values from 20 to 200
Outputs:
- losses: float32 [4096], P('dp')
- query_grads: bfloat16 [4096, 4096], P('dp', 'mp')
- passage_grads: bfloat16 [32768, 4096], P('dp', 'mp')
The draws below stay inside these ranges and needn't reach their ends.
Inputs may be any that keep to these rules, and one draw needn't show every extreme that they name: `positives`: the queries of one aligned block of 32 rows name, over their positive and hard negatives together, at most 4 passages of any one aligned block of 256 passages (repeats counted); in every draw one block of passages is named exactly 4 times by the queries of every block. `negatives`: see positives: the bound counts both arguments together.
All inputs are finite; a program needn't handle non-finite values.
Results may differ from the reference program's by a relative error of at most 0.015.
Values may be sent and summed in bfloat16 or wider, within the bound.
No kernel may reach another device: no remote copies, remote signals or barrier semaphores. Data moves between devices by JAX's collectives and lax.ppermute only.
A program may use at most 128 MiB of HBM per device.

```python
import math
import jax
import jax.numpy as jnp
from jax import lax

D = 4096
E = 2048
NEG = 8
Q_DEV = 32
P_DEV = 256
QUERIES = 4096
PASSAGES = 32768
PASSAGE_LIMIT = 4
N_DP = 128


passage_common = 0.65


query_common = 2.86


query_noise = 3.8


def passage_lists(key):
    key = jax.random.fold_in(key, 11)
    rank_key, pick_key, row_key, order_key = jax.random.split(key, 4)
    owner_ranks = jax.random.permutation(rank_key, N_DP)
    popular_count = max(1, N_DP // 16)
    requests = Q_DEV * (NEG + 1)
    slot_owner = jnp.arange(N_DP * PASSAGE_LIMIT) // PASSAGE_LIMIT
    entry_ranking = owner_ranks[slot_owner]
    holder_offset = jnp.where(entry_ranking == 0, -4 * N_DP * PASSAGE_LIMIT, jnp.where(entry_ranking < popular_count, -2 * N_DP * PASSAGE_LIMIT, 0))

    def one_device(device_random_key):
        entry_logits = jax.random.permutation(device_random_key, N_DP * PASSAGE_LIMIT) + holder_offset
        chosen = jnp.argsort(entry_logits, stable=True)[:requests]
        return slot_owner[chosen]
    owners = jax.vmap(one_device)(jax.random.split(pick_key, N_DP))
    local_rows = jax.random.randint(row_key, (N_DP, requests), 0, P_DEV)
    shuffled = jax.vmap(lambda sub_key: jax.random.permutation(sub_key, requests))(jax.random.split(order_key, N_DP))
    passage_ids = jnp.take_along_axis(owners * P_DEV + local_rows, shuffled, axis=1)
    return passage_ids.reshape(QUERIES, NEG + 1).astype(jnp.int32)


def shared_parts(key):
    identity_key = jax.random.fold_in(key, 41)
    common_row = jax.random.normal(jax.random.fold_in(key, 43), (1, D), jnp.float32)
    column_scale = jnp.exp(jax.random.uniform(jax.random.fold_in(key, 31), (1, D), jnp.float32, math.log(0.5), math.log(2.0)))
    return (identity_key, common_row, column_scale)


def identity_rows(identity_key, passage_ids):
    return jax.vmap(lambda passage_id: jax.random.normal(jax.random.fold_in(identity_key, passage_id), (D,), jnp.float32))(passage_ids)


def row_scales(key, count, spread):
    return jnp.exp(jax.random.uniform(key, (count, 1), jnp.float32, 0.0, math.log(spread)))


def draw_positives(key, part):
    return passage_lists(key)[:, 0]


def draw_negatives(key, part):
    return passage_lists(key)[:, 1:]


def draw_query_states(key, part):
    passage_ids = passage_lists(key)
    identity_key, common_row, column_scale = shared_parts(key)
    partner_key = jax.random.fold_in(key, 9)
    key = jax.random.fold_in(key, 5)
    weight_key, ratio_key, noise_key, scale_key = jax.random.split(key, 4)
    leading = jnp.exp(jax.random.uniform(weight_key, (QUERIES, 1), jnp.float32, math.log(0.8), math.log(1.25)))
    ratios = jax.random.uniform(ratio_key, (QUERIES, NEG + 1), jnp.float32, 0.55, 0.8)
    first_column = jnp.arange(NEG + 1)[None, :] == 0
    ratios = jnp.where(first_column, 1.0, ratios)
    signal = jnp.zeros((QUERIES, D), jnp.float32) + query_common * common_row
    for column in range(NEG + 1):
        signal = signal + leading * ratios[:, column:column + 1] * identity_rows(identity_key, passage_ids[:, column])
    partner_ids = jnp.roll(passage_ids[:, 0], -(QUERIES // 2))
    partner_ratio = jax.random.uniform(partner_key, (QUERIES, 1), jnp.float32, 0.55, 0.8)
    signal = signal + leading * partner_ratio * identity_rows(identity_key, partner_ids)
    noise_part = jax.random.normal(noise_key, (QUERIES, D), jnp.float32)
    row_scale = row_scales(scale_key, QUERIES, 10.0)
    return ((signal + query_noise * noise_part) * row_scale * column_scale).astype(jnp.bfloat16)


def draw_passage_states(key, part):
    identity_key, common_row, column_scale = shared_parts(key)
    key = jax.random.fold_in(key, 7)
    identities = identity_rows(identity_key, jnp.arange(PASSAGES))
    row_scale = row_scales(key, PASSAGES, 10.0)
    return ((identities + passage_common * common_row) * row_scale * column_scale).astype(jnp.bfloat16)


def level_of(key, shape, pieces, low, largest):
    def one(axis_at, shards_of):
        draws = jax.random.uniform(jax.random.fold_in(jax.random.fold_in(key, 6), axis_at), (shards_of,), jnp.float32, low / len(pieces), largest / len(pieces))
        return jnp.repeat(jnp.exp(draws), shape[axis_at] // shards_of).reshape((-1,) + (1,) * (len(shape) - axis_at - 1))

    level = one(*pieces[0])
    for cut in pieces[1:]:
        level = level * one(*cut)
    return level


def centred(own_key, shape, scale, reach, pieces=(), dtype=jnp.bfloat16):
    loudness = level_of(own_key, shape, pieces, -0.22, 0.18) if pieces else 1.0
    entries = jax.random.normal(own_key, shape, jnp.float32) * scale * loudness
    return jnp.minimum(jnp.maximum(entries, -reach), reach).astype(dtype)


def setup_inputs(seed: int = 0) -> dict:
    streams_of = jax.random.split(jax.random.key(seed), 7)
    query_states = draw_query_states(jax.random.fold_in(streams_of[6], 71), 0)
    passage_states = draw_passage_states(jax.random.fold_in(streams_of[6], 71), 0)
    head_weight = centred(streams_of[2], (D, E), D ** -0.5, 0.09375, ((1, 2),))
    positives = draw_positives(jax.random.fold_in(streams_of[6], 71), 0)
    negatives = draw_negatives(jax.random.fold_in(streams_of[6], 71), 0)
    search_cost_incoming_slope = jnp.clip(jnp.exp(math.log(200.0) - 2.3025851 * jax.random.uniform(streams_of[5], (QUERIES,), jnp.float32) ** level_of(streams_of[5], (QUERIES,), ((0, 128),), -0.2, 0.2)), 20.0, 200.0)
    return dict(query_states=query_states, passage_states=passage_states, head_weight=head_weight, positives=positives, negatives=negatives, search_cost_incoming_slope=search_cost_incoming_slope)


sharpness_divisor = 0.02

def normalize(states, weight):
    projected = jnp.dot(states, weight, preferred_element_type=jnp.float32)
    inv_norm = lax.rsqrt(lax.optimization_barrier(jnp.sum(projected * projected, axis=1, keepdims=True)) + 1e-06)
    return (projected * inv_norm, inv_norm)

def tangent(unit_rows, inv_norm, upstream):
    radial = lax.optimization_barrier(jnp.sum(unit_rows * upstream, axis=1, keepdims=True))
    return (inv_norm * (upstream - unit_rows * radial)).astype(jnp.bfloat16)

def reference(query_states, passage_states, head_weight, positives, negatives, search_cost_incoming_slope):
    q_unit, q_inv = normalize(query_states, head_weight)
    p_unit, p_inv = normalize(passage_states, head_weight)
    search_embedding_matrix = q_unit.astype(jnp.bfloat16)
    p_embed = p_unit.astype(jnp.bfloat16)
    matching_document_matrix = p_embed[positives]
    distractor_embedding_matrix = p_embed[negatives]
    sibling_document_similarity = jnp.dot(search_embedding_matrix, matching_document_matrix.T, preferred_element_type=jnp.float32) / sharpness_divisor
    fetched_distractor_similarity = jnp.einsum('bm,bgm->bg', search_embedding_matrix.astype(jnp.float32), distractor_embedding_matrix.astype(jnp.float32), precision=lax.Precision.HIGHEST) / sharpness_divisor
    log_total = jnp.log(lax.optimization_barrier(jnp.sum(jnp.exp(sibling_document_similarity), axis=1)) + lax.optimization_barrier(jnp.sum(jnp.exp(fetched_distractor_similarity), axis=1)))
    losses = log_total - jnp.diagonal(sibling_document_similarity)
    indices = jnp.arange(QUERIES)
    self_match_filter = (indices[:, None] == indices[None, :]).astype(jnp.float32)
    sibling_document_likelihood = jnp.exp(sibling_document_similarity - log_total[:, None])
    fetched_distractor_likelihood = jnp.exp(fetched_distractor_similarity - log_total[:, None])
    sibling_document_slope = (search_cost_incoming_slope[:, None] * (sibling_document_likelihood - self_match_filter) / sharpness_divisor).astype(jnp.bfloat16)
    fetched_distractor_slope = search_cost_incoming_slope[:, None] * fetched_distractor_likelihood / sharpness_divisor
    q_grad = jnp.dot(sibling_document_slope, matching_document_matrix, preferred_element_type=jnp.float32)
    q_grad = q_grad + jnp.einsum('qk,qke->qe', fetched_distractor_slope, distractor_embedding_matrix.astype(jnp.float32), precision=lax.Precision.HIGHEST)
    pos_grad = lax.dot_general(sibling_document_slope, search_embedding_matrix, (((0,), (0,)), ((), ())), preferred_element_type=jnp.float32)
    neg_grad = fetched_distractor_slope[:, :, None] * search_embedding_matrix.astype(jnp.float32)[:, None, :]
    p_grad = jnp.zeros((PASSAGES, E), jnp.float32)
    p_grad = p_grad.at[positives].add(pos_grad)
    p_grad = p_grad.at[negatives.reshape(-1)].add(neg_grad.reshape(-1, E))
    q_dir = tangent(q_unit, q_inv, q_grad)
    p_dir = tangent(p_unit, p_inv, p_grad)
    dims = (((1,), (1,)), ((), ()))
    query_grads = lax.dot_general(q_dir, head_weight, dims, preferred_element_type=jnp.float32).astype(jnp.bfloat16)
    passage_grads = lax.dot_general(p_dir, head_weight, dims, preferred_element_type=jnp.float32).astype(jnp.bfloat16)
    return (losses, query_grads, passage_grads)
```

```python
import jax
import jax.numpy as jnp
from jax import lax
from jax.sharding import Mesh, PartitionSpec as P

sharpness_divisor = 0.02
bf16 = jnp.bfloat16
f32 = jnp.float32
AUX = 128


def shifted(value, axis, shift):
    n = lax.axis_size(axis)
    return lax.ppermute(value, axis, [(i, (i + shift) % n) for i in range(n)])


def gather_slots(value, axis):
    return [value] + [shifted(value, axis, s) for s in range(1, lax.axis_size(axis))]


def return_slots(parts, axis):
    return [parts[0]] + [shifted(parts[s], axis, -s) for s in range(1, lax.axis_size(axis))]


def split_three(value):
    high = lax.reduce_precision(value, 8, 7)
    rest = value - high
    middle = lax.reduce_precision(rest, 8, 7)
    return high, middle, rest - middle


def contract(a, b, dims):
    return lax.dot_general(a, b, (dims, ((), ())), preferred_element_type=f32)


def per_device(query_states, passage_states, head_weight, positives, negatives, slope):
    n_y, n_x, n_z = (lax.axis_size(a) for a in ("y", "x", "z"))
    y, x, z, core = (lax.axis_index(a) for a in ("y", "x", "z", "mp"))
    q_rows, p_rows = query_states.shape[0], passage_states.shape[0]
    width = head_weight.shape[1]
    half = q_rows // 2

    def own_first(rows):
        return jnp.where(core == 0, rows, jnp.roll(rows, half, axis=0))

    q_proj = contract(query_states, head_weight, ((1,), (0,)))
    p_proj = contract(passage_states, head_weight, ((1,), (0,)))
    q_square, p_square = lax.psum(
        (jnp.sum(q_proj * q_proj, axis=1), jnp.sum(p_proj * p_proj, axis=1)), "mp"
    )
    q_inv = lax.rsqrt(q_square + 1e-06)[:, None]
    p_inv = lax.rsqrt(p_square + 1e-06)[:, None]
    q_unit = q_proj * q_inv
    p_unit = p_proj * p_inv
    p_embed = p_unit.astype(bf16)

    ids = jnp.concatenate([positives[:, None], negatives], axis=1)
    aux = jnp.concatenate(
        [(ids // 256).astype(f32), (ids % 256).astype(f32)]
        + [part[:, None] for part in split_three(slope)],
        axis=1,
    )
    per_query = ids.shape[1]
    aux = jnp.pad(aux, ((0, 0), (0, AUX - aux.shape[1])))
    message = own_first(jnp.concatenate([q_unit, aux], axis=1).astype(bf16))

    p_slots = gather_slots(p_embed, "y")
    q_z = jnp.concatenate(gather_slots(message, "z"), axis=0)
    q_all = jnp.concatenate(gather_slots(q_z, "x"), axis=0)
    slots = n_x * n_z
    q_all = q_all.reshape(slots, 2, half, width + AUX)
    q_own = q_all[:, 0, :, :width].reshape(slots * half, width)
    q_other = q_all[:, 1, :, :width].reshape(slots * half, width)
    p_all = jnp.concatenate(p_slots, axis=0)
    passages = p_all.shape[0]

    info = q_all[..., width:].astype(f32)
    id_all = info[..., :per_query] * 256.0 + info[..., per_query : 2 * per_query]
    id_own = id_all[:, 0].reshape(slots * half, per_query)
    base = 2 * per_query
    slope_own = (info[:, 0, :, base] + info[:, 0, :, base + 1]) + info[:, 0, :, base + 2]
    slope_own = slope_own.reshape(slots * half)

    row = jnp.arange(passages)
    row_y = (y - row // p_rows + n_y) % n_y
    row_id = (((row_y * n_x + x) * n_z + z) * p_rows + row % p_rows).astype(f32)
    named = (id_all[..., 0].reshape(-1)[:, None] == row_id[None, :]).astype(f32)
    count = jnp.sum(named, axis=0).reshape(n_y, p_rows)
    total_count = count
    for s in range(1, n_y):
        total_count = total_count + shifted(jnp.roll(count, s, axis=0), "y", s)
    total_count = total_count.reshape(passages)

    score_other = contract(q_other, p_all, ((1,), (1,)))
    score_own = contract(q_own, p_all, ((1,), (1,)))
    scores = (score_own + shifted(score_other, "mp", 1)) / sharpness_divisor
    match = id_own[:, :1] == row_id[None, :]
    weight = total_count[None, :] + sum(
        (id_own[:, k : k + 1] == row_id[None, :]).astype(f32) for k in range(1, per_query)
    )
    weighted = weight * jnp.exp(scores)
    sums = jnp.stack(
        [jnp.sum(weighted, axis=1), jnp.sum(jnp.where(match, scores, 0.0), axis=1)]
    ).reshape(2, n_x, n_z, half)

    def summed(value, axis, dim):
        total = value
        for s in range(1, lax.axis_size(axis)):
            total = total + shifted(jnp.roll(value, s, axis=dim), axis, s)
        return total

    sums = summed(summed(sums, "z", 2), "x", 1)
    own_loss = jnp.log(sums[0, 0, 0]) - sums[1, 0, 0]
    losses = own_first(jnp.concatenate([own_loss, shifted(own_loss, "mp", 1)]))
    total = sums[0].reshape(slots * half)

    grad_own = (
        (slope_own / sharpness_divisor)[:, None]
        * (weighted / total[:, None] - match.astype(f32))
    ).astype(bf16)
    grad_other = shifted(grad_own, "mp", 1)

    q_part = jnp.stack(
        [
            contract(grad_own, p_all, ((1,), (0,))).astype(bf16).reshape(slots, half, width),
            contract(grad_other, p_all, ((1,), (0,))).astype(bf16).reshape(slots, half, width),
        ],
        axis=1,
    ).reshape(n_x, n_z * q_rows, width)
    p_part = (
        contract(grad_own, q_own, ((0,), (0,))) + contract(grad_other, q_other, ((0,), (0,)))
    ).astype(bf16).reshape(n_y, p_rows, width)

    q_back = return_slots([q_part[s] for s in range(n_x)], "x")
    p_back = return_slots([p_part[s] for s in range(n_y)], "y")
    q_sum = sum(part.astype(f32) for part in q_back).astype(bf16).reshape(n_z, q_rows, width)
    q_grad = sum(
        part.astype(f32) for part in return_slots([q_sum[s] for s in range(n_z)], "z")
    )
    q_grad = own_first(q_grad)
    p_grad = sum(part.astype(f32) for part in p_back)

    q_radial, p_radial = lax.psum(
        (jnp.sum(q_unit * q_grad, axis=1), jnp.sum(p_unit * p_grad, axis=1)), "mp"
    )
    q_dir = (q_inv * (q_grad - q_unit * q_radial[:, None])).astype(bf16)
    p_dir = (p_inv * (p_grad - p_unit * p_radial[:, None])).astype(bf16)
    out_width = head_weight.shape[0] // 2

    def finish(direction):
        state = contract(direction, head_weight, ((1,), (1,)))
        kept = lax.dynamic_slice_in_dim(state, core * out_width, out_width, 1)
        sent = lax.dynamic_slice_in_dim(state, (1 - core) * out_width, out_width, 1)
        return (kept + shifted(sent.astype(bf16), "mp", 1).astype(f32)).astype(bf16)

    return losses, finish(q_dir), finish(p_dir)


def solution(mesh):
    n_dp, n_core = mesh.devices.shape
    n_z = 8 if n_dp == 128 else 2
    n_x = 4 if n_dp == 128 else 2
    grid = Mesh(
        mesh.devices.reshape(n_dp // (n_x * n_z), n_x, n_z, n_core), ("y", "x", "z", "mp")
    )
    dp = ("y", "x", "z")
    placed = (P(dp, None), P(dp, None), P(None, "mp"), P(dp), P(dp, None), P(dp))
    return jax.shard_map(
        per_device,
        mesh=grid,
        in_specs=placed,
        out_specs=(P(dp), P(dp, "mp"), P(dp, "mp")),
        check_vma=False,
    )
```

```python
import jax
import jax.numpy as jnp
from jax import lax
from jax.sharding import Mesh, PartitionSpec as P

sharpness_divisor = 0.02
bf16 = jnp.bfloat16
f32 = jnp.float32
AUX = 128


def shifted(value, axis, shift):
    n = lax.axis_size(axis)
    return lax.ppermute(value, axis, [(i, (i + shift) % n) for i in range(n)])


def exchanged(parts, axis):
    return lax.all_to_all(parts, axis, split_axis=0, concat_axis=0, tiled=True)


def to_all(value, axis):
    n = lax.axis_size(axis)
    return exchanged(jnp.broadcast_to(value[None], (n,) + value.shape), axis)


def split_three(value):
    high = lax.reduce_precision(value, 8, 7)
    rest = value - high
    middle = lax.reduce_precision(rest, 8, 7)
    return high, middle, rest - middle


def contract(a, b, dims):
    return lax.dot_general(a, b, (dims, ((), ())), preferred_element_type=f32)


def per_device(query_states, passage_states, head_weight, positives, negatives, slope):
    n_y, n_x, n_z = (lax.axis_size(a) for a in ("y", "x", "z"))
    x, z, core = (lax.axis_index(a) for a in ("x", "z", "mp"))
    q_rows, p_rows = query_states.shape[0], passage_states.shape[0]
    depth, width = head_weight.shape
    out_width = depth // 2
    half = q_rows // 2
    slots = n_x * n_z

    def own_first(rows):
        return jnp.where(core == 0, rows, jnp.roll(rows, half, axis=0))

    weight_kept = lax.dynamic_slice_in_dim(head_weight, core * out_width, out_width, 0)
    weight_sent = lax.dynamic_slice_in_dim(head_weight, (1 - core) * out_width, out_width, 0)
    weight_got = shifted(weight_sent, "mp", 1)
    line_positives = [shifted(positives, "y", s) for s in range(1, n_y)]

    q_proj = contract(query_states, head_weight, ((1,), (0,)))
    p_proj = contract(passage_states, head_weight, ((1,), (0,)))
    q_square, p_square = lax.psum(
        (jnp.sum(q_proj * q_proj, axis=1), jnp.sum(p_proj * p_proj, axis=1)), "mp"
    )
    q_inv = lax.rsqrt(q_square + 1e-06)[:, None]
    p_inv = lax.rsqrt(p_square + 1e-06)[:, None]
    q_unit = q_proj * q_inv
    p_unit = p_proj * p_inv
    p_embed = p_unit.astype(bf16)
    p_all = lax.all_gather(p_embed, "y", axis=0, tiled=True)

    ids = jnp.concatenate(
        [positives[:, None], negatives] + [other[:, None] for other in line_positives], axis=1
    )
    named = ids.shape[1]
    per_query = 1 + negatives.shape[1]
    aux = jnp.concatenate(
        [(ids // 256).astype(f32), (ids % 256).astype(f32)]
        + [part[:, None] for part in split_three(slope)],
        axis=1,
    )
    aux = jnp.pad(aux, ((0, 0), (0, AUX - aux.shape[1])))
    message = own_first(jnp.concatenate([q_unit, aux], axis=1).astype(bf16))
    q_z = to_all(message, "z").reshape(n_z * q_rows, width + AUX)
    q_all = to_all(q_z, "x").reshape(slots, 2, half, width + AUX)
    q_own = q_all[:, 0, :, :width].reshape(slots * half, width)
    q_other = q_all[:, 1, :, :width].reshape(slots * half, width)

    info = q_all[..., width:].astype(f32)
    high, low = info[..., :named], info[..., named : 2 * named]
    blocks = 256 * slots
    column = (x * n_z + z).astype(f32) * p_rows
    place = high * 256.0 + low
    line = jnp.floor(place / blocks)
    offset = place - line * blocks - column
    place = jnp.where((offset >= 0) & (offset < p_rows), line * p_rows + offset, -1.0)
    passages = n_y * p_rows
    row = jnp.arange(passages).astype(f32)
    positive_places = jnp.concatenate(
        [place[..., 0].reshape(-1)]
        + [place[..., k].reshape(-1) for k in range(per_query, named)]
    )
    count = jnp.sum((positive_places[:, None] == row[None, :]).astype(f32), axis=0)
    place_own = place[:, 0].reshape(slots * half, named)
    base = 2 * named
    slope_own = (info[:, 0, :, base] + info[:, 0, :, base + 1]) + info[:, 0, :, base + 2]
    slope_own = slope_own.reshape(slots * half)

    score_other = contract(q_other, p_all, ((1,), (1,)))
    score_own = contract(q_own, p_all, ((1,), (1,)))
    scores = (score_own + shifted(score_other, "mp", 1)) / sharpness_divisor
    match = place_own[:, :1] == row[None, :]
    weight = count[None, :] + sum(
        (place_own[:, k : k + 1] == row[None, :]).astype(f32) for k in range(1, per_query)
    )
    weighted = weight * jnp.exp(scores)
    sums = jnp.concatenate(
        [jnp.sum(weighted, axis=1), jnp.sum(jnp.where(match, scores, 0.0), axis=1)]
    ).reshape(-1, 128)
    sums = jnp.sum(to_all(sums, ("x", "z")).reshape((slots,) + sums.shape), axis=0)
    sums = sums.reshape(2, slots, half)
    own_sums = lax.dynamic_index_in_dim(sums, x * n_z + z, 1, keepdims=False)
    own_loss = jnp.log(own_sums[0]) - own_sums[1]
    losses = own_first(jnp.concatenate([own_loss, shifted(own_loss, "mp", 1)]))
    total = sums[0].reshape(slots * half)

    grad_own = (
        (slope_own / sharpness_divisor)[:, None]
        * (weighted / total[:, None] - match.astype(f32))
    ).astype(bf16)
    grad_other = shifted(grad_own, "mp", 1)

    p_part = (
        contract(grad_own, q_own, ((0,), (0,))) + contract(grad_other, q_other, ((0,), (0,)))
    ).astype(bf16)
    p_grad = lax.psum_scatter(p_part, "y", scatter_dimension=0, tiled=True).astype(f32)
    q_part = jnp.stack(
        [
            contract(grad_own, p_all, ((1,), (0,))).astype(bf16).reshape(slots, half, width),
            contract(grad_other, p_all, ((1,), (0,))).astype(bf16).reshape(slots, half, width),
        ],
        axis=1,
    ).reshape(n_x, n_z * q_rows, width)
    q_part = jnp.sum(exchanged(q_part, "x").astype(f32), axis=0).astype(bf16)
    q_part = q_part.reshape(n_z, q_rows, width)
    q_grad = own_first(jnp.sum(exchanged(q_part, "z").astype(f32), axis=0))

    q_radial, p_radial = lax.psum(
        (jnp.sum(q_unit * q_grad, axis=1), jnp.sum(p_unit * p_grad, axis=1)), "mp"
    )
    q_dir = (q_inv * (q_grad - q_unit * q_radial[:, None])).astype(bf16)
    p_dir = (p_inv * (p_grad - p_unit * p_radial[:, None])).astype(bf16)

    def finish(direction):
        other = shifted(direction, "mp", 1)
        both = contract(direction, weight_kept, ((1,), (1,)))
        return (both + contract(other, weight_got, ((1,), (1,)))).astype(bf16)

    return losses, finish(q_dir), finish(p_dir)


def solution(mesh):
    n_dp, n_core = mesh.devices.shape
    n_z = 8 if n_dp == 128 else 2
    n_x = 4 if n_dp == 128 else 2
    grid = Mesh(
        mesh.devices.reshape(n_dp // (n_x * n_z), n_x, n_z, n_core), ("y", "x", "z", "mp")
    )
    dp = ("y", "x", "z")
    placed = (P(dp, None), P(dp, None), P(None, "mp"), P(dp), P(dp, None), P(dp))
    return jax.shard_map(
        per_device,
        mesh=grid,
        in_specs=placed,
        out_specs=(P(dp), P(dp, "mp"), P(dp, "mp")),
        check_vma=False,
    )
```

```python
import jax
import jax.numpy as jnp
from jax import lax
from jax.experimental import pallas as pl
from jax.experimental.pallas import tpu as pltpu
from jax.sharding import Mesh, PartitionSpec as P

sharpness = 1.0 / 0.02
bf16 = jnp.bfloat16
f32 = jnp.float32
AUX = 128
TILE = 256
VMEM_LIMIT = 40 * 1024 * 1024


def shifted(value, axis, shift):
    n = lax.axis_size(axis)
    return lax.ppermute(value, axis, [(i, (i + shift) % n) for i in range(n)])


def exchanged(parts, axis):
    return lax.all_to_all(parts, axis, split_axis=0, concat_axis=0, tiled=True)


def to_all(value, axis):
    n = lax.axis_size(axis)
    return exchanged(jnp.broadcast_to(value[None], (n,) + value.shape), axis)


def split_three(value):
    high = lax.reduce_precision(value, 8, 7)
    rest = value - high
    middle = lax.reduce_precision(rest, 8, 7)
    return high, middle, rest - middle


def contract(a, b, dims):
    return lax.dot_general(a, b, (dims, ((), ())), preferred_element_type=f32)


def whole(*shape):
    return pl.BlockSpec(shape, lambda j, meta: (0,) * len(shape))


def struct(shape, dtype=f32):
    return jax.ShapeDtypeStruct(shape, dtype)


def call(body, meta, steps, in_specs, out_specs, out_shape, args, scratch=(), flops=0):
    return pl.pallas_call(
        body,
        grid_spec=pltpu.PrefetchScalarGridSpec(
            num_scalar_prefetch=1,
            grid=(steps,),
            in_specs=in_specs,
            out_specs=out_specs,
            scratch_shapes=list(scratch),
        ),
        out_shape=out_shape,
        compiler_params=pltpu.CompilerParams(
            dimension_semantics=("arbitrary",), vmem_limit_bytes=VMEM_LIMIT
        ),
        cost_estimate=pl.CostEstimate(flops=flops, bytes_accessed=0, transcendentals=0),
    )(meta, *args)


def row_of_lane_sums(block):
    return jnp.sum(block.T, axis=0, keepdims=True)


def lanes_to_rows(row):
    return jnp.broadcast_to(row, (128, row.shape[1])).T


def project_body(meta, q_ref, p_ref, w_ref, qo_ref, po_ref, square_ref, x_ref, acc_ref):
    step = pl.program_id(0)
    n_q = q_ref.shape[0]

    @pl.when(step == 0)
    def _():
        x_ref[:n_q] = q_ref[...]
        x_ref[n_q:] = p_ref[...]
        acc_ref[...] = jnp.zeros_like(acc_ref)

    proj = contract(x_ref[...], w_ref[...], ((1,), (0,)))
    qo_ref[...] = proj[:n_q]
    po_ref[...] = proj[n_q:]
    square = proj * proj
    acc_ref[...] += square[:, :128] + square[:, 128:]

    @pl.when(step == pl.num_programs(0) - 1)
    def _():
        padded = jnp.concatenate([acc_ref[:n_q], jnp.zeros((128 - n_q, 128), f32)], axis=0)
        square_ref[:, :128] = row_of_lane_sums(padded)
        square_ref[:, 128:] = row_of_lane_sums(acc_ref[n_q:])


def project(meta, queries, passages, weight):
    n_q, n_p, (depth, width) = queries.shape[0], passages.shape[0], weight.shape
    column = lambda rows: pl.BlockSpec((rows, TILE), lambda j, meta: (0, j))
    return call(
        project_body,
        meta,
        width // TILE,
        [whole(n_q, depth), whole(n_p, depth), column(depth)],
        [column(n_q), column(n_p), whole(1, 128 + n_p)],
        [struct((n_q, width)), struct((n_p, width)), struct((1, 128 + n_p))],
        (queries, passages, weight),
        [pltpu.VMEM((n_q + n_p, depth), bf16), pltpu.VMEM((n_q + n_p, 128), f32)],
        2 * (n_q + n_p) * depth * width,
    )


def normalize_body(
    meta, q_ref, p_ref, own_ref, got_ref, aux_ref, message_ref, qu_ref, pu_ref, pe_ref, qi_ref, pi_ref
):
    n_q, width = q_ref.shape
    inv = lanes_to_rows(lax.rsqrt(own_ref[...] + got_ref[...] + 1e-06))
    q_inv, p_inv = inv[:n_q], inv[128:]
    qi_ref[...] = q_inv
    pi_ref[...] = p_inv
    q_unit = q_ref[...] * q_inv[:, :1]
    p_unit = p_ref[...] * p_inv[:, :1]
    qu_ref[...] = q_unit
    pu_ref[...] = p_unit
    pe_ref[...] = p_unit.astype(bf16)
    half = n_q // 2
    first = meta[0] == 0

    def store(columns, value):
        top, bottom = value[:half], value[half:]
        message_ref[:half, columns] = jnp.where(first, top, bottom).astype(bf16)
        message_ref[half:, columns] = jnp.where(first, bottom, top).astype(bf16)

    store(slice(0, width), q_unit)
    store(slice(width, width + AUX), aux_ref[...])


def normalize(meta, q_proj, p_proj, square, square_got, aux):
    (n_q, width), n_p = q_proj.shape, p_proj.shape[0]
    shapes = [
        struct((n_q, width + AUX), bf16),
        struct((n_q, width)),
        struct((n_p, width)),
        struct((n_p, width), bf16),
        struct((n_q, 128)),
        struct((n_p, 128)),
    ]
    args = (q_proj, p_proj, square, square_got, aux)
    return call(
        normalize_body,
        meta,
        1,
        [whole(*a.shape) for a in args],
        [whole(*s.shape) for s in shapes],
        shapes,
        args,
    )


def flat(block):
    return block.reshape(-1, block.shape[-1])


def score_sent_body(meta, q_ref, p_ref, score_ref):
    width = p_ref.shape[1]
    score_ref[...] = contract(flat(q_ref[:, 0, :, :width]), p_ref[...], ((1,), (1,)))


def score_sent(meta, q_all, p_all, n_y):
    slots, _, half, full = q_all.shape
    passages, width = p_all.shape
    rows, block = slots * half, passages // n_y
    return call(
        score_sent_body,
        meta,
        n_y,
        [
            pl.BlockSpec((slots, 1, half, full), lambda j, meta: (0, 1, 0, 0)),
            pl.BlockSpec((block, width), lambda j, meta: (j, 0)),
        ],
        pl.BlockSpec((rows, block), lambda j, meta: (0, j)),
        struct((rows, passages)),
        (q_all, p_all),
        flops=2 * rows * passages * width,
    )


def places(info, step, meta, slots, named):
    owner = (step * slots + meta[1]).astype(f32)
    return jnp.where(info == owner, pltpu.roll(info, AUX - named, 1), -1.0)


def score_kept_body(per_query, named, meta, q_ref, p_ref, score_ref, weight_ref, info_ref, place_ref):
    step = pl.program_id(0)
    slots, _, half, full = q_ref.shape
    block, width = p_ref.shape
    rows = slots * half
    score_ref[...] = contract(flat(q_ref[:, 0, :, :width]), p_ref[...], ((1,), (1,)))
    info = flat(q_ref[:, 0, :, width:]).astype(f32)
    info_ref[...] = info
    place_ref[:rows] = places(info, step, meta, slots, named)
    place_ref[rows:] = places(flat(q_ref[:, 1, :, width:]).astype(f32), step, meta, slots, named)
    chunk = 32
    column = lax.broadcasted_iota(jnp.int32, (chunk, block), 1).astype(f32)

    def hits(start, columns):
        place = place_ref[pl.ds(pl.multiple_of(start, chunk), chunk), :]
        return sum((place[:, k : k + 1] == column).astype(f32) for k in columns)

    def add(i, total):
        return total + hits(i * chunk, [0] + list(range(per_query, named)))

    total = lax.fori_loop(0, 2 * rows // chunk, add, jnp.zeros((chunk, block), f32))
    count = jnp.sum(total, axis=0, keepdims=True)

    def put(i, carry):
        at = pl.ds(pl.multiple_of(i * chunk, chunk), chunk)
        weight_ref[at, :] = hits(i * chunk, range(1, per_query)) + count
        return carry

    lax.fori_loop(0, rows // chunk, put, 0)


def score_kept(meta, q_all, p_all, n_y, per_query, named):
    slots, _, half, full = q_all.shape
    passages, width = p_all.shape
    rows, block = slots * half, passages // n_y
    out = pl.BlockSpec((rows, block), lambda j, meta: (0, j))

    def body(*refs):
        score_kept_body(per_query, named, *refs)

    return call(
        body,
        meta,
        n_y,
        [
            whole(slots, 2, half, full),
            pl.BlockSpec((block, width), lambda j, meta: (j, 0)),
        ],
        [out, out, whole(rows, AUX)],
        [struct((rows, passages)), struct((rows, passages)), struct((rows, AUX))],
        (q_all, p_all),
        [pltpu.VMEM((2 * rows, AUX), f32)],
        4 * rows * passages * width,
    )


def matches(info, step, meta, slots, named, block):
    place = places(info, step, meta, slots, named)
    column = lax.broadcasted_iota(jnp.int32, (info.shape[0], block), 1).astype(f32)
    return place[:, :1] == column


def weigh_body(slots, named, meta, kept_ref, got_ref, weight_ref, info_ref, e_ref, sum_ref, acc_ref):
    step = pl.program_id(0)

    @pl.when(step == 0)
    def _():
        acc_ref[...] = jnp.zeros_like(acc_ref)

    score = (kept_ref[...] + got_ref[...]) * sharpness
    weighted = weight_ref[...] * jnp.exp(score)
    e_ref[...] = weighted
    match = matches(info_ref[...], step, meta, slots, named, score.shape[1])
    own = jnp.where(match, score, 0.0)
    acc_ref[0] += weighted[:, :128] + weighted[:, 128:]
    acc_ref[1] += own[:, :128] + own[:, 128:]

    @pl.when(step == pl.num_programs(0) - 1)
    def _():
        sum_ref[0:1] = row_of_lane_sums(acc_ref[0])
        sum_ref[1:2] = row_of_lane_sums(acc_ref[1])


def weigh(meta, kept, got, weight, info, n_y, slots, named):
    rows, passages = kept.shape
    block = pl.BlockSpec((rows, passages // n_y), lambda j, meta: (0, j))

    def body(*refs):
        weigh_body(slots, named, *refs)

    return call(
        body,
        meta,
        n_y,
        [block, block, block, whole(rows, AUX)],
        [block, whole(2, rows)],
        [struct((rows, passages)), struct((2, rows))],
        (kept, got, weight, info),
        [pltpu.VMEM((2, rows, 128), f32)],
    )


def slope_body(slots, named, meta, e_ref, sums_ref, info_ref, grad_ref, loss_ref, scale_ref, inv_ref):
    step = pl.program_id(0)

    @pl.when(step == 0)
    def _():
        sums = jnp.sum(sums_ref[...], axis=0)
        total = sums[0:1]
        loss_ref[...] = jnp.log(total) - sums[1:2]
        inv_ref[...] = 1.0 / lanes_to_rows(total)
        base = 2 * named
        info = info_ref[...]
        slope = (info[:, base : base + 1] + info[:, base + 1 : base + 2]) + info[:, base + 2 : base + 3]
        scale_ref[...] = jnp.broadcast_to(slope * sharpness, scale_ref.shape)

    match = matches(info_ref[...], step, meta, slots, named, e_ref.shape[1])
    likelihood = e_ref[...] * inv_ref[:, :1]
    grad_ref[...] = (scale_ref[:, :1] * (likelihood - match.astype(f32))).astype(bf16)


def slopes(meta, e, sums, info, n_y, slots, named):
    rows, passages = e.shape
    block = pl.BlockSpec((rows, passages // n_y), lambda j, meta: (0, j))

    def body(*refs):
        slope_body(slots, named, *refs)

    return call(
        body,
        meta,
        n_y,
        [block, whole(*sums.shape), whole(rows, AUX)],
        [block, whole(1, rows)],
        [struct((rows, passages), bf16), struct((1, rows))],
        (e, sums, info),
        [pltpu.VMEM((rows, 128), f32), pltpu.VMEM((rows, 128), f32)],
    )


def grads_first_body(meta, grad_ref, p_ref, q_ref, qo_ref, po_ref, turned_ref):
    @pl.when(pl.program_id(0) == 0)
    def _():
        turned_ref[...] = grad_ref[...].T

    qo_ref[...] = contract(grad_ref[...], p_ref[...], ((1,), (0,))).astype(bf16)
    po_ref[...] = contract(turned_ref[...], flat(q_ref[:, 0]), ((1,), (0,)))


def grads_first(meta, grad, p_all, q_all):
    rows, passages = grad.shape
    width = p_all.shape[1]
    slots, _, half, _ = q_all.shape
    column = lambda r: pl.BlockSpec((r, TILE), lambda j, meta: (0, j))
    return call(
        grads_first_body,
        meta,
        width // TILE,
        [
            whole(rows, passages),
            column(passages),
            pl.BlockSpec((slots, 1, half, TILE), lambda j, meta: (0, 0, 0, j)),
        ],
        [column(rows), column(passages)],
        [struct((rows, width), bf16), struct((passages, width))],
        (grad, p_all, q_all),
        [pltpu.VMEM((passages, rows), bf16)],
        4 * rows * passages * width,
    )


def grads_second_body(meta, grad_ref, p_ref, q_ref, qi_ref, pi_ref, qo_ref, po_ref, turned_ref):
    @pl.when(pl.program_id(0) == 0)
    def _():
        turned_ref[...] = grad_ref[...].T

    slots, _, half, tile = qo_ref.shape
    po_ref[...] = (
        pi_ref[...] + contract(turned_ref[...], flat(q_ref[:, 0]), ((1,), (0,)))
    ).astype(bf16)
    qo_ref[:, 0] = qi_ref[...].reshape(slots, half, tile)
    second = contract(grad_ref[...], p_ref[...], ((1,), (0,))).astype(bf16)
    qo_ref[:, 1] = second.reshape(slots, half, tile)


def grads_second(meta, grad, p_all, q_all, q_part, p_part):
    rows, passages = grad.shape
    width = p_all.shape[1]
    slots, _, half, _ = q_all.shape
    column = lambda r: pl.BlockSpec((r, TILE), lambda j, meta: (0, j))
    return call(
        grads_second_body,
        meta,
        width // TILE,
        [
            whole(rows, passages),
            column(passages),
            pl.BlockSpec((slots, 1, half, TILE), lambda j, meta: (0, 1, 0, j)),
            column(rows),
            column(passages),
        ],
        [pl.BlockSpec((slots, 2, half, TILE), lambda j, meta: (0, 0, 0, j)), column(passages)],
        [struct((slots, 2, half, width), bf16), struct((passages, width), bf16)],
        (grad, p_all, q_all, q_part, p_part),
        [pltpu.VMEM((passages, rows), bf16)],
        4 * rows * passages * width,
    )


def finish_body(
    meta, qg_ref, qgo_ref, qu_ref, quo_ref, qi_ref, pg_ref, pgo_ref, pu_ref, puo_ref, pi_ref,
    w_ref, wo_ref, q_out, p_out, dir_ref
):
    n_q, width = qg_ref.shape

    @pl.when(pl.program_id(0) == 0)
    def _():
        def tangent(at, grad_ref, grad_other, unit_ref, unit_other, inv_ref):
            grad, other = grad_ref[...].astype(f32), grad_other[...].astype(f32)
            unit, beyond = unit_ref[...], unit_other[...]
            radial = jnp.sum(unit * grad + beyond * other, axis=1, keepdims=True)
            inv = inv_ref[:, :1]
            dir_ref[at, :width] = (inv * (grad - unit * radial)).astype(bf16)
            dir_ref[at, width:] = (inv * (other - beyond * radial)).astype(bf16)

        tangent(slice(0, n_q), qg_ref, qgo_ref, qu_ref, quo_ref, qi_ref)
        tangent(slice(n_q, dir_ref.shape[0]), pg_ref, pgo_ref, pu_ref, puo_ref, pi_ref)

    state = contract(dir_ref[:, :width], w_ref[...], ((1,), (1,)))
    state = (state + contract(dir_ref[:, width:], wo_ref[...], ((1,), (1,)))).astype(bf16)
    q_out[...] = state[:n_q]
    p_out[...] = state[n_q:]


def finish(meta, rows_in, weight, weight_got):
    depth, width = weight.shape
    n_q, n_p = rows_in[0].shape[0], rows_in[5].shape[0]
    tile = min(512, depth // 2)
    steps = depth // 2 // tile
    rows = pl.BlockSpec((tile, width), lambda j, meta: (meta[0] * steps + j, 0))
    column = lambda r: pl.BlockSpec((r, tile), lambda j, meta: (0, j))
    return call(
        finish_body,
        meta,
        steps,
        [whole(*a.shape) for a in rows_in] + [rows, rows],
        [column(n_q), column(n_p)],
        [struct((n_q, depth // 2), bf16), struct((n_p, depth // 2), bf16)],
        (*rows_in, weight, weight_got),
        [pltpu.VMEM((n_q + n_p, 2 * width), bf16)],
        2 * (n_q + n_p) * depth * width,
    )


def per_device(query_states, passage_states, head_weight, positives, negatives, slope):
    n_y, n_x, n_z = (lax.axis_size(a) for a in ("y", "x", "z"))
    x, z, core = (lax.axis_index(a) for a in ("x", "z", "mp"))
    q_rows, p_rows = query_states.shape[0], passage_states.shape[0]
    width = head_weight.shape[1]
    half = q_rows // 2
    slots = n_x * n_z
    column = x * n_z + z
    meta = jnp.stack([core, column]).astype(jnp.int32)

    def own_first(rows):
        return jnp.where(core == 0, rows, jnp.roll(rows, half, axis=0))

    q_proj, p_proj, square = project(meta, query_states, passage_states, head_weight)
    square_got = shifted(square, "mp", 1)
    line_positives = [shifted(positives, "y", s) for s in range(1, n_y)]
    ids = jnp.concatenate(
        [positives[:, None], negatives] + [other[:, None] for other in line_positives], axis=1
    )
    named = ids.shape[1]
    per_query = 1 + negatives.shape[1]
    aux = jnp.concatenate(
        [(ids // p_rows).astype(f32), (ids % p_rows).astype(f32)]
        + [part[:, None] for part in split_three(slope)],
        axis=1,
    )
    aux = jnp.pad(aux, ((0, 0), (0, AUX - aux.shape[1])))
    message, q_unit, p_unit, p_embed, q_inv, p_inv = normalize(
        meta, q_proj, p_proj, square, square_got, aux
    )
    p_all = lax.all_gather(p_embed, "y", axis=0, tiled=True)
    weight_got = shifted(lax.optimization_barrier((head_weight, square_got))[0], "mp", 1)
    q_unit_got, p_unit_got = shifted(q_unit, "mp", 1), shifted(p_unit, "mp", 1)

    q_z = to_all(message, "z").reshape(n_z * q_rows, width + AUX)
    q_all = to_all(q_z, "x").reshape(slots, 2, half, width + AUX)

    sent = score_sent(meta, q_all, p_all, n_y)
    got = shifted(sent, "mp", 1)
    kept, weight, info = score_kept(meta, q_all, p_all, n_y, per_query, named)
    e, sums = weigh(meta, kept, got, weight, info, n_y, slots, named)
    sums = to_all(sums, ("x", "z")).reshape((slots,) + sums.shape)
    grad, loss = slopes(meta, e, sums, info, n_y, slots, named)
    grad_got = shifted(grad, "mp", 1)
    own_loss = lax.dynamic_slice_in_dim(loss[0], column * half, half, 0)
    losses = own_first(jnp.concatenate([own_loss, shifted(own_loss, "mp", 1)]))

    q_part, p_part = grads_first(meta, grad, p_all, q_all)
    q_part, p_part = grads_second(meta, grad_got, p_all, q_all, q_part, p_part)
    p_grad = lax.psum_scatter(p_part, "y", scatter_dimension=0, tiled=True)
    back = exchanged(q_part.reshape(n_x, n_z * q_rows, width), "x")
    q_part = sum(back[s].astype(f32) for s in range(n_x)).astype(bf16)
    back = exchanged(q_part.reshape(n_z, q_rows, width), "z")
    q_grad = own_first(sum(back[s].astype(f32) for s in range(n_z)))

    q_grad_got, p_grad_got = shifted(q_grad, "mp", 1), shifted(p_grad, "mp", 1)
    query_grads, passage_grads = finish(
        meta,
        (q_grad, q_grad_got, q_unit, q_unit_got, q_inv, p_grad, p_grad_got, p_unit, p_unit_got, p_inv),
        head_weight,
        weight_got,
    )
    return losses, query_grads, passage_grads


def solution(mesh):
    n_dp, n_core = mesh.devices.shape
    n_z = 8 if n_dp == 128 else 2
    n_x = 4 if n_dp == 128 else 2
    grid = Mesh(
        mesh.devices.reshape(n_dp // (n_x * n_z), n_x, n_z, n_core), ("y", "x", "z", "mp")
    )
    dp = ("y", "x", "z")
    placed = (P(dp, None), P(dp, None), P(None, "mp"), P(dp), P(dp, None), P(dp))
    return jax.shard_map(
        per_device,
        mesh=grid,
        in_specs=placed,
        out_specs=(P(dp), P(dp, "mp"), P(dp, "mp")),
        check_vma=False,
    )
```

```python
import jax
import jax.numpy as jnp
from jax import lax
from jax.experimental import pallas as pl
from jax.experimental.pallas import tpu as pltpu
from jax.sharding import Mesh, PartitionSpec as P

sharpness = 1.0 / 0.02
bf16 = jnp.bfloat16
f32 = jnp.float32
AUX = 128
TILE = 256
INDEX = 16
MIB = 1024 * 1024
SHAPES = {128: (4, 4, 8), 16: (4, 4, 1), 8: (2, 2, 2)}


def shifted(value, axis, shift):
    n = lax.axis_size(axis)
    return lax.ppermute(value, axis, [(i, (i + shift) % n) for i in range(n)])


def exchanged(parts, axis):
    return lax.all_to_all(parts, axis, split_axis=0, concat_axis=0, tiled=True)


def to_all(value, axis):
    n = lax.axis_size(axis)
    return exchanged(jnp.broadcast_to(value[None], (n,) + value.shape), axis)


def gather_ring(value, axis):
    n = lax.axis_size(axis)
    if n == 2:
        return [value, shifted(value, axis, 1)]
    cut = value.shape[0] // 2
    before, after = shifted(value, axis, 1), shifted(value, axis, -1)
    far = [shifted(before[:cut], axis, 1), shifted(after[cut:], axis, -1)]
    return [value, before] + far + [after]


def return_ring(parts, axis):
    n = lax.axis_size(axis)
    if n == 2:
        return parts[0].astype(f32) + shifted(parts[1], axis, 1).astype(f32)
    cut = parts.shape[1] // 2
    up = shifted(parts[2, :cut], axis, 1).astype(f32)
    down = shifted(parts[2, cut:], axis, -1).astype(f32)
    ahead = jnp.concatenate([(parts[3, :cut].astype(f32) + up).astype(bf16), parts[3, cut:]])
    behind = jnp.concatenate([parts[1, :cut], (parts[1, cut:].astype(f32) + down).astype(bf16)])
    total = parts[0].astype(f32) + shifted(ahead, axis, 1).astype(f32)
    return total + shifted(behind, axis, -1).astype(f32)


def split_three(value):
    high = lax.reduce_precision(value, 8, 7)
    rest = value - high
    middle = lax.reduce_precision(rest, 8, 7)
    return high, middle, rest - middle


def contract(a, b, dims):
    return lax.dot_general(a, b, (dims, ((), ())), preferred_element_type=f32)


def whole(*shape):
    return pl.BlockSpec(shape, lambda j, meta: (0,) * len(shape))


def struct(shape, dtype=f32):
    return jax.ShapeDtypeStruct(shape, dtype)


def call(body, meta, steps, in_specs, out_specs, out_shape, args, scratch=(), flops=0, vmem=24):
    return pl.pallas_call(
        body,
        grid_spec=pltpu.PrefetchScalarGridSpec(
            num_scalar_prefetch=1,
            grid=(steps,),
            in_specs=in_specs,
            out_specs=out_specs,
            scratch_shapes=list(scratch),
        ),
        out_shape=out_shape,
        compiler_params=pltpu.CompilerParams(
            dimension_semantics=("arbitrary",), vmem_limit_bytes=vmem * MIB
        ),
        cost_estimate=pl.CostEstimate(flops=flops, bytes_accessed=0, transcendentals=0),
    )(meta, *args)


def row_of_lane_sums(block):
    return jnp.sum(block.T, axis=0, keepdims=True)


def lanes_to_rows(row):
    return jnp.broadcast_to(row, (128, row.shape[1])).T


def project_body(meta, q_ref, p_ref, w_ref, qo_ref, po_ref, square_ref, x_ref, acc_ref):
    step = pl.program_id(0)
    n_q = q_ref.shape[0]

    @pl.when(step == 0)
    def _():
        x_ref[:n_q] = q_ref[...]
        x_ref[n_q:] = p_ref[...]
        acc_ref[...] = jnp.zeros_like(acc_ref)

    proj = contract(x_ref[...], w_ref[...], ((1,), (0,)))
    qo_ref[...] = proj[:n_q]
    po_ref[...] = proj[n_q:]
    square = proj * proj
    acc_ref[...] += square[:, :128] + square[:, 128:]

    @pl.when(step == pl.num_programs(0) - 1)
    def _():
        padded = jnp.concatenate([acc_ref[:n_q], jnp.zeros((128 - n_q, 128), f32)], axis=0)
        square_ref[:, :128] = row_of_lane_sums(padded)
        square_ref[:, 128:] = row_of_lane_sums(acc_ref[n_q:])


def project(meta, queries, passages, weight):
    n_q, n_p, (depth, width) = queries.shape[0], passages.shape[0], weight.shape
    column = lambda rows: pl.BlockSpec((rows, TILE), lambda j, meta: (0, j))
    return call(
        project_body,
        meta,
        width // TILE,
        [whole(n_q, depth), whole(n_p, depth), column(depth)],
        [column(n_q), column(n_p), whole(1, 128 + n_p)],
        [struct((n_q, width)), struct((n_p, width)), struct((1, 128 + n_p))],
        (queries, passages, weight),
        [pltpu.VMEM((n_q + n_p, depth), bf16), pltpu.VMEM((n_q + n_p, 128), f32)],
        2 * (n_q + n_p) * depth * width,
        60,
    )


def normalize_body(
    meta, q_ref, p_ref, own_ref, got_ref, aux_ref, message_ref, qu_ref, pu_ref, pe_ref, qi_ref, pi_ref
):
    n_q, width = q_ref.shape
    inv = lanes_to_rows(lax.rsqrt(own_ref[...] + got_ref[...] + 1e-06))
    q_inv, p_inv = inv[:n_q], inv[128:]
    qi_ref[...] = q_inv
    pi_ref[...] = p_inv
    q_unit = q_ref[...] * q_inv[:, :1]
    p_unit = p_ref[...] * p_inv[:, :1]
    qu_ref[...] = q_unit
    pu_ref[...] = p_unit
    pe_ref[...] = p_unit.astype(bf16)
    half = n_q // 2
    first = meta[0] == 0

    def store(columns, value):
        top, bottom = value[:half], value[half:]
        message_ref[:half, columns] = jnp.where(first, top, bottom).astype(bf16)
        message_ref[half:, columns] = jnp.where(first, bottom, top).astype(bf16)

    store(slice(0, width), q_unit)
    store(slice(width, width + AUX), aux_ref[...])


def normalize(meta, q_proj, p_proj, square, square_got, aux):
    (n_q, width), n_p = q_proj.shape, p_proj.shape[0]
    shapes = [
        struct((n_q, width + AUX), bf16),
        struct((n_q, width)),
        struct((n_p, width)),
        struct((n_p, width), bf16),
        struct((n_q, 128)),
        struct((n_p, 128)),
    ]
    args = (q_proj, p_proj, square, square_got, aux)
    return call(
        normalize_body,
        meta,
        1,
        [whole(*a.shape) for a in args],
        [whole(*s.shape) for s in shapes],
        shapes,
        args,
    )


def flat(block):
    return block.reshape(-1, block.shape[-1])


def rem(value, n):
    return lax.rem(value, jnp.int32(n))


def owner_of(meta, step, n_y, slots):
    return (rem(meta[3] - step + n_y, n_y) * slots + meta[1]).astype(f32)


def chunks(rows, size=32):
    return [slice(at, at + size) for at in range(0, rows, size)]


def row_index(rows, columns, start=0):
    return (lax.broadcasted_iota(jnp.int32, (rows, columns), 0) + start).astype(f32)


def score_sent_body(meta, q_ref, p_ref, score_ref):
    width = p_ref.shape[1]
    score_ref[...] = contract(p_ref[...], flat(q_ref[:, 0, :, :width]), ((1,), (1,)))


def score_sent(meta, q_all, p_all, n_y):
    slots, _, half, full = q_all.shape
    passages, width = p_all.shape
    rows, block = slots * half, passages // n_y
    return call(
        score_sent_body,
        meta,
        n_y,
        [
            pl.BlockSpec((slots, 1, half, full), lambda j, meta: (0, 1, 0, 0)),
            pl.BlockSpec((block, width), lambda j, meta: (j, 0)),
        ],
        pl.BlockSpec((block, rows), lambda j, meta: (j, 0)),
        struct((passages, rows)),
        (q_all, p_all),
        flops=2 * rows * passages * width,
    )


def score_kept_body(
    n_y, per_query, named, meta, q_ref, p_ref, score_ref, weight_ref, info_ref, count_ref
):
    step = pl.program_id(0)
    slots, _, half, full = q_ref.shape
    block, width = p_ref.shape
    rows = slots * half

    @pl.when(step == 0)
    def _():
        own = flat(q_ref[:, 0, :, width:]).astype(f32).T
        other = flat(q_ref[:, 1, :, width:]).astype(f32).T
        info_ref[...] = own
        turn = meta[3] - lax.broadcasted_iota(jnp.int32, (8, 1), 0)
        turn = jnp.where(turn < 0, turn + n_y, turn)
        owners = (turn * slots + meta[1]).astype(f32)
        row = row_index(block, rows)
        count = jnp.zeros((block, 8), f32)
        for info in (own, other):
            for k in [0] + list(range(per_query, named)):
                owned = (info[k : k + 1] == owners).astype(f32).astype(bf16)
                placed = (info[INDEX + k : INDEX + k + 1] == row).astype(f32).astype(bf16)
                count = count + contract(placed, owned, ((1,), (1,)))
        count_ref[...] = count

    score_ref[...] = contract(p_ref[...], flat(q_ref[:, 0, :, :width]), ((1,), (1,)))
    owner = owner_of(meta, step, n_y, slots)
    place = jnp.where(info_ref[:INDEX] == owner, info_ref[INDEX : 2 * INDEX], -1.0)
    line = lax.broadcasted_iota(jnp.int32, (1, 8), 1)
    count = jnp.sum(jnp.where(line == step, count_ref[...], 0.0), axis=1, keepdims=True)
    for at in chunks(block):
        row = row_index(at.stop - at.start, rows, at.start)
        weight = jnp.broadcast_to(count[at], row.shape)
        for k in range(1, per_query):
            weight = weight + (place[k : k + 1] == row).astype(f32)
        weight_ref[at] = weight


def score_kept(meta, q_all, p_all, n_y, per_query, named):
    slots, _, half, full = q_all.shape
    passages, width = p_all.shape
    rows, block = slots * half, passages // n_y
    out = pl.BlockSpec((block, rows), lambda j, meta: (j, 0))

    def body(*refs):
        score_kept_body(n_y, per_query, named, *refs)

    return call(
        body,
        meta,
        n_y,
        [
            whole(slots, 2, half, full),
            pl.BlockSpec((block, width), lambda j, meta: (j, 0)),
        ],
        [out, out, whole(AUX, rows)],
        [struct((passages, rows)), struct((passages, rows)), struct((AUX, rows))],
        (q_all, p_all),
        [pltpu.VMEM((block, 8), f32)],
        4 * rows * passages * width,
    )


def positive_place(meta, step, n_y, slots, info_ref):
    owner = owner_of(meta, step, n_y, slots)
    return jnp.where(info_ref[0:1] == owner, info_ref[INDEX : INDEX + 1], -1.0)


def turned_slots(meta, n_x, rows):
    size = rows // n_x
    for s in range(n_x):
        start = pl.multiple_of(rem(meta[2] - s + n_x, n_x) * size, size)
        yield slice(s * size, (s + 1) * size), pl.ds(start, size)


def weigh_body(n_y, n_x, slots, meta, kept_ref, got_ref, weight_ref, info_ref, e_ref, sum_ref, acc_ref):
    step = pl.program_id(0)
    block, rows = kept_ref.shape

    @pl.when(step == 0)
    def _():
        acc_ref[...] = jnp.zeros_like(acc_ref)

    place = positive_place(meta, step, n_y, slots, info_ref)
    for at in chunks(block):
        score = (kept_ref[at] + got_ref[at]) * sharpness
        weighted = weight_ref[at] * jnp.exp(score)
        e_ref[at] = weighted
        own = jnp.where(place == row_index(at.stop - at.start, rows, at.start), score, 0.0)
        acc_ref[0] += jnp.sum(weighted.reshape(-1, 8, rows), axis=0)
        acc_ref[1] += jnp.sum(own.reshape(-1, 8, rows), axis=0)

    @pl.when(step == pl.num_programs(0) - 1)
    def _():
        for i in range(2):
            total = jnp.sum(acc_ref[i], axis=0, keepdims=True)
            for here, there in turned_slots(meta, n_x, rows):
                sum_ref[i : i + 1, there] = total[:, here]


def weigh(meta, kept, got, weight, info, n_y, n_x, slots):
    passages, rows = kept.shape
    block = pl.BlockSpec((passages // n_y, rows), lambda j, meta: (j, 0))

    def body(*refs):
        weigh_body(n_y, n_x, slots, *refs)

    return call(
        body,
        meta,
        n_y,
        [block, block, block, whole(AUX, rows)],
        [block, whole(2, rows)],
        [struct((passages, rows)), struct((2, rows))],
        (kept, got, weight, info),
        [pltpu.VMEM((2, 8, rows), f32)],
    )


def slope_body(n_y, n_x, slots, meta, e_ref, sums_ref, info_ref, grad_ref, loss_ref, scale_ref, inv_ref):
    step = pl.program_id(0)
    block, rows = e_ref.shape

    @pl.when(step == 0)
    def _():
        loss_ref[...] = jnp.sum(sums_ref[...], axis=0)
        for here, there in turned_slots(meta, n_x, rows):
            inv_ref[:, here] = loss_ref[0:1, there]
        for here, there in turned_slots(meta, n_x, rows):
            scale_ref[:, here] = loss_ref[1:2, there]
        total = inv_ref[...]
        loss_ref[0:1] = jnp.log(total) - scale_ref[...]
        inv_ref[...] = 1.0 / total
        base = 2 * INDEX
        slope = (info_ref[base : base + 1] + info_ref[base + 1 : base + 2]) + info_ref[base + 2 : base + 3]
        scale_ref[...] = slope * sharpness

    place = positive_place(meta, step, n_y, slots, info_ref)
    inv, scale = inv_ref[...], scale_ref[...]
    for at in chunks(block):
        match = (place == row_index(at.stop - at.start, rows, at.start)).astype(f32)
        grad_ref[at] = (scale * (e_ref[at] * inv - match)).astype(bf16)


def slopes(meta, e, sums, info, n_y, n_x, slots):
    passages, rows = e.shape
    block = pl.BlockSpec((passages // n_y, rows), lambda j, meta: (j, 0))

    def body(*refs):
        slope_body(n_y, n_x, slots, *refs)

    return call(
        body,
        meta,
        n_y,
        [block, whole(*sums.shape), whole(AUX, rows)],
        [block, whole(2, rows)],
        [struct((passages, rows), bf16), struct((2, rows))],
        (e, sums, info),
        [pltpu.VMEM((1, rows), f32), pltpu.VMEM((1, rows), f32)],
    )


def query_part_body(meta, grad_ref, p_ref, out_ref, turned_ref):
    @pl.when(pl.program_id(0) == 0)
    def _():
        turned_ref[...] = grad_ref[...].T

    out_ref[...] = contract(turned_ref[...], p_ref[...], ((1,), (0,))).astype(bf16)


def query_part(meta, grad, p_all):
    passages, rows = grad.shape
    width = p_all.shape[1]
    column = lambda r: pl.BlockSpec((r, TILE), lambda j, meta: (0, j))
    return call(
        query_part_body,
        meta,
        width // TILE,
        [whole(passages, rows), column(passages)],
        column(rows),
        struct((rows, width), bf16),
        (grad, p_all),
        [pltpu.VMEM((rows, passages), bf16)],
        2 * rows * passages * width,
    )


def query_rest_body(meta, grad_ref, p_ref, first_ref, out_ref, turned_ref):
    @pl.when(pl.program_id(0) == 0)
    def _():
        turned_ref[...] = grad_ref[...].T

    slots, _, half, tile = out_ref.shape
    out_ref[:, 0] = first_ref[...].reshape(slots, half, tile)
    rest = contract(turned_ref[...], p_ref[...], ((1,), (0,))).astype(bf16)
    out_ref[:, 1] = rest.reshape(slots, half, tile)


def query_rest(meta, grad, p_all, first, slots):
    passages, rows = grad.shape
    width = p_all.shape[1]
    half = rows // slots
    column = lambda r: pl.BlockSpec((r, TILE), lambda j, meta: (0, j))
    return call(
        query_rest_body,
        meta,
        width // TILE,
        [whole(passages, rows), column(passages), column(rows)],
        pl.BlockSpec((slots, 2, half, TILE), lambda j, meta: (0, 0, 0, j)),
        struct((slots, 2, half, width), bf16),
        (grad, p_all, first),
        [pltpu.VMEM((rows, passages), bf16)],
        2 * rows * passages * width,
    )


def passage_part_body(meta, grad_ref, other_ref, q_ref, out_ref):
    total = contract(grad_ref[...], flat(q_ref[:, 0]), ((1,), (0,)))
    total = total + contract(other_ref[...], flat(q_ref[:, 1]), ((1,), (0,)))
    out_ref[...] = total.astype(bf16)


def passage_part(meta, grad, other, q_all, width):
    passages, rows = grad.shape
    slots, _, half, _ = q_all.shape
    return call(
        passage_part_body,
        meta,
        width // TILE,
        [
            whole(passages, rows),
            whole(passages, rows),
            pl.BlockSpec((slots, 2, half, TILE), lambda j, meta: (0, 0, 0, j)),
        ],
        pl.BlockSpec((passages, TILE), lambda j, meta: (0, j)),
        struct((passages, width), bf16),
        (grad, other, q_all),
        flops=4 * rows * passages * width,
    )


def finish_body(
    meta, qg_ref, qgo_ref, qu_ref, quo_ref, qi_ref, pg_ref, pgo_ref, pu_ref, puo_ref, pi_ref,
    w_ref, wo_ref, q_out, p_out, dir_ref
):
    n_q, width = qg_ref.shape

    @pl.when(pl.program_id(0) == 0)
    def _():
        def tangent(at, grad_ref, grad_other, unit_ref, unit_other, inv_ref):
            grad, other = grad_ref[...].astype(f32), grad_other[...].astype(f32)
            unit, beyond = unit_ref[...], unit_other[...]
            radial = jnp.sum(unit * grad + beyond * other, axis=1, keepdims=True)
            inv = inv_ref[:, :1]
            dir_ref[at, :width] = (inv * (grad - unit * radial)).astype(bf16)
            dir_ref[at, width:] = (inv * (other - beyond * radial)).astype(bf16)

        tangent(slice(0, n_q), qg_ref, qgo_ref, qu_ref, quo_ref, qi_ref)
        tangent(slice(n_q, dir_ref.shape[0]), pg_ref, pgo_ref, pu_ref, puo_ref, pi_ref)

    state = contract(dir_ref[:, :width], w_ref[...], ((1,), (1,)))
    state = (state + contract(dir_ref[:, width:], wo_ref[...], ((1,), (1,)))).astype(bf16)
    q_out[...] = state[:n_q]
    p_out[...] = state[n_q:]


def finish(meta, rows_in, weight, weight_got):
    depth, width = weight.shape
    n_q, n_p = rows_in[0].shape[0], rows_in[5].shape[0]
    tile = min(512, depth // 2)
    steps = depth // 2 // tile
    rows = pl.BlockSpec((tile, width), lambda j, meta: (meta[0] * steps + j, 0))
    column = lambda r: pl.BlockSpec((r, tile), lambda j, meta: (0, j))
    return call(
        finish_body,
        meta,
        steps,
        [whole(*a.shape) for a in rows_in] + [rows, rows],
        [column(n_q), column(n_p)],
        [struct((n_q, depth // 2), bf16), struct((n_p, depth // 2), bf16)],
        (*rows_in, weight, weight_got),
        [pltpu.VMEM((n_q + n_p, 2 * width), bf16)],
        2 * (n_q + n_p) * depth * width,
        60,
    )


def per_device(query_states, passage_states, head_weight, positives, negatives, slope):
    n_y, n_x, n_z = (lax.axis_size(a) for a in ("y", "x", "z"))
    y, x, z, core = (lax.axis_index(a) for a in ("y", "x", "z", "mp"))
    q_rows, p_rows = query_states.shape[0], passage_states.shape[0]
    width = head_weight.shape[1]
    half = q_rows // 2
    slots = n_x * n_z
    column = x * n_z + z
    meta = jnp.stack([core, column, x, y]).astype(jnp.int32)

    def own_first(rows):
        return jnp.where(core == 0, rows, jnp.roll(rows, half, axis=0))

    q_proj, p_proj, square = project(meta, query_states, passage_states, head_weight)
    square_got = shifted(square, "mp", 1)
    started = lax.optimization_barrier((positives, square))[0]
    line_positives = [shifted(started, "y", s) for s in range(1, n_y)]
    ids = jnp.concatenate(
        [positives[:, None], negatives] + [other[:, None] for other in line_positives], axis=1
    )
    named = ids.shape[1]
    per_query = 1 + negatives.shape[1]
    padded = ((0, 0), (0, INDEX - named))
    aux = jnp.concatenate(
        [jnp.pad((ids // p_rows).astype(f32), padded), jnp.pad((ids % p_rows).astype(f32), padded)]
        + [part[:, None] for part in split_three(slope)],
        axis=1,
    )
    aux = jnp.pad(aux, ((0, 0), (0, AUX - aux.shape[1])))
    message, q_unit, p_unit, p_embed, q_inv, p_inv = normalize(
        meta, q_proj, p_proj, square, square_got, aux
    )
    p_all = jnp.concatenate(gather_ring(p_embed, "y"), axis=0)
    weight_got = shifted(lax.optimization_barrier((head_weight, square_got))[0], "mp", 1)
    q_unit_got, p_unit_got = shifted(q_unit, "mp", 1), shifted(p_unit, "mp", 1)

    q_z = to_all(message, "z").reshape(n_z * q_rows, width + AUX)
    q_all = jnp.concatenate(gather_ring(q_z, "x"), axis=0)
    q_all = q_all.reshape(slots, 2, half, width + AUX)

    sent = score_sent(meta, q_all, p_all, n_y)
    got = shifted(sent, "mp", 1)
    kept, weight, info = score_kept(meta, q_all, p_all, n_y, per_query, named)
    e, sums = weigh(meta, kept, got, weight, info, n_y, n_x, slots)
    sums = to_all(sums, ("x", "z")).reshape((slots,) + sums.shape)
    grad, loss = slopes(meta, e, sums, info, n_y, n_x, slots)
    grad_got = shifted(grad, "mp", 1)
    own_loss = lax.dynamic_slice_in_dim(loss[0], z * half, half, 0)
    losses = own_first(jnp.concatenate([own_loss, shifted(own_loss, "mp", 1)]))

    q_part = query_part(meta, grad, p_all)
    q_part = query_rest(meta, grad_got, p_all, q_part, slots)
    p_part = passage_part(meta, grad, grad_got, q_all, width)
    q_part = return_ring(q_part.reshape(n_x, n_z * q_rows, width), "x").astype(bf16)
    p_grad = return_ring(p_part.reshape(n_y, p_rows, width), "y").astype(bf16)
    back = exchanged(q_part.reshape(n_z, q_rows, width), "z")
    q_grad = own_first(sum(back[s].astype(f32) for s in range(n_z)))

    q_grad_got, p_grad_got = shifted(q_grad, "mp", 1), shifted(p_grad, "mp", 1)
    query_grads, passage_grads = finish(
        meta,
        (q_grad, q_grad_got, q_unit, q_unit_got, q_inv, p_grad, p_grad_got, p_unit, p_unit_got, p_inv),
        head_weight,
        weight_got,
    )
    return losses, query_grads, passage_grads


def solution(mesh):
    n_dp, n_core = mesh.devices.shape
    shape = SHAPES[n_dp] + (n_core,)
    grid = Mesh(mesh.devices.reshape(shape), ("y", "x", "z", "mp"))
    dp = ("y", "x", "z")
    placed = (P(dp, None), P(dp, None), P(None, "mp"), P(dp), P(dp, None), P(dp))
    return jax.shard_map(
        per_device,
        mesh=grid,
        in_specs=placed,
        out_specs=(P(dp), P(dp, "mp"), P(dp, "mp")),
        check_vma=False,
    )
```

```python
import jax
import jax.numpy as jnp
from jax import lax
from jax.experimental import pallas as pl
from jax.experimental.pallas import tpu as pltpu
from jax.sharding import Mesh, PartitionSpec as P

sharpness = 1.0 / 0.02
bf16 = jnp.bfloat16
f32 = jnp.float32
AUX = 128
TILE = 256
CHUNK = 512
INDEX = 16
MIB = 1024 * 1024
SHAPES = {128: (4, 4, 8), 32: (4, 4, 2), 8: (2, 2, 2)}


def shifted(value, axis, shift):
    n = lax.axis_size(axis)
    return lax.ppermute(value, axis, [(i, (i + shift) % n) for i in range(n)])


def exchanged(parts, axis):
    return lax.all_to_all(parts, axis, split_axis=0, concat_axis=0, tiled=True)


def to_all(value, axis):
    n = lax.axis_size(axis)
    return exchanged(jnp.broadcast_to(value[None], (n,) + value.shape), axis)


def after(value, *others):
    return lax.optimization_barrier((value, *others))[0]


def ring_near(value, axis):
    shifts = (1, -1) if lax.axis_size(axis) > 2 else (1,)
    return [shifted(value, axis, shift) for shift in shifts]


def ring_far(value, near, axis):
    if len(near) == 1:
        return [value] + near
    cut = value.shape[0] // 2
    before, behind = near
    return [value, before, shifted(before[:cut], axis, 1), shifted(behind[cut:], axis, -1), behind]


def return_first(pieces, axis, gate=None):
    if len(pieces) == 2:
        return [pieces[1]]
    up, down = shifted(pieces[2], axis, 1), shifted(pieces[3], axis, -1)
    if gate is not None:
        up = after(up, gate)
    return join(pieces[4], up, pieces[1], down)


def return_second(pieces, leaving, axis):
    coming = [shifted(value, axis, shift) for shift, value in zip((1, -1), leaving)]
    return total([pieces[0]] + coming, bf16)


def split_three(value):
    high = lax.reduce_precision(value, 8, 7)
    rest = value - high
    middle = lax.reduce_precision(rest, 8, 7)
    return high, middle, rest - middle


def contract(a, b, dims):
    return lax.dot_general(a, b, (dims, ((), ())), preferred_element_type=f32)


def struct(shape, dtype=f32):
    return jax.ShapeDtypeStruct(shape, dtype)


def call(body, args, outs, scratch=(), flops=0, hbm=(), free=(), vmem=8, loose=False):
    specs, operands = [], []
    for i, arg in enumerate(args):
        if i == 0:
            specs.append(pl.BlockSpec(memory_space=pltpu.SMEM))
        elif i in hbm:
            specs.append(pl.BlockSpec(memory_space=pl.ANY))
            arg = pltpu.with_memory_space_constraint(arg, pltpu.HBM)
        else:
            specs.append(pl.BlockSpec(memory_space=pltpu.VMEM))
            arg = arg if loose else pltpu.with_memory_space_constraint(arg, pltpu.VMEM)
        operands.append(arg)
    kept = [s if loose or i in free else pltpu.VMEM(s.shape, s.dtype) for i, s in enumerate(outs)]
    return pl.pallas_call(
        body,
        in_specs=specs,
        out_specs=[pl.BlockSpec(memory_space=pltpu.VMEM)] * len(outs),
        out_shape=kept,
        scratch_shapes=list(scratch),
        compiler_params=pltpu.CompilerParams(vmem_limit_bytes=vmem * 1024 * 1024),
        cost_estimate=pl.CostEstimate(flops=flops, bytes_accessed=0, transcendentals=0),
    )(*operands)


def row_of_lane_sums(block):
    return jnp.sum(block.T, axis=0, keepdims=True)


def lanes_to_rows(row):
    return jnp.broadcast_to(row, (128, row.shape[1])).T


def rem(value, n):
    return lax.rem(value, jnp.int32(n))


def spans(rows, size):
    return [slice(at, min(at + size, rows)) for at in range(0, rows, size)]


def pieces_at(pieces):
    at = 0
    for piece in pieces:
        yield slice(at, at + piece.shape[0]), piece
        at += piece.shape[0]


def row_index(rows, columns, start=0):
    return (lax.broadcasted_iota(jnp.int32, (rows, columns), 0) + start).astype(f32)


def total_body(meta, *refs):
    value = refs[0][...].astype(f32)
    for ref in refs[1:-1]:
        value = value + ref[...].astype(f32)
    refs[-1][...] = value.astype(refs[-1].dtype)


def total(parts, dtype):
    meta = jnp.zeros((1,), jnp.int32)
    return call(total_body, [meta] + list(parts), [struct(parts[0].shape, dtype)], loose=True)[0]


def total_slots_body(size, meta, ref, loss_ref, out_ref):
    value = ref[0].astype(f32)
    for s in range(1, ref.shape[0]):
        value = value + ref[s].astype(f32)
    n = value.shape[0]
    out_ref[:n] = value
    own = loss_ref[0:1, :size]
    own = pltpu.roll(own, rem(size - meta[4], size), 1)
    out_ref[n:] = jnp.zeros((8, value.shape[1]), f32)
    out_ref[n : n + 1, :size] = own


def total_slots(meta, stacked, loss, size):
    def body(*refs):
        total_slots_body(size, *refs)

    shape = (stacked.shape[1] + 8, stacked.shape[2])
    return call(body, [meta, stacked, loss], [struct(shape)], loose=True)[0]


def join_body(meta, ahead_ref, up_ref, behind_ref, down_ref, ahead_out, behind_out):
    cut = up_ref.shape[0]
    ahead_out[:cut] = (ahead_ref[:cut].astype(f32) + up_ref[...].astype(f32)).astype(bf16)
    ahead_out[cut:] = ahead_ref[cut:]
    behind_out[:cut] = behind_ref[:cut]
    behind_out[cut:] = (behind_ref[cut:].astype(f32) + down_ref[...].astype(f32)).astype(bf16)


def join(ahead, up, behind, down):
    meta = jnp.zeros((1,), jnp.int32)
    shape = struct(ahead.shape, bf16)
    return call(join_body, [meta, ahead, up, behind, down], [shape, shape], loose=True)


def project_body(
    meta, q_ref, p_ref, w_ref, qo_ref, po_ref, square_ref, x_ref, acc_ref, head_ref, sems
):
    n_q = q_ref.shape[0]
    depth, width = w_ref.shape
    chunk = min(CHUNK, depth)
    loads = [
        pltpu.make_async_copy(q_ref, x_ref.at[pl.ds(0, n_q)], sems.at[0]),
        pltpu.make_async_copy(p_ref, x_ref.at[pl.ds(n_q, p_ref.shape[0])], sems.at[1]),
    ]
    blocks = []
    for at in spans(depth, chunk):
        rows = pl.ds(at.start, chunk)
        blocks.append(pltpu.make_async_copy(w_ref.at[rows], head_ref.at[rows], sems.at[2 + len(blocks)]))
    for load in loads:
        load.start()
    for block in blocks:
        block.start()
    for load in loads:
        load.wait()
    for i, at in enumerate(spans(depth, chunk)):
        blocks[i].wait()
        part = contract(x_ref[:, at], head_ref[at], ((1,), (0,)))
        acc_ref[...] = part if i == 0 else acc_ref[...] + part
    qo_ref[...] = acc_ref[:n_q]
    po_ref[...] = acc_ref[n_q:]
    square = jnp.zeros((acc_ref.shape[0], 128), f32)
    for at in range(0, width, 128):
        block = acc_ref[:, at : at + 128]
        square = square + block * block
    padded = jnp.concatenate([square[:n_q], jnp.zeros((128 - n_q, 128), f32)], axis=0)
    square_ref[:, :128] = row_of_lane_sums(padded)
    square_ref[:, 128:] = row_of_lane_sums(square[n_q:])


def project(meta, queries, passages, weight):
    n_q, n_p, (depth, width) = queries.shape[0], passages.shape[0], weight.shape
    copies = 2 + depth // min(CHUNK, depth)
    return call(
        project_body,
        [meta, queries, passages, weight],
        [struct((n_q, width)), struct((n_p, width)), struct((1, 128 + n_p))],
        [
            pltpu.VMEM((n_q + n_p, depth), bf16),
            pltpu.VMEM((n_q + n_p, width), f32),
            pltpu.VMEM((depth, width), bf16),
            pltpu.SemaphoreType.DMA((copies,)),
        ],
        2 * (n_q + n_p) * depth * width,
        hbm=(1, 2, 3),
        vmem=18,
    )


def normalize_body(
    meta, q_ref, p_ref, own_ref, got_ref, aux_ref, message_ref, unit_ref, embed_ref, inv_ref
):
    n_q, width = q_ref.shape
    inv = lanes_to_rows(lax.rsqrt(own_ref[...] + got_ref[...] + 1e-06))
    inv_ref[:n_q] = inv[:n_q]
    inv_ref[n_q:] = inv[128:]
    q_unit = q_ref[...] * inv[:n_q, :1]
    p_unit = p_ref[...] * inv[128:, :1]
    unit_ref[:n_q] = q_unit
    unit_ref[n_q:] = p_unit
    embed_ref[...] = p_unit.astype(bf16)
    half = n_q // 2
    first = meta[0] == 0

    def store(columns, value):
        top, bottom = value[:half], value[half:]
        message_ref[:half, columns] = jnp.where(first, top, bottom).astype(bf16)
        message_ref[half:, columns] = jnp.where(first, bottom, top).astype(bf16)

    store(slice(0, width), q_unit)
    store(slice(width, width + AUX), aux_ref[...])


def normalize(meta, q_proj, p_proj, square, square_got, aux):
    (n_q, width), n_p = q_proj.shape, p_proj.shape[0]
    return call(
        normalize_body,
        [meta, q_proj, p_proj, square, square_got, aux],
        [
            struct((n_q, width + AUX), bf16),
            struct((n_q + n_p, width)),
            struct((n_p, width), bf16),
            struct((n_q + n_p, 128)),
        ],
    )


def owner_of(meta, line, n_y, slots):
    return (rem(meta[3] - line + n_y, n_y) * slots + meta[1]).astype(f32)


def score_sent_body(n_pieces, meta, *refs):
    q_refs, p_refs = refs[:n_pieces[0]], refs[n_pieces[0] : sum(n_pieces)]
    score_ref, own_ref, other_ref, all_ref, aux_ref, aux_other_ref = refs[sum(n_pieces) :]
    width = own_ref.shape[1]
    at = 0
    for ref in q_refs:
        value = ref[...].reshape(-1, 2, 16, ref.shape[1])
        rows = value.shape[0] * 16
        for i, (to_ref, aux) in enumerate(((own_ref, aux_ref), (other_ref, aux_other_ref))):
            side = value[:, i].reshape(rows, -1)
            to_ref[at : at + rows] = side[:, :width]
            aux[at : at + rows] = side[:, width:].astype(f32)
        at += rows
    for at, ref in pieces_at(p_refs):
        all_ref[at] = ref[...]
        score_ref[at] = contract(ref[...], other_ref[...], ((1,), (1,)))


def score_sent(meta, q_pieces, p_pieces):
    width = p_pieces[0].shape[1]
    passages = sum(p.shape[0] for p in p_pieces)
    rows = sum(q.shape[0] for q in q_pieces) // 2

    def body(*refs):
        score_sent_body((len(q_pieces), len(p_pieces)), *refs)

    return call(
        body,
        [meta] + q_pieces + p_pieces,
        [
            struct((passages, rows)),
            struct((rows, width), bf16),
            struct((rows, width), bf16),
            struct((passages, width), bf16),
            struct((rows, AUX)),
            struct((rows, AUX)),
        ],
        flops=2 * rows * passages * width,
    )


def count_body(slots, meta, aux_ref, other_ref, info_ref, count_ref):
    block = count_ref.shape[1]
    info_ref[...] = aux_ref[...].T
    owners = (lax.broadcasted_iota(jnp.int32, (8, 1), 0) * slots + meta[1]).astype(f32)
    count = jnp.zeros(count_ref.shape, f32)
    for info in (info_ref[...], other_ref[...].T):
        owned = (info[0:1] == owners).astype(f32).astype(bf16)
        placed = info[INDEX : INDEX + 1] == row_index(block, info.shape[1])
        count = count + contract(owned, placed.astype(f32).astype(bf16), ((1,), (1,)))
    count_ref[...] = count


def count_positives(meta, aux, aux_other, block, slots):
    def body(*refs):
        count_body(slots, *refs)

    return call(
        body, [meta, aux, aux_other], [struct((AUX, aux.shape[0])), struct((8, block))]
    )


def score_kept_body(n_y, slots, per_query, meta, q_ref, p_ref, info_ref, score_ref, weight_ref):
    passages, rows = score_ref.shape
    block = passages // n_y
    for line in range(n_y):
        owner = owner_of(meta, line, n_y, slots)
        place = jnp.where(info_ref[:INDEX] == owner, info_ref[INDEX : 2 * INDEX], -1.0)
        at = slice(line * block, (line + 1) * block)
        score_ref[at] = contract(p_ref[at], q_ref[...], ((1,), (1,)))
        for span in spans(block, 32):
            row = row_index(span.stop - span.start, rows, span.start)
            weight = (place[1:2] == row).astype(f32)
            for k in range(2, per_query):
                weight = weight + (place[k : k + 1] == row).astype(f32)
            weight_ref[line * block + span.start : line * block + span.stop] = weight


def score_kept(meta, q_own, p_all, info, n_y, slots, per_query):
    passages, rows = p_all.shape[0], q_own.shape[0]

    def body(*refs):
        score_kept_body(n_y, slots, per_query, *refs)

    return call(
        body,
        [meta, q_own, p_all, info],
        [struct((passages, rows)), struct((passages, rows))],
        flops=4 * rows * passages * p_all.shape[1],
    )


def positive_place(meta, line, n_y, slots, info_ref):
    owner = owner_of(meta, line, n_y, slots)
    return jnp.where(info_ref[0:1] == owner, info_ref[INDEX : INDEX + 1], -1.0)


def turned_slots(meta, n_x, rows):
    size = rows // n_x
    for s in range(n_x):
        start = pl.multiple_of(rem(meta[2] - s + n_x, n_x) * size, size)
        yield slice(s * size, (s + 1) * size), pl.ds(start, size)


def weigh_body(
    n_y, n_x, slots, meta, kept_ref, got_ref, weight_ref, info_ref, *rest_refs
):
    counts_ref, (e_ref, sum_ref) = rest_refs[:-2], rest_refs[-2:]
    passages, rows = kept_ref.shape
    block = passages // n_y
    counts = counts_ref[0][...]
    for ref in counts_ref[1:]:
        counts = counts + ref[...]
    rest = jnp.zeros((128 - counts.shape[0], block), f32)
    counts = jnp.concatenate([counts, rest], axis=0).T
    lane = lax.broadcasted_iota(jnp.int32, (1, 128), 1)
    sums = [jnp.zeros((8, rows), f32), jnp.zeros((8, rows), f32)]
    for line in range(n_y):
        mine = lane == rem(meta[3] - line + n_y, n_y)
        count = jnp.sum(jnp.where(mine, counts, 0.0), axis=1, keepdims=True)
        place = positive_place(meta, line, n_y, slots, info_ref)
        for span in spans(block, 32):
            at = slice(line * block + span.start, line * block + span.stop)
            score = (kept_ref[at] + got_ref[at]) * sharpness
            weighted = (weight_ref[at] + count[span]) * jnp.exp(score)
            e_ref[at] = weighted
            own = jnp.where(place == row_index(span.stop - span.start, rows, span.start), score, 0.0)
            sums[0] = sums[0] + jnp.sum(weighted.reshape(-1, 8, rows), axis=0)
            sums[1] = sums[1] + jnp.sum(own.reshape(-1, 8, rows), axis=0)
    for i in range(2):
        row = jnp.sum(sums[i], axis=0, keepdims=True)
        for here, there in turned_slots(meta, n_x, rows):
            sum_ref[i : i + 1, there] = row[:, here]


def weigh(meta, kept, got, weight, info, counts, n_y, n_x, slots):
    passages, rows = kept.shape

    def body(*refs):
        weigh_body(n_y, n_x, slots, *refs)

    return call(
        body,
        [meta, kept, got, weight, info, *counts],
        [struct((passages, rows)), struct((2, rows))],
    )


def slope_body(n_y, n_x, slots, meta, e_ref, sums_ref, info_ref, grad_ref, loss_ref, scale_ref, inv_ref):
    passages, rows = e_ref.shape
    block = passages // n_y
    loss_ref[...] = jnp.sum(sums_ref[...], axis=0)
    for here, there in turned_slots(meta, n_x, rows):
        inv_ref[:, here] = loss_ref[0:1, there]
    for here, there in turned_slots(meta, n_x, rows):
        scale_ref[:, here] = loss_ref[1:2, there]
    sums = inv_ref[...]
    loss_ref[0:1] = jnp.log(sums) - scale_ref[...]
    inv = 1.0 / sums
    base = 2 * INDEX
    scale = (info_ref[base : base + 1] + info_ref[base + 1 : base + 2]) + info_ref[base + 2 : base + 3]
    scale = scale * sharpness
    for line in range(n_y):
        place = positive_place(meta, line, n_y, slots, info_ref)
        for span in spans(block, 32):
            at = slice(line * block + span.start, line * block + span.stop)
            match = (place == row_index(span.stop - span.start, rows, span.start)).astype(f32)
            grad_ref[at] = (scale * (e_ref[at] * inv - match)).astype(bf16)


def slopes(meta, e, sums, info, n_y, n_x, slots):
    passages, rows = e.shape

    def body(*refs):
        slope_body(n_y, n_x, slots, *refs)

    return call(
        body,
        [meta, e, sums, info],
        [struct((passages, rows), bf16), struct((2, rows))],
        [pltpu.VMEM((1, rows), f32), pltpu.VMEM((1, rows), f32)],
    )


def query_part_body(meta, grad_ref, p_ref, out_ref, turned_ref):
    turned_ref[...] = grad_ref[...].T
    for at in spans(p_ref.shape[1], TILE):
        out_ref[:, at] = contract(turned_ref[...], p_ref[:, at], ((1,), (0,))).astype(bf16)


def query_part(meta, grad, p_all):
    (passages, rows), width = grad.shape, p_all.shape[1]
    return call(
        query_part_body,
        [meta, grad, p_all],
        [struct((rows, width), bf16)],
        [pltpu.VMEM((rows, passages), bf16)],
        2 * rows * passages * width,
    )[0]


def query_rest_body(meta, grad_ref, p_ref, first_ref, *refs):
    out_refs, turned_ref = refs[:-1], refs[-1]
    turned_ref[...] = grad_ref[...].T
    for span in spans(p_ref.shape[1], TILE):
        rest = contract(turned_ref[...], p_ref[:, span], ((1,), (0,))).astype(bf16)
        at = 0
        for ref in out_refs:
            rows = ref.shape[0] * 16
            for i, value in enumerate((first_ref[at : at + rows, span], rest[at : at + rows])):
                ref[:, i, :, span] = value.reshape(-1, 16, value.shape[1])
            at += rows


def query_rest(meta, grad, p_all, first, shapes):
    (passages, rows), width = grad.shape, p_all.shape[1]
    return call(
        query_rest_body,
        [meta, grad, p_all, first],
        [struct((n // 32, 2, 16, width), bf16) for n in shapes],
        [pltpu.VMEM((rows, passages), bf16)],
        2 * rows * passages * width,
    )


def passage_part_body(meta, grad_ref, other_ref, own_ref, q_ref, *out_refs):
    for at, ref in pieces_at(out_refs):
        value = contract(grad_ref[at], own_ref[...], ((1,), (0,)))
        value = value + contract(other_ref[at], q_ref[...], ((1,), (0,)))
        ref[...] = value.astype(bf16)


def passage_part(meta, grad, other, q_own, q_other, shapes):
    (passages, rows), width = grad.shape, q_own.shape[1]
    return call(
        passage_part_body,
        [meta, grad, other, q_own, q_other],
        [struct((n, width), bf16) for n in shapes],
        flops=4 * rows * passages * width,
    )


def tangent(grad, other, unit, beyond, inv):
    radial = jnp.sum(unit * grad + beyond * other, axis=1, keepdims=True)
    return (inv * (grad - unit * radial)).astype(bf16), (inv * (other - beyond * radial)).astype(bf16)


def finish_body(
    meta, qg_ref, qgo_ref, pg_ref, pgo_ref, unit_ref, beyond_ref, inv_ref, w_hbm, wo_hbm,
    q_out, p_out, loss_out, here_ref, there_ref, w_ref, wo_ref, sems
):
    half = w_ref.shape[0]
    blocks = spans(half, CHUNK)
    loads = []
    for i, at in enumerate(blocks):
        size, to = at.stop - at.start, pl.ds(at.start, at.stop - at.start)
        rows = pl.ds(pl.multiple_of(meta[0] * half + at.start, size), size)
        loads.append(pltpu.make_async_copy(w_hbm.at[rows], w_ref.at[to], sems.at[2 * i]))
        loads.append(pltpu.make_async_copy(wo_hbm.at[rows], wo_ref.at[to], sems.at[2 * i + 1]))
    for load in loads:
        load.start()
    n_q = q_out.shape[0]
    part = n_q // 2
    first = meta[0] == 0
    turn = lambda rows: jnp.concatenate([rows[part:], rows[:part]], axis=0)
    grad, other = qg_ref[:n_q], qgo_ref[:n_q]
    grad, other = jnp.where(first, grad, turn(grad)), jnp.where(first, turn(other), other)
    here_ref[:n_q], there_ref[:n_q] = tangent(
        grad, other, unit_ref[:n_q], beyond_ref[:n_q], inv_ref[:n_q, :1]
    )
    own, got = qg_ref[n_q : n_q + 1, :128], qgo_ref[n_q : n_q + 1, :128]
    low, high = jnp.where(first, own, got), jnp.where(first, got, own)
    lane = lax.broadcasted_iota(jnp.int32, (1, 128), 1)
    loss_out[...] = jnp.where(lane < part, low, pltpu.roll(high, part, 1))
    for at in spans(pg_ref.shape[0], 64):
        to = slice(n_q + at.start, n_q + at.stop)
        here_ref[to], there_ref[to] = tangent(
            pg_ref[at].astype(f32), pgo_ref[at].astype(f32), unit_ref[to], beyond_ref[to], inv_ref[to, :1]
        )
    for i, at in enumerate(blocks):
        loads[2 * i].wait()
        loads[2 * i + 1].wait()
        state = contract(here_ref[...], w_ref[at], ((1,), (1,)))
        state = (state + contract(there_ref[...], wo_ref[at], ((1,), (1,)))).astype(bf16)
        q_out[:, at] = state[:n_q]
        p_out[:, at] = state[n_q:]


def finish(meta, rows_in, weight, weight_got):
    depth, width = weight.shape
    n, n_p, out_width = rows_in[4].shape[0], rows_in[2].shape[0], depth // 2
    copies = 2 * len(spans(out_width, CHUNK))
    return call(
        finish_body,
        [meta, *rows_in, weight, weight_got],
        [struct((n - n_p, out_width), bf16), struct((n_p, out_width), bf16), struct((1, 128))],
        [
            pltpu.VMEM((n, width), bf16),
            pltpu.VMEM((n, width), bf16),
            pltpu.VMEM((out_width, width), bf16),
            pltpu.VMEM((out_width, width), bf16),
            pltpu.SemaphoreType.DMA((copies,)),
        ],
        4 * n * out_width * width,
        hbm=(8, 9),
        free=(0, 1, 2),
        vmem=20,
    )


def per_device(query_states, passage_states, head_weight, positives, negatives, slope):
    n_y, n_x, n_z = (lax.axis_size(a) for a in ("y", "x", "z"))
    y, x, z, core = (lax.axis_index(a) for a in ("y", "x", "z", "mp"))
    q_rows, p_rows = query_states.shape[0], passage_states.shape[0]
    width = head_weight.shape[1]
    half = q_rows // 2
    slots = n_x * n_z
    column = x * n_z + z
    meta = jnp.stack([core, column, x, y, z * half]).astype(jnp.int32)

    q_proj, p_proj, square = project(meta, query_states, passage_states, head_weight)
    square_got = shifted(square, "mp", 1)
    ids = jnp.concatenate([positives[:, None], negatives], axis=1)
    per_query = ids.shape[1]
    padded = ((0, 0), (0, INDEX - per_query))
    aux = jnp.concatenate(
        [jnp.pad((ids // p_rows).astype(f32), padded), jnp.pad((ids % p_rows).astype(f32), padded)]
        + [part[:, None] for part in split_three(slope)],
        axis=1,
    )
    aux = jnp.pad(aux, ((0, 0), (0, AUX - aux.shape[1])))
    message, unit, p_embed, inv = normalize(
        meta, q_proj, p_proj, square, square_got, aux
    )
    unit_got = shifted(unit, "mp", 1)
    weight_got = shifted(after(head_weight, unit), "mp", 1)
    p_near = ring_near(p_embed, "y")
    q_z = to_all(message, "z").reshape(n_z * q_rows, width + AUX)
    q_z = after(q_z, unit_got, weight_got, *p_near)
    q_near = ring_near(q_z, "x")
    q_pieces = ring_far(q_z, q_near, "x")
    p_pieces = ring_far(p_embed, [after(piece, *q_near) for piece in p_near], "y")
    q_shapes, p_shapes = ([piece.shape[0] for piece in pieces] for pieces in (q_pieces, p_pieces))
    sent, q_own, q_other, p_all, aux, aux_other = score_sent(meta, q_pieces, p_pieces)
    got = shifted(sent, "mp", 1)
    info, count = count_positives(meta, aux, aux_other, p_rows, slots)
    counts = [count] + [shifted(count, "y", s) for s in range(1, n_y)]
    kept, named = score_kept(meta, q_own, p_all, info, n_y, slots, per_query)
    e, sums = weigh(meta, kept, got, named, info, counts, n_y, n_x, slots)
    sums = to_all(sums, ("x", "z")).reshape((slots,) + sums.shape)
    grad, loss = slopes(meta, e, sums, info, n_y, n_x, slots)
    grad_got = shifted(grad, "mp", 1)
    q_part = query_part(meta, grad, p_all)
    grad_got = after(grad_got, q_part)
    p_parts = passage_part(meta, grad, grad_got, q_own, q_other, p_shapes)
    q_parts = query_rest(meta, grad_got, p_all, q_part, q_shapes)
    p_leaving = return_first(p_parts, "y", q_parts[0])
    q_leaving = return_first([part.reshape(-1, width) for part in q_parts], "x")
    p_grad = return_second(p_parts, p_leaving, "y")
    p_grad_got = shifted(p_grad, "mp", 1)
    q_part = return_second([part.reshape(-1, width) for part in q_parts], q_leaving, "x")
    q_part = after(q_part, p_grad_got)
    back = exchanged(q_part.reshape(n_z, q_rows, width), "z")
    q_grad = total_slots(meta, back, loss, n_z * half)
    q_grad_got = shifted(q_grad, "mp", 1)
    query_grads, passage_grads, losses = finish(
        meta, (q_grad, q_grad_got, p_grad, p_grad_got, unit, unit_got, inv), head_weight, weight_got
    )
    return losses[0, :q_rows], query_grads, passage_grads


def solution(mesh):
    n_dp, n_core = mesh.devices.shape
    shape = SHAPES[n_dp] + (n_core,)
    grid = Mesh(mesh.devices.reshape(shape), ("y", "x", "z", "mp"))
    dp = ("y", "x", "z")
    placed = (P(dp, None), P(dp, None), P(None, "mp"), P(dp), P(dp, None), P(dp))
    return jax.shard_map(
        per_device,
        mesh=grid,
        in_specs=placed,
        out_specs=(P(dp), P(dp, "mp"), P(dp, "mp")),
        check_vma=False,
    )
```

```python
import jax
import jax.numpy as jnp
from jax import lax
from jax.experimental import pallas as pl
from jax.experimental.pallas import tpu as pltpu
from jax.sharding import Mesh, PartitionSpec as P

sharpness = 1.0 / 0.02
bf16 = jnp.bfloat16
f32 = jnp.float32
AUX = 128
TILE = 256
CHUNK = 512
INDEX = 16
MIB = 1024 * 1024
SHAPES = {128: (4, 4, 8), 32: (4, 4, 2), 8: (2, 2, 2)}


def shifted(value, axis, shift):
    n = lax.axis_size(axis)
    return lax.ppermute(value, axis, [(i, (i + shift) % n) for i in range(n)])


def exchanged(parts, axis):
    return lax.all_to_all(parts, axis, split_axis=0, concat_axis=0, tiled=True)


def to_all(value, axis):
    n = lax.axis_size(axis)
    return exchanged(jnp.broadcast_to(value[None], (n,) + value.shape), axis)


def after(value, *others):
    return lax.optimization_barrier((value, *others))[0]


def ring_near(value, axis):
    shifts = (1, -1) if lax.axis_size(axis) > 2 else (1,)
    return [shifted(value, axis, shift) for shift in shifts]


def ring_far(value, near, axis):
    if len(near) == 1:
        return [value] + near
    cut = value.shape[0] // 2
    before, behind = near
    return [value, before, shifted(before[:cut], axis, 1), shifted(behind[cut:], axis, -1), behind]


def return_far(pieces, axis):
    if len(pieces) == 2:
        return [pieces[1]]
    return [shifted(pieces[2], axis, 1), shifted(pieces[3], axis, -1)]


def near_coming(leaving, axis):
    return [shifted(value, axis, shift) for shift, value in zip((1, -1), leaving)]


def return_near(pieces, leaving, axis):
    return total([pieces[0]] + near_coming(leaving, axis), bf16)


def split_three(value):
    high = lax.reduce_precision(value, 8, 7)
    rest = value - high
    middle = lax.reduce_precision(rest, 8, 7)
    return high, middle, rest - middle


def contract(a, b, dims):
    return lax.dot_general(a, b, (dims, ((), ())), preferred_element_type=f32)


def struct(shape, dtype=f32):
    return jax.ShapeDtypeStruct(shape, dtype)


def call(body, args, outs, scratch=(), flops=0, hbm=(), free=(), vmem=8, loose=False):
    specs, operands = [], []
    for i, arg in enumerate(args):
        if i == 0:
            specs.append(pl.BlockSpec(memory_space=pltpu.SMEM))
        elif i in hbm:
            specs.append(pl.BlockSpec(memory_space=pl.ANY))
            arg = pltpu.with_memory_space_constraint(arg, pltpu.HBM)
        else:
            specs.append(pl.BlockSpec(memory_space=pltpu.VMEM))
            arg = arg if loose else pltpu.with_memory_space_constraint(arg, pltpu.VMEM)
        operands.append(arg)
    kept = [s if loose or i in free else pltpu.VMEM(s.shape, s.dtype) for i, s in enumerate(outs)]
    return pl.pallas_call(
        body,
        in_specs=specs,
        out_specs=[pl.BlockSpec(memory_space=pltpu.VMEM)] * len(outs),
        out_shape=kept,
        scratch_shapes=list(scratch),
        compiler_params=pltpu.CompilerParams(vmem_limit_bytes=vmem * 1024 * 1024),
        cost_estimate=pl.CostEstimate(flops=flops, bytes_accessed=0, transcendentals=0),
    )(*operands)


def row_of_lane_sums(block):
    return jnp.sum(block.T, axis=0, keepdims=True)


def lanes_to_rows(row):
    return jnp.broadcast_to(row, (128, row.shape[1])).T


def rem(value, n):
    return lax.rem(value, jnp.int32(n))


def spans(rows, size):
    return [slice(at, min(at + size, rows)) for at in range(0, rows, size)]


def pieces_at(pieces):
    at = 0
    for piece in pieces:
        yield slice(at, at + piece.shape[0]), piece
        at += piece.shape[0]


def row_index(rows, columns, start=0):
    return (lax.broadcasted_iota(jnp.int32, (rows, columns), 0) + start).astype(f32)


def total_body(meta, *refs):
    value = refs[0][...].astype(f32)
    for ref in refs[1:-1]:
        value = value + ref[...].astype(f32)
    refs[-1][...] = value.astype(refs[-1].dtype)


def total(parts, dtype):
    meta = jnp.zeros((1,), jnp.int32)
    return call(total_body, [meta] + list(parts), [struct(parts[0].shape, dtype)], loose=True)[0]


def total_slots_body(size, meta, ref, loss_ref, out_ref):
    value = ref[0].astype(f32)
    for s in range(1, ref.shape[0]):
        value = value + ref[s].astype(f32)
    n = value.shape[0]
    out_ref[:n] = value
    own = loss_ref[0:1, :size]
    own = pltpu.roll(own, rem(size - meta[4], size), 1)
    out_ref[n:] = jnp.zeros((8, value.shape[1]), f32)
    out_ref[n : n + 1, :size] = own


def total_slots(meta, stacked, loss, size):
    def body(*refs):
        total_slots_body(size, *refs)

    shape = (stacked.shape[1] + 8, stacked.shape[2])
    return call(body, [meta, stacked, loss], [struct(shape)], loose=True)[0]


def join_body(meta, ahead_ref, up_ref, behind_ref, down_ref, ahead_out, behind_out):
    cut = up_ref.shape[0]
    ahead_out[:cut] = (ahead_ref[:cut].astype(f32) + up_ref[...].astype(f32)).astype(bf16)
    ahead_out[cut:] = ahead_ref[cut:]
    behind_out[:cut] = behind_ref[:cut]
    behind_out[cut:] = (behind_ref[cut:].astype(f32) + down_ref[...].astype(f32)).astype(bf16)


def join(pieces, far):
    if len(pieces) == 2:
        return far
    meta = jnp.zeros((1,), jnp.int32)
    shape = struct(pieces[1].shape, bf16)
    return call(join_body, [meta, pieces[4], far[0], pieces[1], far[1]], [shape, shape], loose=True)


def project_body(
    meta, q_ref, p_ref, w_ref, qo_ref, po_ref, square_ref, x_ref, acc_ref, head_ref, sems
):
    n_q = q_ref.shape[0]
    depth, width = w_ref.shape
    chunk = min(CHUNK, depth)
    loads = [
        pltpu.make_async_copy(q_ref, x_ref.at[pl.ds(0, n_q)], sems.at[0]),
        pltpu.make_async_copy(p_ref, x_ref.at[pl.ds(n_q, p_ref.shape[0])], sems.at[1]),
    ]
    blocks = []
    for at in spans(depth, chunk):
        rows = pl.ds(at.start, chunk)
        blocks.append(pltpu.make_async_copy(w_ref.at[rows], head_ref.at[rows], sems.at[2 + len(blocks)]))
    for load in loads:
        load.start()
    for block in blocks:
        block.start()
    for load in loads:
        load.wait()
    for i, at in enumerate(spans(depth, chunk)):
        blocks[i].wait()
        part = contract(x_ref[:, at], head_ref[at], ((1,), (0,)))
        acc_ref[...] = part if i == 0 else acc_ref[...] + part
    qo_ref[...] = acc_ref[:n_q]
    po_ref[...] = acc_ref[n_q:]
    square = jnp.zeros((acc_ref.shape[0], 128), f32)
    for at in range(0, width, 128):
        block = acc_ref[:, at : at + 128]
        square = square + block * block
    padded = jnp.concatenate([square[:n_q], jnp.zeros((128 - n_q, 128), f32)], axis=0)
    square_ref[:, :128] = row_of_lane_sums(padded)
    square_ref[:, 128:] = row_of_lane_sums(square[n_q:])


def project(meta, queries, passages, weight):
    n_q, n_p, (depth, width) = queries.shape[0], passages.shape[0], weight.shape
    copies = 2 + depth // min(CHUNK, depth)
    return call(
        project_body,
        [meta, queries, passages, weight],
        [struct((n_q, width)), struct((n_p, width)), struct((1, 128 + n_p))],
        [
            pltpu.VMEM((n_q + n_p, depth), bf16),
            pltpu.VMEM((n_q + n_p, width), f32),
            pltpu.VMEM((depth, width), bf16),
            pltpu.SemaphoreType.DMA((copies,)),
        ],
        2 * (n_q + n_p) * depth * width,
        hbm=(1, 2, 3),
        vmem=18,
    )


def normalize_body(
    meta, q_ref, p_ref, own_ref, got_ref, aux_ref, message_ref, unit_ref, embed_ref, inv_ref
):
    n_q, width = q_ref.shape
    inv = lanes_to_rows(lax.rsqrt(own_ref[...] + got_ref[...] + 1e-06))
    inv_ref[:n_q] = inv[:n_q]
    inv_ref[n_q:] = inv[128:]
    q_unit = q_ref[...] * inv[:n_q, :1]
    p_unit = p_ref[...] * inv[128:, :1]
    unit_ref[:n_q] = q_unit
    unit_ref[n_q:] = p_unit
    embed_ref[...] = p_unit.astype(bf16)
    half = n_q // 2
    first = meta[0] == 0

    def store(columns, value):
        top, bottom = value[:half], value[half:]
        upper, lower = jnp.where(first, top, bottom), jnp.where(first, bottom, top)
        for s in range(message_ref.shape[0]):
            message_ref[s, :half, columns] = upper.astype(bf16)
            message_ref[s, half:, columns] = lower.astype(bf16)

    store(slice(0, width), q_unit)
    store(slice(width, width + AUX), aux_ref[...])


def normalize(meta, q_proj, p_proj, square, square_got, aux, copies):
    (n_q, width), n_p = q_proj.shape, p_proj.shape[0]
    return call(
        normalize_body,
        [meta, q_proj, p_proj, square, square_got, aux],
        [
            struct((copies, n_q, width + AUX), bf16),
            struct((n_q + n_p, width)),
            struct((n_p, width), bf16),
            struct((n_q + n_p, 128)),
        ],
    )


def owner_of(meta, line, n_y, slots):
    return (rem(meta[3] - line + n_y, n_y) * slots + meta[1]).astype(f32)


def score_sent_body(n_pieces, meta, *refs):
    q_refs, p_refs = refs[:n_pieces[0]], refs[n_pieces[0] : sum(n_pieces)]
    score_ref, own_ref, other_ref, all_ref, aux_ref, aux_other_ref = refs[sum(n_pieces) :]
    width = own_ref.shape[1]
    at = 0
    for ref in q_refs:
        value = ref[...].reshape(-1, 2, 16, ref.shape[1])
        rows = value.shape[0] * 16
        for i, (to_ref, aux) in enumerate(((own_ref, aux_ref), (other_ref, aux_other_ref))):
            side = value[:, i].reshape(rows, -1)
            to_ref[at : at + rows] = side[:, :width]
            aux[at : at + rows] = side[:, width:].astype(f32)
        at += rows
    for at, ref in pieces_at(p_refs):
        all_ref[at] = ref[...]
        score_ref[at] = contract(ref[...], other_ref[...], ((1,), (1,)))


def score_sent(meta, q_pieces, p_pieces):
    width = p_pieces[0].shape[1]
    passages = sum(p.shape[0] for p in p_pieces)
    rows = sum(q.shape[0] for q in q_pieces) // 2

    def body(*refs):
        score_sent_body((len(q_pieces), len(p_pieces)), *refs)

    return call(
        body,
        [meta] + q_pieces + p_pieces,
        [
            struct((passages, rows)),
            struct((rows, width), bf16),
            struct((rows, width), bf16),
            struct((passages, width), bf16),
            struct((rows, AUX)),
            struct((rows, AUX)),
        ],
        flops=2 * rows * passages * width,
    )


def count_body(slots, meta, aux_ref, other_ref, info_ref, count_ref):
    block = count_ref.shape[1]
    info_ref[...] = aux_ref[...].T
    owners = (lax.broadcasted_iota(jnp.int32, (8, 1), 0) * slots + meta[1]).astype(f32)
    count = jnp.zeros(count_ref.shape, f32)
    for info in (info_ref[...], other_ref[...].T):
        owned = (info[0:1] == owners).astype(f32).astype(bf16)
        placed = info[INDEX : INDEX + 1] == row_index(block, info.shape[1])
        count = count + contract(owned, placed.astype(f32).astype(bf16), ((1,), (1,)))
    count_ref[...] = count


def count_positives(meta, aux, aux_other, block, slots):
    def body(*refs):
        count_body(slots, *refs)

    return call(
        body, [meta, aux, aux_other], [struct((AUX, aux.shape[0])), struct((8, block))]
    )


def score_kept_body(n_y, slots, per_query, meta, q_ref, p_ref, info_ref, score_ref, weight_ref):
    passages, rows = score_ref.shape
    block = passages // n_y
    for line in range(n_y):
        owner = owner_of(meta, line, n_y, slots)
        place = jnp.where(info_ref[:INDEX] == owner, info_ref[INDEX : 2 * INDEX], -1.0)
        at = slice(line * block, (line + 1) * block)
        score_ref[at] = contract(p_ref[at], q_ref[...], ((1,), (1,)))
        for span in spans(block, 32):
            row = row_index(span.stop - span.start, rows, span.start)
            weight = (place[1:2] == row).astype(f32)
            for k in range(2, per_query):
                weight = weight + (place[k : k + 1] == row).astype(f32)
            weight_ref[line * block + span.start : line * block + span.stop] = weight


def score_kept(meta, q_own, p_all, info, n_y, slots, per_query):
    passages, rows = p_all.shape[0], q_own.shape[0]

    def body(*refs):
        score_kept_body(n_y, slots, per_query, *refs)

    return call(
        body,
        [meta, q_own, p_all, info],
        [struct((passages, rows)), struct((passages, rows))],
        flops=4 * rows * passages * p_all.shape[1],
    )


def positive_place(meta, line, n_y, slots, info_ref):
    owner = owner_of(meta, line, n_y, slots)
    return jnp.where(info_ref[0:1] == owner, info_ref[INDEX : INDEX + 1], -1.0)


def turned_slots(meta, n_x, rows):
    size = rows // n_x
    for s in range(n_x):
        start = pl.multiple_of(rem(meta[2] - s + n_x, n_x) * size, size)
        yield slice(s * size, (s + 1) * size), pl.ds(start, size)


def weigh_body(
    n_y, n_x, slots, meta, kept_ref, got_ref, weight_ref, info_ref, *rest_refs
):
    counts_ref, (e_ref, sum_ref) = rest_refs[:-2], rest_refs[-2:]
    passages, rows = kept_ref.shape
    block = passages // n_y
    counts = counts_ref[0][...]
    for ref in counts_ref[1:]:
        counts = counts + ref[...]
    rest = jnp.zeros((128 - counts.shape[0], block), f32)
    counts = jnp.concatenate([counts, rest], axis=0).T
    lane = lax.broadcasted_iota(jnp.int32, (1, 128), 1)
    sums = [jnp.zeros((8, rows), f32), jnp.zeros((8, rows), f32)]
    for line in range(n_y):
        mine = lane == rem(meta[3] - line + n_y, n_y)
        count = jnp.sum(jnp.where(mine, counts, 0.0), axis=1, keepdims=True)
        place = positive_place(meta, line, n_y, slots, info_ref)
        for span in spans(block, 32):
            at = slice(line * block + span.start, line * block + span.stop)
            score = (kept_ref[at] + got_ref[at]) * sharpness
            weighted = (weight_ref[at] + count[span]) * jnp.exp(score)
            e_ref[at] = weighted
            own = jnp.where(place == row_index(span.stop - span.start, rows, span.start), score, 0.0)
            sums[0] = sums[0] + jnp.sum(weighted.reshape(-1, 8, rows), axis=0)
            sums[1] = sums[1] + jnp.sum(own.reshape(-1, 8, rows), axis=0)
    for i in range(2):
        row = jnp.sum(sums[i], axis=0, keepdims=True)
        for here, there in turned_slots(meta, n_x, rows):
            sum_ref[i : i + 1, there] = row[:, here]


def weigh(meta, kept, got, weight, info, counts, n_y, n_x, slots):
    passages, rows = kept.shape

    def body(*refs):
        weigh_body(n_y, n_x, slots, *refs)

    return call(
        body,
        [meta, kept, got, weight, info, *counts],
        [struct((passages, rows)), struct((2, rows))],
    )


def slope_body(n_y, n_x, slots, meta, e_ref, sums_ref, info_ref, grad_ref, loss_ref, scale_ref, inv_ref):
    passages, rows = e_ref.shape
    block = passages // n_y
    loss_ref[...] = jnp.sum(sums_ref[...], axis=0)
    for here, there in turned_slots(meta, n_x, rows):
        inv_ref[:, here] = loss_ref[0:1, there]
    for here, there in turned_slots(meta, n_x, rows):
        scale_ref[:, here] = loss_ref[1:2, there]
    sums = inv_ref[...]
    loss_ref[0:1] = jnp.log(sums) - scale_ref[...]
    inv = 1.0 / sums
    base = 2 * INDEX
    scale = (info_ref[base : base + 1] + info_ref[base + 1 : base + 2]) + info_ref[base + 2 : base + 3]
    scale = scale * sharpness
    for line in range(n_y):
        place = positive_place(meta, line, n_y, slots, info_ref)
        for span in spans(block, 32):
            at = slice(line * block + span.start, line * block + span.stop)
            match = (place == row_index(span.stop - span.start, rows, span.start)).astype(f32)
            grad_ref[at] = (scale * (e_ref[at] * inv - match)).astype(bf16)


def slopes(meta, e, sums, info, n_y, n_x, slots):
    passages, rows = e.shape

    def body(*refs):
        slope_body(n_y, n_x, slots, *refs)

    return call(
        body,
        [meta, e, sums, info],
        [struct((passages, rows), bf16), struct((2, rows))],
        [pltpu.VMEM((1, rows), f32), pltpu.VMEM((1, rows), f32)],
    )


def query_part_body(meta, grad_ref, p_ref, out_ref, turned_ref):
    turned_ref[...] = grad_ref[...].T
    for at in spans(p_ref.shape[1], TILE):
        out_ref[:, at] = contract(turned_ref[...], p_ref[:, at], ((1,), (0,))).astype(bf16)


def query_part(meta, grad, p_all):
    (passages, rows), width = grad.shape, p_all.shape[1]
    return call(
        query_part_body,
        [meta, grad, p_all],
        [struct((rows, width), bf16)],
        [pltpu.VMEM((rows, passages), bf16)],
        2 * rows * passages * width,
    )[0]


def query_rest_body(meta, grad_ref, p_ref, first_ref, *refs):
    out_refs, turned_ref = refs[:-1], refs[-1]
    turned_ref[...] = grad_ref[...].T
    for span in spans(p_ref.shape[1], TILE):
        rest = contract(turned_ref[...], p_ref[:, span], ((1,), (0,))).astype(bf16)
        at = 0
        for ref in out_refs:
            rows = ref.shape[0] * 16
            for i, value in enumerate((first_ref[at : at + rows, span], rest[at : at + rows])):
                ref[:, i, :, span] = value.reshape(-1, 16, value.shape[1])
            at += rows


def query_rest(meta, grad, p_all, first, shapes):
    (passages, rows), width = grad.shape, p_all.shape[1]
    return call(
        query_rest_body,
        [meta, grad, p_all, first],
        [struct((n // 32, 2, 16, width), bf16) for n in shapes],
        [pltpu.VMEM((rows, passages), bf16)],
        2 * rows * passages * width,
    )


def passage_part_body(meta, grad_ref, other_ref, own_ref, q_ref, *out_refs):
    for at, ref in pieces_at(out_refs):
        value = contract(grad_ref[at], own_ref[...], ((1,), (0,)))
        value = value + contract(other_ref[at], q_ref[...], ((1,), (0,)))
        ref[...] = value.astype(bf16)


def passage_part(meta, grad, other, q_own, q_other, shapes):
    (passages, rows), width = grad.shape, q_own.shape[1]
    return call(
        passage_part_body,
        [meta, grad, other, q_own, q_other],
        [struct((n, width), bf16) for n in shapes],
        flops=4 * rows * passages * width,
    )


def head_rows_body(meta, w_ref, wo_ref, keep_ref, got_ref, sems):
    half = keep_ref.shape[0]
    copies = []
    for at in spans(half, CHUNK):
        rows = pl.ds(pl.multiple_of(meta[0] * half + at.start, CHUNK), at.stop - at.start)
        to = pl.ds(at.start, at.stop - at.start)
        for from_ref, to_ref in ((w_ref, keep_ref), (wo_ref, got_ref)):
            sem = sems.at[len(copies)]
            copies.append(pltpu.make_async_copy(from_ref.at[rows], to_ref.at[to], sem))
    for copy in copies:
        copy.start()
    for copy in copies:
        copy.wait()


def head_rows(meta, weight, weight_got):
    depth, width = weight.shape
    shape = struct((depth // 2, width), bf16)
    count = 2 * len(spans(depth // 2, CHUNK))
    return call(
        head_rows_body,
        [meta, weight, weight_got],
        [shape, shape],
        [pltpu.SemaphoreType.DMA((count,))],
        hbm=(1, 2),
        vmem=4,
    )


def tangent(grad, other, unit, beyond, inv):
    radial = jnp.sum(unit * grad + beyond * other, axis=1, keepdims=True)
    return (inv * (grad - unit * radial)).astype(bf16), (inv * (other - beyond * radial)).astype(bf16)


def finish_body(
    meta, qg_ref, qgo_ref, pg_ref, pgo_ref, unit_ref, beyond_ref, inv_ref, w_ref, wo_ref,
    q_out, p_out, loss_out, here_ref, there_ref
):
    n_q = q_out.shape[0]
    part = n_q // 2
    first = meta[0] == 0
    turn = lambda rows: jnp.concatenate([rows[part:], rows[:part]], axis=0)
    grad, other = qg_ref[:n_q], qgo_ref[:n_q]
    grad, other = jnp.where(first, grad, turn(grad)), jnp.where(first, turn(other), other)
    here_ref[:n_q], there_ref[:n_q] = tangent(
        grad, other, unit_ref[:n_q], beyond_ref[:n_q], inv_ref[:n_q, :1]
    )
    own, got = qg_ref[n_q : n_q + 1, :128], qgo_ref[n_q : n_q + 1, :128]
    low, high = jnp.where(first, own, got), jnp.where(first, got, own)
    lane = lax.broadcasted_iota(jnp.int32, (1, 128), 1)
    loss_out[...] = jnp.where(lane < part, low, pltpu.roll(high, part, 1))
    for at in spans(pg_ref.shape[0], 64):
        to = slice(n_q + at.start, n_q + at.stop)
        here_ref[to], there_ref[to] = tangent(
            pg_ref[at].astype(f32), pgo_ref[at].astype(f32), unit_ref[to], beyond_ref[to], inv_ref[to, :1]
        )
    for at in spans(w_ref.shape[0], CHUNK):
        state = contract(here_ref[...], w_ref[at], ((1,), (1,)))
        state = (state + contract(there_ref[...], wo_ref[at], ((1,), (1,)))).astype(bf16)
        q_out[:, at] = state[:n_q]
        p_out[:, at] = state[n_q:]


def finish(meta, rows_in, weight, weight_got):
    out_width, width = weight.shape
    n, n_p = rows_in[4].shape[0], rows_in[2].shape[0]
    return call(
        finish_body,
        [meta, *rows_in, weight, weight_got],
        [struct((n - n_p, out_width), bf16), struct((n_p, out_width), bf16), struct((1, 128))],
        [
            pltpu.VMEM((n, width), bf16),
            pltpu.VMEM((n, width), bf16),
        ],
        4 * n * out_width * width,
        free=(0, 1, 2),
    )


def per_device(query_states, passage_states, head_weight, positives, negatives, slope):
    n_y, n_x, n_z = (lax.axis_size(a) for a in ("y", "x", "z"))
    y, x, z, core = (lax.axis_index(a) for a in ("y", "x", "z", "mp"))
    q_rows, p_rows = query_states.shape[0], passage_states.shape[0]
    width = head_weight.shape[1]
    half = q_rows // 2
    slots = n_x * n_z
    column = x * n_z + z
    meta = jnp.stack([core, column, x, y, z * half]).astype(jnp.int32)

    q_proj, p_proj, square = project(meta, query_states, passage_states, head_weight)
    square_got = shifted(square, "mp", 1)
    ids = jnp.concatenate([positives[:, None], negatives], axis=1)
    per_query = ids.shape[1]
    padded = ((0, 0), (0, INDEX - per_query))
    aux = jnp.concatenate(
        [jnp.pad((ids // p_rows).astype(f32), padded), jnp.pad((ids % p_rows).astype(f32), padded)]
        + [part[:, None] for part in split_three(slope)],
        axis=1,
    )
    aux = jnp.pad(aux, ((0, 0), (0, AUX - aux.shape[1])))
    message, unit, p_embed, inv = normalize(
        meta, q_proj, p_proj, square, square_got, aux, n_z
    )
    unit_got = shifted(unit, "mp", 1)
    weight_got = shifted(after(head_weight, unit), "mp", 1)
    p_near = ring_near(p_embed, "y")
    q_z = exchanged(message, "z").reshape(n_z * q_rows, width + AUX)
    q_z = after(q_z, unit_got, weight_got, *p_near)
    q_near = ring_near(q_z, "x")
    q_pieces = ring_far(q_z, q_near, "x")
    p_pieces = ring_far(p_embed, [after(piece, *q_near) for piece in p_near], "y")
    q_shapes, p_shapes = ([piece.shape[0] for piece in pieces] for pieces in (q_pieces, p_pieces))
    sent, q_own, q_other, p_all, aux, aux_other = score_sent(meta, q_pieces, p_pieces)
    got = shifted(sent, "mp", 1)
    info, count = count_positives(meta, aux, aux_other, p_rows, slots)
    counts = [count] + [shifted(count, "y", s) for s in range(1, n_y)]
    kept, named = score_kept(meta, q_own, p_all, info, n_y, slots, per_query)
    e, sums = weigh(meta, kept, got, named, info, counts, n_y, n_x, slots)
    sums = to_all(sums, ("x", "z")).reshape((slots,) + sums.shape)
    grad, loss = slopes(meta, e, sums, info, n_y, n_x, slots)
    grad_got = shifted(grad, "mp", 1)
    q_part = query_part(meta, grad, p_all)
    grad_got = after(grad_got, q_part)
    p_parts = passage_part(meta, grad, grad_got, q_own, q_other, p_shapes)
    q_parts = query_rest(meta, grad_got, p_all, q_part, q_shapes)
    q_parts = [part.reshape(-1, width) for part in q_parts]
    p_far, q_far = return_far(p_parts, "y"), return_far(q_parts, "x")
    q_leaving = join(q_parts, q_far)
    p_leaving = join(p_parts, [after(p_far[0], *q_leaving)] + p_far[1:])
    p_coming = near_coming(p_leaving, "y")
    q_part = return_near(q_parts, q_leaving, "x")
    weight, weight_got = head_rows(after(meta, *q_leaving), head_weight, weight_got)
    q_part = after(q_part, *p_coming, weight, weight_got)
    back = exchanged(q_part.reshape(n_z, q_rows, width), "z")
    p_grad = total([after(p_parts[0], back)] + p_coming, bf16)
    p_grad_got = shifted(p_grad, "mp", 1)
    q_grad = total_slots(meta, back, loss, n_z * half)
    q_grad_got = shifted(q_grad, "mp", 1)
    query_grads, passage_grads, losses = finish(
        meta, (q_grad, q_grad_got, p_grad, p_grad_got, unit, unit_got, inv), weight, weight_got
    )
    return losses[0, :q_rows], query_grads, passage_grads


def solution(mesh):
    n_dp, n_core = mesh.devices.shape
    shape = SHAPES[n_dp] + (n_core,)
    grid = Mesh(mesh.devices.reshape(shape), ("y", "x", "z", "mp"))
    dp = ("y", "x", "z")
    placed = (P(dp, None), P(dp, None), P(None, "mp"), P(dp), P(dp, None), P(dp))
    return jax.shard_map(
        per_device,
        mesh=grid,
        in_specs=placed,
        out_specs=(P(dp), P(dp, "mp"), P(dp, "mp")),
        check_vma=False,
    )
```

```python
import jax
import jax.numpy as jnp
from jax import lax
from jax.experimental import pallas as pl
from jax.experimental.pallas import tpu as pltpu
from jax.sharding import Mesh, PartitionSpec as P

sharpness = 1.0 / 0.02
bf16 = jnp.bfloat16
f32 = jnp.float32
AUX = 128
TILE = 256
CHUNK = 512
INDEX = 16
MIB = 1024 * 1024
SHAPES = {128: (4, 4, 8), 32: (4, 4, 2), 8: (2, 2, 2)}


def shifted(value, axis, shift):
    n = lax.axis_size(axis)
    return lax.ppermute(value, axis, [(i, (i + shift) % n) for i in range(n)])


def exchanged(parts, axis):
    return lax.all_to_all(parts, axis, split_axis=0, concat_axis=0, tiled=True)


def to_all(value, axis):
    n = lax.axis_size(axis)
    return exchanged(jnp.broadcast_to(value[None], (n,) + value.shape), axis)


def after(value, *others):
    return lax.optimization_barrier((value, *others))[0]


def ring_near(value, axis):
    shifts = (1, -1) if lax.axis_size(axis) > 2 else (1,)
    return [shifted(value, axis, shift) for shift in shifts]


def ring_far(value, near, axis):
    if len(near) == 1:
        return [value] + near
    cut = value.shape[0] // 2
    before, behind = near
    return [value, before, shifted(before[:cut], axis, 1), shifted(behind[cut:], axis, -1), behind]


def return_far(pieces, axis):
    if len(pieces) == 2:
        return [pieces[1]]
    return [shifted(pieces[2], axis, 1), shifted(pieces[3], axis, -1)]


def near_coming(leaving, axis):
    return [shifted(value, axis, shift) for shift, value in zip((1, -1), leaving)]


def return_near(pieces, leaving, axis):
    return total([pieces[0]] + near_coming(leaving, axis), bf16)


def split_three(value):
    high = lax.reduce_precision(value, 8, 7)
    rest = value - high
    middle = lax.reduce_precision(rest, 8, 7)
    return high, middle, rest - middle


def contract(a, b, dims):
    return lax.dot_general(a, b, (dims, ((), ())), preferred_element_type=f32)


def struct(shape, dtype=f32):
    return jax.ShapeDtypeStruct(shape, dtype)


def call(body, args, outs, scratch=(), flops=0, hbm=(), free=(), vmem=8, loose=False):
    specs, operands = [], []
    for i, arg in enumerate(args):
        if i == 0:
            specs.append(pl.BlockSpec(memory_space=pltpu.SMEM))
        elif i in hbm:
            specs.append(pl.BlockSpec(memory_space=pl.ANY))
            arg = pltpu.with_memory_space_constraint(arg, pltpu.HBM)
        else:
            specs.append(pl.BlockSpec(memory_space=pltpu.VMEM))
            arg = arg if loose else pltpu.with_memory_space_constraint(arg, pltpu.VMEM)
        operands.append(arg)
    kept = [s if loose or i in free else pltpu.VMEM(s.shape, s.dtype) for i, s in enumerate(outs)]
    return pl.pallas_call(
        body,
        in_specs=specs,
        out_specs=[pl.BlockSpec(memory_space=pltpu.VMEM)] * len(outs),
        out_shape=kept,
        scratch_shapes=list(scratch),
        compiler_params=pltpu.CompilerParams(vmem_limit_bytes=vmem * 1024 * 1024),
        cost_estimate=pl.CostEstimate(flops=flops, bytes_accessed=0, transcendentals=0),
    )(*operands)


def row_of_lane_sums(block):
    return jnp.sum(block.T, axis=0, keepdims=True)


def lanes_to_rows(row):
    return jnp.broadcast_to(row, (128, row.shape[1])).T


def rem(value, n):
    return lax.rem(value, jnp.int32(n))


def spans(rows, size):
    return [slice(at, min(at + size, rows)) for at in range(0, rows, size)]


def pieces_at(pieces):
    at = 0
    for piece in pieces:
        yield slice(at, at + piece.shape[0]), piece
        at += piece.shape[0]


def row_index(rows, columns, start=0):
    return (lax.broadcasted_iota(jnp.int32, (rows, columns), 0) + start).astype(f32)


def total_body(meta, *refs):
    value = refs[0][...].astype(f32)
    for ref in refs[1:-1]:
        value = value + ref[...].astype(f32)
    refs[-1][...] = value.astype(refs[-1].dtype)


def total(parts, dtype):
    meta = jnp.zeros((1,), jnp.int32)
    return call(total_body, [meta] + list(parts), [struct(parts[0].shape, dtype)], loose=True)[0]


def total_slots_body(size, meta, ref, loss_ref, out_ref):
    value = ref[0].astype(f32)
    for s in range(1, ref.shape[0]):
        value = value + ref[s].astype(f32)
    n = value.shape[0]
    out_ref[:n] = value
    own = loss_ref[0:1, :size]
    own = pltpu.roll(own, rem(size - meta[4], size), 1)
    out_ref[n:] = jnp.zeros((8, value.shape[1]), f32)
    out_ref[n : n + 1, :size] = own


def total_slots(meta, stacked, loss, size):
    def body(*refs):
        total_slots_body(size, *refs)

    shape = (stacked.shape[1] + 8, stacked.shape[2])
    return call(body, [meta, stacked, loss], [struct(shape)], loose=True)[0]


def join_body(meta, ahead_ref, up_ref, behind_ref, down_ref, ahead_out, behind_out):
    cut = up_ref.shape[0]
    ahead_out[:cut] = (ahead_ref[:cut].astype(f32) + up_ref[...].astype(f32)).astype(bf16)
    ahead_out[cut:] = ahead_ref[cut:]
    behind_out[:cut] = behind_ref[:cut]
    behind_out[cut:] = (behind_ref[cut:].astype(f32) + down_ref[...].astype(f32)).astype(bf16)


def join(pieces, far):
    if len(pieces) == 2:
        return far
    meta = jnp.zeros((1,), jnp.int32)
    shape = struct(pieces[1].shape, bf16)
    return call(join_body, [meta, pieces[4], far[0], pieces[1], far[1]], [shape, shape], loose=True)


def project_body(
    meta, q_ref, p_ref, w_ref, qo_ref, po_ref, square_ref, x_ref, acc_ref, head_ref, sems
):
    n_q = q_ref.shape[0]
    depth, width = w_ref.shape
    chunk = min(CHUNK, depth)
    loads = [
        pltpu.make_async_copy(q_ref, x_ref.at[pl.ds(0, n_q)], sems.at[0]),
        pltpu.make_async_copy(p_ref, x_ref.at[pl.ds(n_q, p_ref.shape[0])], sems.at[1]),
    ]
    blocks = []
    for at in spans(depth, chunk):
        rows = pl.ds(at.start, chunk)
        blocks.append(pltpu.make_async_copy(w_ref.at[rows], head_ref.at[rows], sems.at[2 + len(blocks)]))
    for load in loads:
        load.start()
    for block in blocks:
        block.start()
    for load in loads:
        load.wait()
    for i, at in enumerate(spans(depth, chunk)):
        blocks[i].wait()
        part = contract(x_ref[:, at], head_ref[at], ((1,), (0,)))
        acc_ref[...] = part if i == 0 else acc_ref[...] + part
    qo_ref[...] = acc_ref[:n_q]
    po_ref[...] = acc_ref[n_q:]
    square = jnp.zeros((acc_ref.shape[0], 128), f32)
    for at in range(0, width, 128):
        block = acc_ref[:, at : at + 128]
        square = square + block * block
    padded = jnp.concatenate([square[:n_q], jnp.zeros((128 - n_q, 128), f32)], axis=0)
    square_ref[:, :128] = row_of_lane_sums(padded)
    square_ref[:, 128:] = row_of_lane_sums(square[n_q:])


def project(meta, queries, passages, weight):
    n_q, n_p, (depth, width) = queries.shape[0], passages.shape[0], weight.shape
    copies = 2 + depth // min(CHUNK, depth)
    return call(
        project_body,
        [meta, queries, passages, weight],
        [struct((n_q, width)), struct((n_p, width)), struct((1, 128 + n_p))],
        [
            pltpu.VMEM((n_q + n_p, depth), bf16),
            pltpu.VMEM((n_q + n_p, width), f32),
            pltpu.VMEM((depth, width), bf16),
            pltpu.SemaphoreType.DMA((copies,)),
        ],
        2 * (n_q + n_p) * depth * width,
        hbm=(1, 2, 3),
        vmem=18,
    )


def normalize_body(
    meta, q_ref, p_ref, own_ref, got_ref, aux_ref, message_ref, unit_ref, embed_ref, inv_ref
):
    n_q, width = q_ref.shape
    inv = lanes_to_rows(lax.rsqrt(own_ref[...] + got_ref[...] + 1e-06))
    inv_ref[:n_q] = inv[:n_q]
    inv_ref[n_q:] = inv[128:]
    q_unit = q_ref[...] * inv[:n_q, :1]
    p_unit = p_ref[...] * inv[128:, :1]
    unit_ref[:n_q] = q_unit
    unit_ref[n_q:] = p_unit
    embed_ref[...] = p_unit.astype(bf16)
    half = n_q // 2
    first = meta[0] == 0

    def store(columns, value):
        top, bottom = value[:half], value[half:]
        upper, lower = jnp.where(first, top, bottom), jnp.where(first, bottom, top)
        for s in range(message_ref.shape[0]):
            message_ref[s, :half, columns] = upper.astype(bf16)
            message_ref[s, half:, columns] = lower.astype(bf16)

    store(slice(0, width), q_unit)
    store(slice(width, width + AUX), aux_ref[...])


def normalize(meta, q_proj, p_proj, square, square_got, aux, copies):
    (n_q, width), n_p = q_proj.shape, p_proj.shape[0]
    return call(
        normalize_body,
        [meta, q_proj, p_proj, square, square_got, aux],
        [
            struct((copies, n_q, width + AUX), bf16),
            struct((n_q + n_p, width)),
            struct((n_p, width), bf16),
            struct((n_q + n_p, 128)),
        ],
    )


def owner_of(meta, line, n_y, slots):
    return (rem(meta[3] - line + n_y, n_y) * slots + meta[1]).astype(f32)


def side_rows(ref, i, width):
    value = ref[:, :width].reshape(-1, 2, 16, width)
    return value[:, i].reshape(value.shape[0] * 16, width)


def score_sent_body(n_pieces, meta, *refs):
    q_refs, p_refs = refs[: n_pieces[0]], refs[n_pieces[0] : sum(n_pieces)]
    score_ref, other_ref, aux_ref, aux_other_ref = refs[sum(n_pieces) :]
    width = other_ref.shape[1]
    at = 0
    for ref in q_refs:
        rows = ref.shape[0] // 2
        other_ref[at : at + rows] = side_rows(ref, 1, width)
        value = ref[:, width:].reshape(-1, 2, 16, AUX)
        for i, aux in enumerate((aux_ref, aux_other_ref)):
            aux[at : at + rows] = value[:, i].reshape(rows, AUX).astype(f32)
        at += rows
    for at, ref in pieces_at(p_refs):
        score_ref[at] = contract(ref[...], other_ref[...], ((1,), (1,)))


def score_sent(meta, q_pieces, p_pieces):
    width = p_pieces[0].shape[1]
    passages = sum(p.shape[0] for p in p_pieces)
    rows = sum(q.shape[0] for q in q_pieces) // 2

    def body(*refs):
        score_sent_body((len(q_pieces), len(p_pieces)), *refs)

    return call(
        body,
        [meta] + q_pieces + p_pieces,
        [
            struct((passages, rows)),
            struct((rows, width), bf16),
            struct((rows, AUX)),
            struct((rows, AUX)),
        ],
        flops=2 * rows * passages * width,
    )


def count_body(slots, meta, aux_ref, other_ref, info_ref, count_ref):
    block = count_ref.shape[1]
    info_ref[...] = aux_ref[...].T
    owners = (lax.broadcasted_iota(jnp.int32, (8, 1), 0) * slots + meta[1]).astype(f32)
    count = jnp.zeros(count_ref.shape, f32)
    for info in (info_ref[...], other_ref[...].T):
        owned = (info[0:1] == owners).astype(f32).astype(bf16)
        placed = info[INDEX : INDEX + 1] == row_index(block, info.shape[1])
        count = count + contract(owned, placed.astype(f32).astype(bf16), ((1,), (1,)))
    count_ref[...] = count


def count_positives(meta, aux, aux_other, block, slots):
    def body(*refs):
        count_body(slots, *refs)

    return call(
        body, [meta, aux, aux_other], [struct((AUX, aux.shape[0])), struct((8, block))]
    )


def score_kept_body(n_y, slots, per_query, n_pieces, meta, info_ref, *refs):
    q_refs, p_refs = refs[: n_pieces[0]], refs[n_pieces[0] : sum(n_pieces)]
    score_ref, weight_ref, q_ref, p_ref = refs[sum(n_pieces) :]
    passages, rows = score_ref.shape
    block = passages // n_y
    at = 0
    for ref in q_refs:
        n = ref.shape[0] // 2
        q_ref[at : at + n] = side_rows(ref, 0, q_ref.shape[1])
        at += n
    for at, ref in pieces_at(p_refs):
        p_ref[at] = ref[...]
    for line in range(n_y):
        owner = owner_of(meta, line, n_y, slots)
        place = jnp.where(info_ref[:INDEX] == owner, info_ref[INDEX : 2 * INDEX], -1.0)
        at = slice(line * block, (line + 1) * block)
        score_ref[at] = contract(p_ref[at], q_ref[...], ((1,), (1,)))
        for span in spans(block, 32):
            row = row_index(span.stop - span.start, rows, span.start)
            weight = (place[1:2] == row).astype(f32)
            for k in range(2, per_query):
                weight = weight + (place[k : k + 1] == row).astype(f32)
            weight_ref[line * block + span.start : line * block + span.stop] = weight


def score_kept(meta, info, q_pieces, p_pieces, n_y, slots, per_query):
    width = p_pieces[0].shape[1]
    passages = sum(p.shape[0] for p in p_pieces)
    rows = sum(q.shape[0] for q in q_pieces) // 2

    def body(*refs):
        score_kept_body(n_y, slots, per_query, (len(q_pieces), len(p_pieces)), *refs)

    return call(
        body,
        [meta, info] + q_pieces + p_pieces,
        [
            struct((passages, rows)),
            struct((passages, rows)),
            struct((rows, width), bf16),
            struct((passages, width), bf16),
        ],
        flops=4 * rows * passages * width,
    )


def positive_place(meta, line, n_y, slots, info_ref):
    owner = owner_of(meta, line, n_y, slots)
    return jnp.where(info_ref[0:1] == owner, info_ref[INDEX : INDEX + 1], -1.0)


def turned_slots(meta, n_x, rows):
    size = rows // n_x
    for s in range(n_x):
        start = pl.multiple_of(rem(meta[2] - s + n_x, n_x) * size, size)
        yield slice(s * size, (s + 1) * size), pl.ds(start, size)


def weigh_body(
    n_y, n_x, slots, meta, kept_ref, got_ref, weight_ref, info_ref, *rest_refs
):
    counts_ref, (e_ref, sum_ref) = rest_refs[:-2], rest_refs[-2:]
    passages, rows = kept_ref.shape
    block = passages // n_y
    counts = counts_ref[0][...]
    for ref in counts_ref[1:]:
        counts = counts + ref[...]
    rest = jnp.zeros((128 - counts.shape[0], block), f32)
    counts = jnp.concatenate([counts, rest], axis=0).T
    lane = lax.broadcasted_iota(jnp.int32, (1, 128), 1)
    sums = [jnp.zeros((8, rows), f32), jnp.zeros((8, rows), f32)]
    for line in range(n_y):
        mine = lane == rem(meta[3] - line + n_y, n_y)
        count = jnp.sum(jnp.where(mine, counts, 0.0), axis=1, keepdims=True)
        place = positive_place(meta, line, n_y, slots, info_ref)
        for span in spans(block, 32):
            at = slice(line * block + span.start, line * block + span.stop)
            score = (kept_ref[at] + got_ref[at]) * sharpness
            weighted = (weight_ref[at] + count[span]) * jnp.exp(score)
            e_ref[at] = weighted
            own = jnp.where(place == row_index(span.stop - span.start, rows, span.start), score, 0.0)
            sums[0] = sums[0] + jnp.sum(weighted.reshape(-1, 8, rows), axis=0)
            sums[1] = sums[1] + jnp.sum(own.reshape(-1, 8, rows), axis=0)
    for i in range(2):
        row = jnp.sum(sums[i], axis=0, keepdims=True)
        for here, there in turned_slots(meta, n_x, rows):
            sum_ref[i : i + 1, there] = row[:, here]


def weigh(meta, kept, got, weight, info, counts, n_y, n_x, slots):
    passages, rows = kept.shape

    def body(*refs):
        weigh_body(n_y, n_x, slots, *refs)

    return call(
        body,
        [meta, kept, got, weight, info, *counts],
        [struct((passages, rows)), struct((2, rows))],
    )


def slope_body(n_y, n_x, slots, meta, e_ref, sums_ref, info_ref, grad_ref, loss_ref, scale_ref, inv_ref):
    passages, rows = e_ref.shape
    block = passages // n_y
    loss_ref[...] = jnp.sum(sums_ref[...], axis=0)
    for here, there in turned_slots(meta, n_x, rows):
        inv_ref[:, here] = loss_ref[0:1, there]
    for here, there in turned_slots(meta, n_x, rows):
        scale_ref[:, here] = loss_ref[1:2, there]
    sums = inv_ref[...]
    loss_ref[0:1] = jnp.log(sums) - scale_ref[...]
    inv = 1.0 / sums
    base = 2 * INDEX
    scale = (info_ref[base : base + 1] + info_ref[base + 1 : base + 2]) + info_ref[base + 2 : base + 3]
    scale = scale * sharpness
    for line in range(n_y):
        place = positive_place(meta, line, n_y, slots, info_ref)
        for span in spans(block, 32):
            at = slice(line * block + span.start, line * block + span.stop)
            match = (place == row_index(span.stop - span.start, rows, span.start)).astype(f32)
            grad_ref[at] = (scale * (e_ref[at] * inv - match)).astype(bf16)


def slopes(meta, e, sums, info, n_y, n_x, slots):
    passages, rows = e.shape

    def body(*refs):
        slope_body(n_y, n_x, slots, *refs)

    return call(
        body,
        [meta, e, sums, info],
        [struct((passages, rows), bf16), struct((2, rows))],
        [pltpu.VMEM((1, rows), f32), pltpu.VMEM((1, rows), f32)],
    )


def query_part_body(meta, grad_ref, p_ref, out_ref, turned_ref):
    turned_ref[...] = grad_ref[...].T
    for at in spans(p_ref.shape[1], TILE):
        out_ref[:, at] = contract(turned_ref[...], p_ref[:, at], ((1,), (0,))).astype(bf16)


def query_part(meta, grad, p_all):
    (passages, rows), width = grad.shape, p_all.shape[1]
    return call(
        query_part_body,
        [meta, grad, p_all],
        [struct((rows, width), bf16)],
        [pltpu.VMEM((rows, passages), bf16)],
        2 * rows * passages * width,
    )[0]


def ranges_of(shapes, chosen):
    starts = [sum(shapes[:i]) for i in range(len(shapes))]
    return [slice(starts[i], starts[i] + shapes[i]) for i in chosen]


def query_rest_body(ranges, meta, grad_ref, p_ref, first_ref, *refs):
    out_refs, turned_refs = refs[: len(ranges)], refs[len(ranges) :]
    for at, ref, turned_ref in zip(ranges, out_refs, turned_refs):
        rows = slice(at.start // 2, at.stop // 2)
        turned_ref[...] = grad_ref[:, rows].T
        for span in spans(p_ref.shape[1], TILE):
            rest = contract(turned_ref[...], p_ref[:, span], ((1,), (0,))).astype(bf16)
            for i, value in enumerate((first_ref[rows, span], rest)):
                ref[:, i, :, span] = value.reshape(-1, 16, value.shape[1])


def query_rest(meta, grad, p_all, first, shapes, chosen):
    passages, width = p_all.shape
    ranges = ranges_of(shapes, chosen)

    def body(*refs):
        query_rest_body(ranges, *refs)

    parts = call(
        body,
        [meta, grad, p_all, first],
        [struct((shapes[i] // 32, 2, 16, width), bf16) for i in chosen],
        [pltpu.VMEM((shapes[i] // 2, passages), bf16) for i in chosen],
        sum(shapes[i] for i in chosen) * passages * width,
    )
    return [part.reshape(-1, width) for part in parts]


def passage_part_body(ranges, meta, grad_ref, other_ref, own_ref, q_ref, *out_refs):
    for at, ref in zip(ranges, out_refs):
        value = contract(grad_ref[at], own_ref[...], ((1,), (0,)))
        value = value + contract(other_ref[at], q_ref[...], ((1,), (0,)))
        ref[...] = value.astype(bf16)


def passage_part(meta, grad, other, q_own, q_other, shapes, chosen):
    rows, width = q_own.shape
    ranges = ranges_of(shapes, chosen)

    def body(*refs):
        passage_part_body(ranges, *refs)

    return call(
        body,
        [meta, grad, other, q_own, q_other],
        [struct((shapes[i], width), bf16) for i in chosen],
        flops=4 * rows * sum(shapes[i] for i in chosen) * width,
    )


def head_rows_body(meta, w_ref, wo_ref, keep_ref, got_ref, sems):
    half = keep_ref.shape[0]
    copies = []
    for at in spans(half, CHUNK):
        rows = pl.ds(pl.multiple_of(meta[0] * half + at.start, CHUNK), at.stop - at.start)
        to = pl.ds(at.start, at.stop - at.start)
        for from_ref, to_ref in ((w_ref, keep_ref), (wo_ref, got_ref)):
            sem = sems.at[len(copies)]
            copies.append(pltpu.make_async_copy(from_ref.at[rows], to_ref.at[to], sem))
    for copy in copies:
        copy.start()
    for copy in copies:
        copy.wait()


def head_rows(meta, weight, weight_got):
    depth, width = weight.shape
    shape = struct((depth // 2, width), bf16)
    count = 2 * len(spans(depth // 2, CHUNK))
    return call(
        head_rows_body,
        [meta, weight, weight_got],
        [shape, shape],
        [pltpu.SemaphoreType.DMA((count,))],
        hbm=(1, 2),
        vmem=4,
    )


def tangent(grad, other, unit, beyond, inv):
    radial = jnp.sum(unit * grad + beyond * other, axis=1, keepdims=True)
    return (inv * (grad - unit * radial)).astype(bf16), (inv * (other - beyond * radial)).astype(bf16)


def finish_body(
    meta, qg_ref, qgo_ref, pg_ref, pgo_ref, unit_ref, beyond_ref, inv_ref, w_ref, wo_ref,
    q_out, p_out, loss_out, here_ref, there_ref
):
    n_q = q_out.shape[0]
    part = n_q // 2
    first = meta[0] == 0
    turn = lambda rows: jnp.concatenate([rows[part:], rows[:part]], axis=0)
    grad, other = qg_ref[:n_q], qgo_ref[:n_q]
    grad, other = jnp.where(first, grad, turn(grad)), jnp.where(first, turn(other), other)
    here_ref[:n_q], there_ref[:n_q] = tangent(
        grad, other, unit_ref[:n_q], beyond_ref[:n_q], inv_ref[:n_q, :1]
    )
    own, got = qg_ref[n_q : n_q + 1, :128], qgo_ref[n_q : n_q + 1, :128]
    low, high = jnp.where(first, own, got), jnp.where(first, got, own)
    lane = lax.broadcasted_iota(jnp.int32, (1, 128), 1)
    loss_out[...] = jnp.where(lane < part, low, pltpu.roll(high, part, 1))
    for at in spans(pg_ref.shape[0], 64):
        to = slice(n_q + at.start, n_q + at.stop)
        here_ref[to], there_ref[to] = tangent(
            pg_ref[at].astype(f32), pgo_ref[at].astype(f32), unit_ref[to], beyond_ref[to], inv_ref[to, :1]
        )
    for at in spans(w_ref.shape[0], CHUNK):
        state = contract(here_ref[...], w_ref[at], ((1,), (1,)))
        state = (state + contract(there_ref[...], wo_ref[at], ((1,), (1,)))).astype(bf16)
        q_out[:, at] = state[:n_q]
        p_out[:, at] = state[n_q:]


def finish(meta, rows_in, weight, weight_got):
    out_width, width = weight.shape
    n, n_p = rows_in[4].shape[0], rows_in[2].shape[0]
    return call(
        finish_body,
        [meta, *rows_in, weight, weight_got],
        [struct((n - n_p, out_width), bf16), struct((n_p, out_width), bf16), struct((1, 128))],
        [
            pltpu.VMEM((n, width), bf16),
            pltpu.VMEM((n, width), bf16),
        ],
        4 * n * out_width * width,
        free=(0, 1, 2),
    )


def per_device(query_states, passage_states, head_weight, positives, negatives, slope):
    n_y, n_x, n_z = (lax.axis_size(a) for a in ("y", "x", "z"))
    y, x, z, core = (lax.axis_index(a) for a in ("y", "x", "z", "mp"))
    q_rows, p_rows = query_states.shape[0], passage_states.shape[0]
    width = head_weight.shape[1]
    half = q_rows // 2
    slots = n_x * n_z
    column = x * n_z + z
    meta = jnp.stack([core, column, x, y, z * half]).astype(jnp.int32)

    q_proj, p_proj, square = project(meta, query_states, passage_states, head_weight)
    square_got = shifted(square, "mp", 1)
    ids = jnp.concatenate([positives[:, None], negatives], axis=1)
    per_query = ids.shape[1]
    padded = ((0, 0), (0, INDEX - per_query))
    aux = jnp.concatenate(
        [jnp.pad((ids // p_rows).astype(f32), padded), jnp.pad((ids % p_rows).astype(f32), padded)]
        + [part[:, None] for part in split_three(slope)],
        axis=1,
    )
    aux = jnp.pad(aux, ((0, 0), (0, AUX - aux.shape[1])))
    message, unit, p_embed, inv = normalize(
        meta, q_proj, p_proj, square, square_got, aux, n_z
    )
    unit_got = shifted(unit, "mp", 1)
    weight_got = shifted(after(head_weight, unit), "mp", 1)
    p_pieces = [p_embed] + [shifted(p_embed, "y", s) for s in range(1, n_y)]
    q_z = exchanged(message, "z").reshape(n_z * q_rows, width + AUX)
    q_z = after(q_z, unit_got, weight_got)
    q_near = ring_near(q_z, "x")
    q_pieces = ring_far(q_z, q_near, "x")
    q_shapes = [piece.shape[0] for piece in q_pieces]
    p_shapes = [p_rows, p_rows, p_rows // 2, p_rows // 2, p_rows] if n_y == 4 else [p_rows, p_rows]
    sent, q_other, aux, aux_other = score_sent(meta, q_pieces, p_pieces)
    got = shifted(sent, "mp", 1)
    info, count = count_positives(meta, aux, aux_other, p_rows, slots)
    counts = [count] + [shifted(count, "y", s) for s in range(1, n_y)]
    kept, named, q_own, p_all = score_kept(
        meta, info, q_pieces, p_pieces, n_y, slots, per_query
    )
    e, sums = weigh(meta, kept, got, named, info, counts, n_y, n_x, slots)
    sums = to_all(sums, ("x", "z")).reshape((slots,) + sums.shape)
    grad, loss = slopes(meta, e, sums, info, n_y, n_x, slots)
    grad_got = shifted(grad, "mp", 1)
    q_part = query_part(meta, grad, p_all)
    grad_got = after(grad_got, q_part)
    far, near = ((2, 3), (0, 1, 4)) if len(q_shapes) > 2 else ((1,), (0,))
    q_parts, p_parts = [None] * len(q_shapes), [None] * len(p_shapes)

    def fill(parts, chosen, values):
        for i, value in zip(chosen, values):
            parts[i] = value

    fill(q_parts, far, query_rest(meta, grad_got, p_all, q_part, q_shapes, far))
    q_far = return_far(q_parts, "x")
    grad_next = after(grad_got, q_parts[far[0]])
    fill(p_parts, far, passage_part(meta, grad, grad_next, q_own, q_other, p_shapes, far))
    p_far = return_far(p_parts, "y")
    grad_last = after(grad_got, p_parts[far[0]])
    fill(q_parts, near, query_rest(meta, grad_last, p_all, q_part, q_shapes, near))
    fill(p_parts, near, passage_part(meta, grad, grad_last, q_own, q_other, p_shapes, near))
    q_leaving = join(q_parts, q_far)
    p_leaving = join(p_parts, [after(p_far[0], *q_leaving)] + p_far[1:])
    p_coming = near_coming(p_leaving, "y")
    q_part = return_near(q_parts, q_leaving, "x")
    weight, weight_got = head_rows(after(meta, *q_leaving), head_weight, weight_got)
    q_part = after(q_part, *p_coming, weight, weight_got)
    back = exchanged(q_part.reshape(n_z, q_rows, width), "z")
    p_grad = total([after(p_parts[0], back)] + p_coming, bf16)
    p_grad_got = shifted(p_grad, "mp", 1)
    q_grad = total_slots(meta, back, loss, n_z * half)
    q_grad_got = shifted(q_grad, "mp", 1)
    query_grads, passage_grads, losses = finish(
        meta, (q_grad, q_grad_got, p_grad, p_grad_got, unit, unit_got, inv), weight, weight_got
    )
    return losses[0, :q_rows], query_grads, passage_grads


def solution(mesh):
    n_dp, n_core = mesh.devices.shape
    shape = SHAPES[n_dp] + (n_core,)
    grid = Mesh(mesh.devices.reshape(shape), ("y", "x", "z", "mp"))
    dp = ("y", "x", "z")
    placed = (P(dp, None), P(dp, None), P(None, "mp"), P(dp), P(dp, None), P(dp))
    return jax.shard_map(
        per_device,
        mesh=grid,
        in_specs=placed,
        out_specs=(P(dp), P(dp, "mp"), P(dp, "mp")),
        check_vma=False,
    )
```

```python
import jax
import jax.numpy as jnp
from jax import lax
from jax.experimental import pallas as pl
from jax.experimental.pallas import tpu as pltpu
from jax.sharding import Mesh, PartitionSpec as P

sharpness = 1.0 / 0.02
bf16 = jnp.bfloat16
f32 = jnp.float32
AUX = 128
TILE = 256
CHUNK = 512
INDEX = 16
MIB = 1024 * 1024
SHAPES = {128: (4, 4, 8), 32: (4, 4, 2), 8: (2, 2, 2)}


def shifted(value, axis, shift):
    n = lax.axis_size(axis)
    return lax.ppermute(value, axis, [(i, (i + shift) % n) for i in range(n)])


def exchanged(parts, axis):
    return lax.all_to_all(parts, axis, split_axis=0, concat_axis=0, tiled=True)


def to_all(value, axis):
    n = lax.axis_size(axis)
    return exchanged(jnp.broadcast_to(value[None], (n,) + value.shape), axis)


def after(value, *others):
    return lax.optimization_barrier((value, *others))[0]


def ring_near(value, axis):
    shifts = (1, -1) if lax.axis_size(axis) > 2 else (1,)
    return [shifted(value, axis, shift) for shift in shifts]


def ring_far(value, near, axis):
    if len(near) == 1:
        return [value] + near
    cut = value.shape[0] // 2
    before, behind = near
    return [value, before, shifted(before[:cut], axis, 1), shifted(behind[cut:], axis, -1), behind]


def return_far(pieces, axis):
    if len(pieces) == 2:
        return [pieces[1]]
    return [shifted(pieces[2], axis, 1), shifted(pieces[3], axis, -1)]


def near_coming(leaving, axis):
    return [shifted(value, axis, shift) for shift, value in zip((1, -1), leaving)]


def return_near(pieces, leaving, axis):
    return total([pieces[0]] + near_coming(leaving, axis), bf16)


def split_three(value):
    high = lax.reduce_precision(value, 8, 7)
    rest = value - high
    middle = lax.reduce_precision(rest, 8, 7)
    return high, middle, rest - middle


def contract(a, b, dims):
    return lax.dot_general(a, b, (dims, ((), ())), preferred_element_type=f32)


def struct(shape, dtype=f32):
    return jax.ShapeDtypeStruct(shape, dtype)


def call(body, args, outs, scratch=(), flops=0, hbm=(), free=(), vmem=8, loose=False):
    specs, operands = [], []
    for i, arg in enumerate(args):
        if i == 0:
            specs.append(pl.BlockSpec(memory_space=pltpu.SMEM))
        elif i in hbm:
            specs.append(pl.BlockSpec(memory_space=pl.ANY))
            arg = pltpu.with_memory_space_constraint(arg, pltpu.HBM)
        else:
            specs.append(pl.BlockSpec(memory_space=pltpu.VMEM))
            arg = arg if loose else pltpu.with_memory_space_constraint(arg, pltpu.VMEM)
        operands.append(arg)
    kept = [s if loose or i in free else pltpu.VMEM(s.shape, s.dtype) for i, s in enumerate(outs)]
    return pl.pallas_call(
        body,
        in_specs=specs,
        out_specs=[pl.BlockSpec(memory_space=pltpu.VMEM)] * len(outs),
        out_shape=kept,
        scratch_shapes=list(scratch),
        compiler_params=pltpu.CompilerParams(vmem_limit_bytes=vmem * 1024 * 1024),
        cost_estimate=pl.CostEstimate(flops=flops, bytes_accessed=0, transcendentals=0),
    )(*operands)


def row_of_lane_sums(block):
    return jnp.sum(block.T, axis=0, keepdims=True)


def lanes_to_rows(row):
    return jnp.broadcast_to(row, (128, row.shape[1])).T


def rem(value, n):
    return lax.rem(value, jnp.int32(n))


def spans(rows, size):
    return [slice(at, min(at + size, rows)) for at in range(0, rows, size)]


def pieces_at(pieces):
    at = 0
    for piece in pieces:
        yield slice(at, at + piece.shape[0]), piece
        at += piece.shape[0]


def row_index(rows, columns, start=0):
    return (lax.broadcasted_iota(jnp.int32, (rows, columns), 0) + start).astype(f32)


def total_body(meta, *refs):
    value = refs[0][...].astype(f32)
    for ref in refs[1:-1]:
        value = value + ref[...].astype(f32)
    refs[-1][...] = value.astype(refs[-1].dtype)


def total(parts, dtype):
    meta = jnp.zeros((1,), jnp.int32)
    return call(total_body, [meta] + list(parts), [struct(parts[0].shape, dtype)], loose=True)[0]


def total_slots_body(size, meta, ref, loss_ref, out_ref):
    value = ref[0].astype(f32)
    for s in range(1, ref.shape[0]):
        value = value + ref[s].astype(f32)
    n = value.shape[0]
    out_ref[:n] = value
    own = loss_ref[0:1, :size]
    own = pltpu.roll(own, rem(size - meta[4], size), 1)
    out_ref[n:] = jnp.zeros((8, value.shape[1]), f32)
    out_ref[n : n + 1, :size] = own


def total_slots(meta, stacked, loss, size):
    def body(*refs):
        total_slots_body(size, *refs)

    shape = (stacked.shape[1] + 8, stacked.shape[2])
    return call(body, [meta, stacked, loss], [struct(shape)], loose=True)[0]


def join_body(meta, ahead_ref, up_ref, behind_ref, down_ref, ahead_out, behind_out):
    cut = up_ref.shape[0]
    ahead_out[:cut] = (ahead_ref[:cut].astype(f32) + up_ref[...].astype(f32)).astype(bf16)
    ahead_out[cut:] = ahead_ref[cut:]
    behind_out[:cut] = behind_ref[:cut]
    behind_out[cut:] = (behind_ref[cut:].astype(f32) + down_ref[...].astype(f32)).astype(bf16)


def join(pieces, far):
    if len(pieces) == 2:
        return far
    meta = jnp.zeros((1,), jnp.int32)
    shape = struct(pieces[1].shape, bf16)
    return call(join_body, [meta, pieces[4], far[0], pieces[1], far[1]], [shape, shape], loose=True)


def project_body(
    meta, q_ref, p_ref, w_ref, qo_ref, po_ref, square_ref, x_ref, acc_ref, head_ref, sems
):
    n_q = q_ref.shape[0]
    depth, width = w_ref.shape
    chunk = min(CHUNK, depth)
    loads = [
        pltpu.make_async_copy(q_ref, x_ref.at[pl.ds(0, n_q)], sems.at[0]),
        pltpu.make_async_copy(p_ref, x_ref.at[pl.ds(n_q, p_ref.shape[0])], sems.at[1]),
    ]
    blocks = []
    for at in spans(depth, chunk):
        rows = pl.ds(at.start, chunk)
        blocks.append(pltpu.make_async_copy(w_ref.at[rows], head_ref.at[rows], sems.at[2 + len(blocks)]))
    for load in loads:
        load.start()
    for block in blocks:
        block.start()
    for load in loads:
        load.wait()
    for i, at in enumerate(spans(depth, chunk)):
        blocks[i].wait()
        part = contract(x_ref[:, at], head_ref[at], ((1,), (0,)))
        acc_ref[...] = part if i == 0 else acc_ref[...] + part
    qo_ref[...] = acc_ref[:n_q]
    po_ref[...] = acc_ref[n_q:]
    square = jnp.zeros((acc_ref.shape[0], 128), f32)
    for at in range(0, width, 128):
        block = acc_ref[:, at : at + 128]
        square = square + block * block
    padded = jnp.concatenate([square[:n_q], jnp.zeros((128 - n_q, 128), f32)], axis=0)
    square_ref[:, :128] = row_of_lane_sums(padded)
    square_ref[:, 128:] = row_of_lane_sums(square[n_q:])


def project(meta, queries, passages, weight):
    n_q, n_p, (depth, width) = queries.shape[0], passages.shape[0], weight.shape
    copies = 2 + depth // min(CHUNK, depth)
    return call(
        project_body,
        [meta, queries, passages, weight],
        [struct((n_q, width)), struct((n_p, width)), struct((1, 128 + n_p))],
        [
            pltpu.VMEM((n_q + n_p, depth), bf16),
            pltpu.VMEM((n_q + n_p, width), f32),
            pltpu.VMEM((depth, width), bf16),
            pltpu.SemaphoreType.DMA((copies,)),
        ],
        2 * (n_q + n_p) * depth * width,
        hbm=(1, 2, 3),
        vmem=18,
    )


def normalize_body(
    meta, q_ref, p_ref, own_ref, got_ref, aux_ref, message_ref, unit_ref, embed_ref, inv_ref
):
    n_q, width = q_ref.shape
    inv = lanes_to_rows(lax.rsqrt(own_ref[...] + got_ref[...] + 1e-06))
    inv_ref[:n_q] = inv[:n_q]
    inv_ref[n_q:] = inv[128:]
    q_unit = q_ref[...] * inv[:n_q, :1]
    p_unit = p_ref[...] * inv[128:, :1]
    unit_ref[:n_q] = q_unit
    unit_ref[n_q:] = p_unit
    embed_ref[...] = p_unit.astype(bf16)
    half = n_q // 2
    first = meta[0] == 0

    def store(columns, value):
        top, bottom = value[:half], value[half:]
        upper, lower = jnp.where(first, top, bottom), jnp.where(first, bottom, top)
        for s in range(message_ref.shape[0]):
            message_ref[s, :half, columns] = upper.astype(bf16)
            message_ref[s, half:, columns] = lower.astype(bf16)

    store(slice(0, width), q_unit)
    store(slice(width, width + AUX), aux_ref[...])


def normalize(meta, q_proj, p_proj, square, square_got, aux, copies):
    (n_q, width), n_p = q_proj.shape, p_proj.shape[0]
    return call(
        normalize_body,
        [meta, q_proj, p_proj, square, square_got, aux],
        [
            struct((copies, n_q, width + AUX), bf16),
            struct((n_q + n_p, width)),
            struct((n_p, width), bf16),
            struct((n_q + n_p, 128)),
        ],
    )


def owner_of(meta, line, n_y, slots):
    return (rem(meta[3] - line + n_y, n_y) * slots + meta[1]).astype(f32)


def side_rows(ref, i, width):
    value = ref[:, :width].reshape(-1, 2, 16, width)
    return value[:, i].reshape(value.shape[0] * 16, width)


def score_sent_body(n_pieces, meta, *refs):
    q_refs, p_refs = refs[: n_pieces[0]], refs[n_pieces[0] : sum(n_pieces)]
    score_ref, other_ref, aux_ref, aux_other_ref = refs[sum(n_pieces) :]
    width = other_ref.shape[1]
    at = 0
    for ref in q_refs:
        rows = ref.shape[0] // 2
        other_ref[at : at + rows] = side_rows(ref, 1, width)
        value = ref[:, width:].reshape(-1, 2, 16, AUX)
        for i, aux in enumerate((aux_ref, aux_other_ref)):
            aux[at : at + rows] = value[:, i].reshape(rows, AUX).astype(f32)
        at += rows
    for at, ref in pieces_at(p_refs):
        score_ref[at] = contract(ref[...], other_ref[...], ((1,), (1,)))


def score_sent(meta, q_pieces, p_pieces):
    width = p_pieces[0].shape[1]
    passages = sum(p.shape[0] for p in p_pieces)
    rows = sum(q.shape[0] for q in q_pieces) // 2

    def body(*refs):
        score_sent_body((len(q_pieces), len(p_pieces)), *refs)

    return call(
        body,
        [meta] + q_pieces + p_pieces,
        [
            struct((passages, rows)),
            struct((rows, width), bf16),
            struct((rows, AUX)),
            struct((rows, AUX)),
        ],
        flops=2 * rows * passages * width,
    )


def count_body(slots, meta, aux_ref, other_ref, info_ref, count_ref):
    block = count_ref.shape[1]
    info_ref[...] = aux_ref[...].T
    owners = (lax.broadcasted_iota(jnp.int32, (8, 1), 0) * slots + meta[1]).astype(f32)
    count = jnp.zeros(count_ref.shape, f32)
    for info in (info_ref[...], other_ref[...].T):
        owned = (info[0:1] == owners).astype(f32).astype(bf16)
        placed = info[INDEX : INDEX + 1] == row_index(block, info.shape[1])
        count = count + contract(owned, placed.astype(f32).astype(bf16), ((1,), (1,)))
    count_ref[...] = count


def count_positives(meta, aux, aux_other, block, slots):
    def body(*refs):
        count_body(slots, *refs)

    return call(
        body, [meta, aux, aux_other], [struct((AUX, aux.shape[0])), struct((8, block))]
    )


def score_kept_body(n_y, slots, per_query, n_pieces, meta, info_ref, *refs):
    q_refs, p_refs = refs[: n_pieces[0]], refs[n_pieces[0] : sum(n_pieces)]
    score_ref, weight_ref, q_ref, p_ref = refs[sum(n_pieces) :]
    passages, rows = score_ref.shape
    block = passages // n_y
    at = 0
    for ref in q_refs:
        n = ref.shape[0] // 2
        q_ref[at : at + n] = side_rows(ref, 0, q_ref.shape[1])
        at += n
    for at, ref in pieces_at(p_refs):
        p_ref[at] = ref[...]
    for line in range(n_y):
        owner = owner_of(meta, line, n_y, slots)
        place = jnp.where(info_ref[:INDEX] == owner, info_ref[INDEX : 2 * INDEX], -1.0)
        at = slice(line * block, (line + 1) * block)
        score_ref[at] = contract(p_ref[at], q_ref[...], ((1,), (1,)))
        for span in spans(block, 32):
            row = row_index(span.stop - span.start, rows, span.start)
            weight = (place[1:2] == row).astype(f32)
            for k in range(2, per_query):
                weight = weight + (place[k : k + 1] == row).astype(f32)
            weight_ref[line * block + span.start : line * block + span.stop] = weight


def score_kept(meta, info, q_pieces, p_pieces, n_y, slots, per_query):
    width = p_pieces[0].shape[1]
    passages = sum(p.shape[0] for p in p_pieces)
    rows = sum(q.shape[0] for q in q_pieces) // 2

    def body(*refs):
        score_kept_body(n_y, slots, per_query, (len(q_pieces), len(p_pieces)), *refs)

    return call(
        body,
        [meta, info] + q_pieces + p_pieces,
        [
            struct((passages, rows)),
            struct((passages, rows)),
            struct((rows, width), bf16),
            struct((passages, width), bf16),
        ],
        flops=4 * rows * passages * width,
    )


def positive_place(meta, line, n_y, slots, info_ref):
    owner = owner_of(meta, line, n_y, slots)
    return jnp.where(info_ref[0:1] == owner, info_ref[INDEX : INDEX + 1], -1.0)


def turned_slots(meta, n_x, rows):
    size = rows // n_x
    for s in range(n_x):
        start = pl.multiple_of(rem(meta[2] - s + n_x, n_x) * size, size)
        yield slice(s * size, (s + 1) * size), pl.ds(start, size)


def weigh_body(
    n_y, n_x, slots, meta, kept_ref, got_ref, weight_ref, info_ref, *rest_refs
):
    counts_ref, (e_ref, sum_ref) = rest_refs[:-2], rest_refs[-2:]
    passages, rows = kept_ref.shape
    block = passages // n_y
    counts = counts_ref[0][...]
    for ref in counts_ref[1:]:
        counts = counts + ref[...]
    rest = jnp.zeros((128 - counts.shape[0], block), f32)
    counts = jnp.concatenate([counts, rest], axis=0).T
    lane = lax.broadcasted_iota(jnp.int32, (1, 128), 1)
    sums = [jnp.zeros((8, rows), f32), jnp.zeros((8, rows), f32)]
    for line in range(n_y):
        mine = lane == rem(meta[3] - line + n_y, n_y)
        count = jnp.sum(jnp.where(mine, counts, 0.0), axis=1, keepdims=True)
        place = positive_place(meta, line, n_y, slots, info_ref)
        for span in spans(block, 32):
            at = slice(line * block + span.start, line * block + span.stop)
            score = (kept_ref[at] + got_ref[at]) * sharpness
            weighted = (weight_ref[at] + count[span]) * jnp.exp(score)
            e_ref[at] = weighted
            own = jnp.where(place == row_index(span.stop - span.start, rows, span.start), score, 0.0)
            sums[0] = sums[0] + jnp.sum(weighted.reshape(-1, 8, rows), axis=0)
            sums[1] = sums[1] + jnp.sum(own.reshape(-1, 8, rows), axis=0)
    for i in range(2):
        row = jnp.sum(sums[i], axis=0, keepdims=True)
        for here, there in turned_slots(meta, n_x, rows):
            sum_ref[i : i + 1, there] = row[:, here]


def weigh(meta, kept, got, weight, info, counts, n_y, n_x, slots):
    passages, rows = kept.shape

    def body(*refs):
        weigh_body(n_y, n_x, slots, *refs)

    return call(
        body,
        [meta, kept, got, weight, info, *counts],
        [struct((passages, rows)), struct((2, rows))],
    )


def slope_body(n_y, n_x, slots, meta, e_ref, sums_ref, info_ref, grad_ref, loss_ref, scale_ref, inv_ref):
    passages, rows = e_ref.shape
    block = passages // n_y
    loss_ref[...] = jnp.sum(sums_ref[...], axis=0)
    for here, there in turned_slots(meta, n_x, rows):
        inv_ref[:, here] = loss_ref[0:1, there]
    for here, there in turned_slots(meta, n_x, rows):
        scale_ref[:, here] = loss_ref[1:2, there]
    sums = inv_ref[...]
    loss_ref[0:1] = jnp.log(sums) - scale_ref[...]
    inv = 1.0 / sums
    base = 2 * INDEX
    scale = (info_ref[base : base + 1] + info_ref[base + 1 : base + 2]) + info_ref[base + 2 : base + 3]
    scale = scale * sharpness
    for line in range(n_y):
        place = positive_place(meta, line, n_y, slots, info_ref)
        for span in spans(block, 32):
            at = slice(line * block + span.start, line * block + span.stop)
            match = (place == row_index(span.stop - span.start, rows, span.start)).astype(f32)
            grad_ref[at] = (scale * (e_ref[at] * inv - match)).astype(bf16)


def slopes(meta, e, sums, info, n_y, n_x, slots):
    passages, rows = e.shape

    def body(*refs):
        slope_body(n_y, n_x, slots, *refs)

    return call(
        body,
        [meta, e, sums, info],
        [struct((passages, rows), bf16), struct((2, rows))],
        [pltpu.VMEM((1, rows), f32), pltpu.VMEM((1, rows), f32)],
    )


def query_part_body(meta, grad_ref, p_ref, out_ref, turned_ref):
    turned_ref[...] = grad_ref[...].T
    for at in spans(p_ref.shape[1], TILE):
        out_ref[:, at] = contract(turned_ref[...], p_ref[:, at], ((1,), (0,))).astype(bf16)


def query_part(meta, grad, p_all):
    (passages, rows), width = grad.shape, p_all.shape[1]
    return call(
        query_part_body,
        [meta, grad, p_all],
        [struct((rows, width), bf16)],
        [pltpu.VMEM((rows, passages), bf16)],
        2 * rows * passages * width,
    )[0]


def ranges_of(shapes, chosen):
    starts = [sum(shapes[:i]) for i in range(len(shapes))]
    return [slice(starts[i], starts[i] + shapes[i]) for i in chosen]


def query_rest_body(ranges, meta, grad_ref, p_ref, first_ref, *refs):
    out_refs, turned_refs = refs[: len(ranges)], refs[len(ranges) :]
    for at, ref, turned_ref in zip(ranges, out_refs, turned_refs):
        rows = slice(at.start // 2, at.stop // 2)
        turned_ref[...] = grad_ref[:, rows].T
        for span in spans(p_ref.shape[1], TILE):
            rest = contract(turned_ref[...], p_ref[:, span], ((1,), (0,))).astype(bf16)
            for i, value in enumerate((first_ref[rows, span], rest)):
                ref[:, i, :, span] = value.reshape(-1, 16, value.shape[1])


def query_rest(meta, grad, p_all, first, shapes, chosen):
    passages, width = p_all.shape
    ranges = ranges_of(shapes, chosen)

    def body(*refs):
        query_rest_body(ranges, *refs)

    parts = call(
        body,
        [meta, grad, p_all, first],
        [struct((shapes[i] // 32, 2, 16, width), bf16) for i in chosen],
        [pltpu.VMEM((shapes[i] // 2, passages), bf16) for i in chosen],
        sum(shapes[i] for i in chosen) * passages * width,
    )
    return [part.reshape(-1, width) for part in parts]


def passage_part_body(ranges, meta, grad_ref, other_ref, own_ref, q_ref, *out_refs):
    for at, ref in zip(ranges, out_refs):
        value = contract(grad_ref[at], own_ref[...], ((1,), (0,)))
        value = value + contract(other_ref[at], q_ref[...], ((1,), (0,)))
        ref[...] = value.astype(bf16)


def passage_part(meta, grad, other, q_own, q_other, shapes, chosen):
    rows, width = q_own.shape
    ranges = ranges_of(shapes, chosen)

    def body(*refs):
        passage_part_body(ranges, *refs)

    return call(
        body,
        [meta, grad, other, q_own, q_other],
        [struct((shapes[i], width), bf16) for i in chosen],
        flops=4 * rows * sum(shapes[i] for i in chosen) * width,
    )


def head_rows_body(meta, w_ref, wo_ref, keep_ref, got_ref, sems):
    half = keep_ref.shape[0]
    copies = []
    for at in spans(half, CHUNK):
        rows = pl.ds(pl.multiple_of(meta[0] * half + at.start, CHUNK), at.stop - at.start)
        to = pl.ds(at.start, at.stop - at.start)
        for from_ref, to_ref in ((w_ref, keep_ref), (wo_ref, got_ref)):
            sem = sems.at[len(copies)]
            copies.append(pltpu.make_async_copy(from_ref.at[rows], to_ref.at[to], sem))
    for copy in copies:
        copy.start()
    for copy in copies:
        copy.wait()


def head_rows(meta, weight, weight_got):
    depth, width = weight.shape
    shape = struct((depth // 2, width), bf16)
    count = 2 * len(spans(depth // 2, CHUNK))
    return call(
        head_rows_body,
        [meta, weight, weight_got],
        [shape, shape],
        [pltpu.SemaphoreType.DMA((count,))],
        hbm=(1, 2),
        vmem=4,
    )


def tangent(grad, other, unit, beyond, inv):
    radial = jnp.sum(unit * grad + beyond * other, axis=1, keepdims=True)
    return (inv * (grad - unit * radial)).astype(bf16), (inv * (other - beyond * radial)).astype(bf16)


def finish_body(
    meta, qg_ref, qgo_ref, pg_ref, pgo_ref, unit_ref, beyond_ref, inv_ref, w_ref, wo_ref,
    q_out, p_out, loss_out, here_ref, there_ref
):
    n_q = q_out.shape[0]
    part = n_q // 2
    first = meta[0] == 0
    turn = lambda rows: jnp.concatenate([rows[part:], rows[:part]], axis=0)
    grad, other = qg_ref[:n_q], qgo_ref[:n_q]
    grad, other = jnp.where(first, grad, turn(grad)), jnp.where(first, turn(other), other)
    here_ref[:n_q], there_ref[:n_q] = tangent(
        grad, other, unit_ref[:n_q], beyond_ref[:n_q], inv_ref[:n_q, :1]
    )
    own, got = qg_ref[n_q : n_q + 1, :128], qgo_ref[n_q : n_q + 1, :128]
    low, high = jnp.where(first, own, got), jnp.where(first, got, own)
    lane = lax.broadcasted_iota(jnp.int32, (1, 128), 1)
    loss_out[...] = jnp.where(lane < part, low, pltpu.roll(high, part, 1))[:, :n_q]
    for at in spans(pg_ref.shape[0], 64):
        to = slice(n_q + at.start, n_q + at.stop)
        here_ref[to], there_ref[to] = tangent(
            pg_ref[at].astype(f32), pgo_ref[at].astype(f32), unit_ref[to], beyond_ref[to], inv_ref[to, :1]
        )
    for at in spans(w_ref.shape[0], CHUNK):
        state = contract(here_ref[...], w_ref[at], ((1,), (1,)))
        state = (state + contract(there_ref[...], wo_ref[at], ((1,), (1,)))).astype(bf16)
        q_out[:, at] = state[:n_q]
        p_out[:, at] = state[n_q:]


def finish(meta, rows_in, weight, weight_got):
    out_width, width = weight.shape
    n, n_p = rows_in[4].shape[0], rows_in[2].shape[0]
    return call(
        finish_body,
        [meta, *rows_in, weight, weight_got],
        [struct((n - n_p, out_width), bf16), struct((n_p, out_width), bf16), struct((1, n - n_p))],
        [
            pltpu.VMEM((n, width), bf16),
            pltpu.VMEM((n, width), bf16),
        ],
        4 * n * out_width * width,
        free=(0, 1, 2),
    )


def per_device(query_states, passage_states, head_weight, positives, negatives, slope):
    n_y, n_x, n_z = (lax.axis_size(a) for a in ("y", "x", "z"))
    y, x, z, core = (lax.axis_index(a) for a in ("y", "x", "z", "mp"))
    q_rows, p_rows = query_states.shape[0], passage_states.shape[0]
    width = head_weight.shape[1]
    half = q_rows // 2
    slots = n_x * n_z
    column = x * n_z + z
    meta = jnp.stack([core, column, x, y, z * half]).astype(jnp.int32)

    q_proj, p_proj, square = project(meta, query_states, passage_states, head_weight)
    square_got = shifted(square, "mp", 1)
    ids = jnp.concatenate([positives[:, None], negatives], axis=1)
    per_query = ids.shape[1]
    padded = ((0, 0), (0, INDEX - per_query))
    aux = jnp.concatenate(
        [jnp.pad((ids // p_rows).astype(f32), padded), jnp.pad((ids % p_rows).astype(f32), padded)]
        + [part[:, None] for part in split_three(slope)],
        axis=1,
    )
    aux = jnp.pad(aux, ((0, 0), (0, AUX - aux.shape[1])))
    message, unit, p_embed, inv = normalize(
        meta, q_proj, p_proj, square, square_got, aux, n_z
    )
    unit_got = shifted(unit, "mp", 1)
    weight_got = shifted(after(head_weight, unit), "mp", 1)
    p_pieces = [p_embed] + [shifted(p_embed, "y", s) for s in range(1, n_y)]
    q_z = exchanged(message, "z").reshape(n_z * q_rows, width + AUX)
    q_z = after(q_z, unit_got, weight_got)
    q_near = ring_near(q_z, "x")
    q_pieces = ring_far(q_z, q_near, "x")
    q_shapes = [piece.shape[0] for piece in q_pieces]
    p_shapes = [p_rows, p_rows, p_rows // 2, p_rows // 2, p_rows] if n_y == 4 else [p_rows, p_rows]
    sent, q_other, aux, aux_other = score_sent(meta, q_pieces, p_pieces)
    got = shifted(sent, "mp", 1)
    info, count = count_positives(meta, aux, aux_other, p_rows, slots)
    counts = [count] + [shifted(count, "y", s) for s in range(1, n_y)]
    kept, named, q_own, p_all = score_kept(
        meta, info, q_pieces, p_pieces, n_y, slots, per_query
    )
    e, sums = weigh(meta, kept, got, named, info, counts, n_y, n_x, slots)
    sums = to_all(sums, ("x", "z")).reshape((slots,) + sums.shape)
    grad, loss = slopes(meta, e, sums, info, n_y, n_x, slots)
    grad_got = shifted(grad, "mp", 1)
    q_part = query_part(meta, grad, p_all)
    grad_got = after(grad_got, q_part)
    far, near = ((2, 3), (1, 4)) if len(q_shapes) > 2 else ((1,), ())
    q_parts, p_parts = [None] * len(q_shapes), [None] * len(p_shapes)

    def fill(parts, chosen, values):
        for i, value in zip(chosen, values):
            parts[i] = value

    fill(q_parts, far, query_rest(meta, grad_got, p_all, q_part, q_shapes, far))
    q_far = return_far(q_parts, "x")
    grad_next = after(grad_got, q_parts[far[0]])
    fill(p_parts, far, passage_part(meta, grad, grad_next, q_own, q_other, p_shapes, far))
    p_far = return_far(p_parts, "y")
    grad_last = after(grad_got, p_parts[far[0]])
    if near:
        fill(q_parts, near, query_rest(meta, grad_last, p_all, q_part, q_shapes, near))
    if near:
        fill(p_parts, near, passage_part(meta, grad, grad_last, q_own, q_other, p_shapes, near))
    q_leaving = join(q_parts, q_far)
    p_leaving = join(p_parts, [after(p_far[0], *q_leaving)] + p_far[1:])
    p_coming = near_coming(p_leaving, "y")
    grad_own = after(grad_got, *p_leaving)
    fill(q_parts, (0,), query_rest(meta, grad_own, p_all, q_part, q_shapes, (0,)))
    fill(p_parts, (0,), passage_part(meta, grad, grad_own, q_own, q_other, p_shapes, (0,)))
    q_part = return_near(q_parts, q_leaving, "x")
    weight, weight_got = head_rows(after(meta, *q_leaving), head_weight, weight_got)
    q_part = after(q_part, p_parts[0], *p_coming, weight, weight_got)
    back = exchanged(q_part.reshape(n_z, q_rows, width), "z")
    p_grad = total([after(p_parts[0], back)] + p_coming, bf16)
    p_grad_got = shifted(p_grad, "mp", 1)
    q_grad = total_slots(meta, back, loss, n_z * half)
    q_grad_got = shifted(q_grad, "mp", 1)
    query_grads, passage_grads, losses = finish(
        meta, (q_grad, q_grad_got, p_grad, p_grad_got, unit, unit_got, inv), weight, weight_got
    )
    return losses.reshape(q_rows), query_grads, passage_grads


def solution(mesh):
    n_dp, n_core = mesh.devices.shape
    shape = SHAPES[n_dp] + (n_core,)
    grid = Mesh(mesh.devices.reshape(shape), ("y", "x", "z", "mp"))
    dp = ("y", "x", "z")
    placed = (P(dp, None), P(dp, None), P(None, "mp"), P(dp), P(dp, None), P(dp))
    return jax.shard_map(
        per_device,
        mesh=grid,
        in_specs=placed,
        out_specs=(P(dp), P(dp, "mp"), P(dp, "mp")),
        check_vma=False,
    )
```

```python
import jax
import jax.numpy as jnp
from jax import lax
from jax.experimental import pallas as pl
from jax.experimental.pallas import tpu as pltpu
from jax.sharding import Mesh, PartitionSpec as P

sharpness = 1.0 / 0.02
bf16 = jnp.bfloat16
f32 = jnp.float32
AUX = 128
TILE = 256
CHUNK = 512
INDEX = 16
MIB = 1024 * 1024
SHAPES = {128: (4, 4, 8), 32: (4, 4, 2), 8: (2, 2, 2)}


def shifted(value, axis, shift):
    n = lax.axis_size(axis)
    return lax.ppermute(value, axis, [(i, (i + shift) % n) for i in range(n)])


def exchanged(parts, axis):
    return lax.all_to_all(parts, axis, split_axis=0, concat_axis=0, tiled=True)


def to_all(value, axis):
    n = lax.axis_size(axis)
    return exchanged(jnp.broadcast_to(value[None], (n,) + value.shape), axis)


def after(value, *others):
    return lax.optimization_barrier((value, *others))[0]


def ring_near(value, axis):
    shifts = (1, -1) if lax.axis_size(axis) > 2 else (1,)
    return [shifted(value, axis, shift) for shift in shifts]


def ring_far(value, near, axis):
    if len(near) == 1:
        return [value] + near
    cut = value.shape[0] // 2
    before, behind = near
    return [value, before, shifted(before[:cut], axis, 1), shifted(behind[cut:], axis, -1), behind]


def return_far(pieces, axis):
    if len(pieces) == 2:
        return [pieces[1]]
    return [shifted(pieces[2], axis, 1), shifted(pieces[3], axis, -1)]


def near_coming(leaving, axis):
    return [shifted(value, axis, shift) for shift, value in zip((1, -1), leaving)]


def return_near(pieces, leaving, axis):
    return total([pieces[0]] + near_coming(leaving, axis), bf16)


def split_three(value):
    high = lax.reduce_precision(value, 8, 7)
    rest = value - high
    middle = lax.reduce_precision(rest, 8, 7)
    return high, middle, rest - middle


def contract(a, b, dims):
    return lax.dot_general(a, b, (dims, ((), ())), preferred_element_type=f32)


def struct(shape, dtype=f32):
    return jax.ShapeDtypeStruct(shape, dtype)


def call(body, args, outs, scratch=(), flops=0, hbm=(), free=(), vmem=8, loose=False):
    specs, operands = [], []
    for i, arg in enumerate(args):
        if i == 0:
            specs.append(pl.BlockSpec(memory_space=pltpu.SMEM))
        elif i in hbm:
            specs.append(pl.BlockSpec(memory_space=pl.ANY))
            arg = pltpu.with_memory_space_constraint(arg, pltpu.HBM)
        else:
            specs.append(pl.BlockSpec(memory_space=pltpu.VMEM))
            arg = arg if loose else pltpu.with_memory_space_constraint(arg, pltpu.VMEM)
        operands.append(arg)
    kept = [s if loose or i in free else pltpu.VMEM(s.shape, s.dtype) for i, s in enumerate(outs)]
    return pl.pallas_call(
        body,
        in_specs=specs,
        out_specs=[pl.BlockSpec(memory_space=pltpu.VMEM)] * len(outs),
        out_shape=kept,
        scratch_shapes=list(scratch),
        compiler_params=pltpu.CompilerParams(vmem_limit_bytes=vmem * 1024 * 1024),
        cost_estimate=pl.CostEstimate(flops=flops, bytes_accessed=0, transcendentals=0),
    )(*operands)


def row_of_lane_sums(block):
    return jnp.sum(block.T, axis=0, keepdims=True)


def lanes_to_rows(row):
    return jnp.broadcast_to(row, (128, row.shape[1])).T


def rem(value, n):
    return lax.rem(value, jnp.int32(n))


def spans(rows, size):
    return [slice(at, min(at + size, rows)) for at in range(0, rows, size)]


def pieces_at(pieces):
    at = 0
    for piece in pieces:
        yield slice(at, at + piece.shape[0]), piece
        at += piece.shape[0]


def row_index(rows, columns, start=0):
    return (lax.broadcasted_iota(jnp.int32, (rows, columns), 0) + start).astype(f32)


def total_body(meta, *refs):
    value = refs[0][...].astype(f32)
    for ref in refs[1:-1]:
        value = value + ref[...].astype(f32)
    refs[-1][...] = value.astype(refs[-1].dtype)


def total(parts, dtype):
    meta = jnp.zeros((1,), jnp.int32)
    return call(total_body, [meta] + list(parts), [struct(parts[0].shape, dtype)], loose=True)[0]


def total_slots_body(size, meta, ref, loss_ref, out_ref):
    value = ref[0].astype(f32)
    for s in range(1, ref.shape[0]):
        value = value + ref[s].astype(f32)
    n = value.shape[0]
    out_ref[:n] = value
    own = loss_ref[0:1, :size]
    own = pltpu.roll(own, rem(size - meta[4], size), 1)
    out_ref[n:] = jnp.zeros((8, value.shape[1]), f32)
    out_ref[n : n + 1, :size] = own


def total_slots(meta, stacked, loss, size):
    def body(*refs):
        total_slots_body(size, *refs)

    shape = (stacked.shape[1] + 8, stacked.shape[2])
    return call(body, [meta, stacked, loss], [struct(shape)], loose=True)[0]


def join_body(meta, ahead_ref, up_ref, behind_ref, down_ref, ahead_out, behind_out):
    cut = up_ref.shape[0]
    ahead_out[:cut] = (ahead_ref[:cut].astype(f32) + up_ref[...].astype(f32)).astype(bf16)
    ahead_out[cut:] = ahead_ref[cut:]
    behind_out[:cut] = behind_ref[:cut]
    behind_out[cut:] = (behind_ref[cut:].astype(f32) + down_ref[...].astype(f32)).astype(bf16)


def join(pieces, far):
    if len(pieces) == 2:
        return far
    meta = jnp.zeros((1,), jnp.int32)
    shape = struct(pieces[1].shape, bf16)
    return call(join_body, [meta, pieces[4], far[0], pieces[1], far[1]], [shape, shape], loose=True)


def project_body(
    meta, q_ref, p_ref, w_ref, qo_ref, po_ref, square_ref, x_ref, acc_ref, head_ref, sems
):
    n_q = q_ref.shape[0]
    depth, width = w_ref.shape
    chunk = min(CHUNK, depth)
    loads = [
        pltpu.make_async_copy(q_ref, x_ref.at[pl.ds(0, n_q)], sems.at[0]),
        pltpu.make_async_copy(p_ref, x_ref.at[pl.ds(n_q, p_ref.shape[0])], sems.at[1]),
    ]
    blocks = []
    for at in spans(depth, chunk):
        rows = pl.ds(at.start, chunk)
        blocks.append(pltpu.make_async_copy(w_ref.at[rows], head_ref.at[rows], sems.at[2 + len(blocks)]))
    for load in loads:
        load.start()
    for block in blocks:
        block.start()
    for load in loads:
        load.wait()
    for i, at in enumerate(spans(depth, chunk)):
        blocks[i].wait()
        part = contract(x_ref[:, at], head_ref[at], ((1,), (0,)))
        acc_ref[...] = part if i == 0 else acc_ref[...] + part
    qo_ref[...] = acc_ref[:n_q]
    po_ref[...] = acc_ref[n_q:]
    square = jnp.zeros((acc_ref.shape[0], 128), f32)
    for at in range(0, width, 128):
        block = acc_ref[:, at : at + 128]
        square = square + block * block
    padded = jnp.concatenate([square[:n_q], jnp.zeros((128 - n_q, 128), f32)], axis=0)
    square_ref[:, :128] = row_of_lane_sums(padded)
    square_ref[:, 128:] = row_of_lane_sums(square[n_q:])


def project(meta, queries, passages, weight):
    n_q, n_p, (depth, width) = queries.shape[0], passages.shape[0], weight.shape
    copies = 2 + depth // min(CHUNK, depth)
    return call(
        project_body,
        [meta, queries, passages, weight],
        [struct((n_q, width)), struct((n_p, width)), struct((1, 128 + n_p))],
        [
            pltpu.VMEM((n_q + n_p, depth), bf16),
            pltpu.VMEM((n_q + n_p, width), f32),
            pltpu.VMEM((depth, width), bf16),
            pltpu.SemaphoreType.DMA((copies,)),
        ],
        2 * (n_q + n_p) * depth * width,
        hbm=(1, 2, 3),
        vmem=18,
    )


def normalize_body(
    meta, q_ref, p_ref, own_ref, got_ref, aux_ref, message_ref, unit_ref, embed_ref, inv_ref
):
    n_q, width = q_ref.shape
    inv = lanes_to_rows(lax.rsqrt(own_ref[...] + got_ref[...] + 1e-06))
    inv_ref[:n_q] = inv[:n_q]
    inv_ref[n_q:] = inv[128:]
    q_unit = q_ref[...] * inv[:n_q, :1]
    p_unit = p_ref[...] * inv[128:, :1]
    unit_ref[:n_q] = q_unit
    unit_ref[n_q:] = p_unit
    embed_ref[...] = p_unit.astype(bf16)
    half = n_q // 2
    first = meta[0] == 0

    def store(columns, value):
        top, bottom = value[:half], value[half:]
        upper, lower = jnp.where(first, top, bottom), jnp.where(first, bottom, top)
        for s in range(message_ref.shape[0]):
            message_ref[s, :half, columns] = upper.astype(bf16)
            message_ref[s, half:, columns] = lower.astype(bf16)

    store(slice(0, width), q_unit)
    store(slice(width, width + AUX), aux_ref[...])


def normalize(meta, q_proj, p_proj, square, square_got, aux, copies):
    (n_q, width), n_p = q_proj.shape, p_proj.shape[0]
    return call(
        normalize_body,
        [meta, q_proj, p_proj, square, square_got, aux],
        [
            struct((copies, n_q, width + AUX), bf16),
            struct((n_q + n_p, width)),
            struct((n_p, width), bf16),
            struct((n_q + n_p, 128)),
        ],
    )


def owner_of(meta, line, n_y, slots):
    return (rem(meta[3] - line + n_y, n_y) * slots + meta[1]).astype(f32)


def side_rows(ref, i, width):
    value = ref[:, :width].reshape(-1, 2, 16, width)
    return value[:, i].reshape(value.shape[0] * 16, width)


def score_sent_body(n_pieces, meta, *refs):
    q_refs, p_refs = refs[: n_pieces[0]], refs[n_pieces[0] : sum(n_pieces)]
    score_ref, other_ref, aux_ref, aux_other_ref = refs[sum(n_pieces) :]
    width = other_ref.shape[1]
    at = 0
    for ref in q_refs:
        rows = ref.shape[0] // 2
        other_ref[at : at + rows] = side_rows(ref, 1, width)
        value = ref[:, width:].reshape(-1, 2, 16, AUX)
        for i, aux in enumerate((aux_ref, aux_other_ref)):
            aux[at : at + rows] = value[:, i].reshape(rows, AUX).astype(f32)
        at += rows
    for at, ref in pieces_at(p_refs):
        score_ref[at] = contract(ref[...], other_ref[...], ((1,), (1,)))


def score_sent(meta, q_pieces, p_pieces):
    width = p_pieces[0].shape[1]
    passages = sum(p.shape[0] for p in p_pieces)
    rows = sum(q.shape[0] for q in q_pieces) // 2

    def body(*refs):
        score_sent_body((len(q_pieces), len(p_pieces)), *refs)

    return call(
        body,
        [meta] + q_pieces + p_pieces,
        [
            struct((passages, rows)),
            struct((rows, width), bf16),
            struct((rows, AUX)),
            struct((rows, AUX)),
        ],
        flops=2 * rows * passages * width,
    )


def count_body(slots, meta, aux_ref, other_ref, info_ref, count_ref):
    block = count_ref.shape[1]
    info_ref[...] = aux_ref[...].T
    owners = (lax.broadcasted_iota(jnp.int32, (8, 1), 0) * slots + meta[1]).astype(f32)
    count = jnp.zeros(count_ref.shape, f32)
    for info in (info_ref[...], other_ref[...].T):
        owned = (info[0:1] == owners).astype(f32).astype(bf16)
        placed = info[INDEX : INDEX + 1] == row_index(block, info.shape[1])
        count = count + contract(owned, placed.astype(f32).astype(bf16), ((1,), (1,)))
    count_ref[...] = count


def count_positives(meta, aux, aux_other, block, slots):
    def body(*refs):
        count_body(slots, *refs)

    return call(
        body, [meta, aux, aux_other], [struct((AUX, aux.shape[0])), struct((8, block))]
    )


def score_kept_body(n_y, slots, per_query, n_pieces, meta, info_ref, *refs):
    q_refs, p_refs = refs[: n_pieces[0]], refs[n_pieces[0] : sum(n_pieces)]
    score_ref, weight_ref, q_ref, p_ref = refs[sum(n_pieces) :]
    passages, rows = score_ref.shape
    block = passages // n_y
    at = 0
    for ref in q_refs:
        n = ref.shape[0] // 2
        q_ref[at : at + n] = side_rows(ref, 0, q_ref.shape[1])
        at += n
    for at, ref in pieces_at(p_refs):
        p_ref[at] = ref[...]
    for line in range(n_y):
        owner = owner_of(meta, line, n_y, slots)
        place = jnp.where(info_ref[:INDEX] == owner, info_ref[INDEX : 2 * INDEX], -1.0)
        at = slice(line * block, (line + 1) * block)
        score_ref[at] = contract(p_ref[at], q_ref[...], ((1,), (1,)))
        for span in spans(block, 32):
            row = row_index(span.stop - span.start, rows, span.start)
            weight = (place[1:2] == row).astype(f32)
            for k in range(2, per_query):
                weight = weight + (place[k : k + 1] == row).astype(f32)
            weight_ref[line * block + span.start : line * block + span.stop] = weight


def score_kept(meta, info, q_pieces, p_pieces, n_y, slots, per_query):
    width = p_pieces[0].shape[1]
    passages = sum(p.shape[0] for p in p_pieces)
    rows = sum(q.shape[0] for q in q_pieces) // 2

    def body(*refs):
        score_kept_body(n_y, slots, per_query, (len(q_pieces), len(p_pieces)), *refs)

    return call(
        body,
        [meta, info] + q_pieces + p_pieces,
        [
            struct((passages, rows)),
            struct((passages, rows)),
            struct((rows, width), bf16),
            struct((passages, width), bf16),
        ],
        flops=4 * rows * passages * width,
    )


def positive_place(meta, line, n_y, slots, info_ref):
    owner = owner_of(meta, line, n_y, slots)
    return jnp.where(info_ref[0:1] == owner, info_ref[INDEX : INDEX + 1], -1.0)


def turned_slots(meta, n_x, rows):
    size = rows // n_x
    for s in range(n_x):
        start = pl.multiple_of(rem(meta[2] - s + n_x, n_x) * size, size)
        yield slice(s * size, (s + 1) * size), pl.ds(start, size)


def weigh_body(
    n_y, n_x, slots, meta, kept_ref, got_ref, weight_ref, info_ref, *rest_refs
):
    counts_ref, (e_ref, sum_ref) = rest_refs[:-2], rest_refs[-2:]
    passages, rows = kept_ref.shape
    block = passages // n_y
    counts = counts_ref[0][...]
    for ref in counts_ref[1:]:
        counts = counts + ref[...]
    rest = jnp.zeros((128 - counts.shape[0], block), f32)
    counts = jnp.concatenate([counts, rest], axis=0).T
    lane = lax.broadcasted_iota(jnp.int32, (1, 128), 1)
    sums = [jnp.zeros((8, rows), f32), jnp.zeros((8, rows), f32)]
    for line in range(n_y):
        mine = lane == rem(meta[3] - line + n_y, n_y)
        count = jnp.sum(jnp.where(mine, counts, 0.0), axis=1, keepdims=True)
        place = positive_place(meta, line, n_y, slots, info_ref)
        for span in spans(block, 32):
            at = slice(line * block + span.start, line * block + span.stop)
            score = (kept_ref[at] + got_ref[at]) * sharpness
            weighted = (weight_ref[at] + count[span]) * jnp.exp(score)
            e_ref[at] = weighted
            own = jnp.where(place == row_index(span.stop - span.start, rows, span.start), score, 0.0)
            sums[0] = sums[0] + jnp.sum(weighted.reshape(-1, 8, rows), axis=0)
            sums[1] = sums[1] + jnp.sum(own.reshape(-1, 8, rows), axis=0)
    for i in range(2):
        row = jnp.sum(sums[i], axis=0, keepdims=True)
        for here, there in turned_slots(meta, n_x, rows):
            sum_ref[i : i + 1, there] = row[:, here]


def weigh(meta, kept, got, weight, info, counts, n_y, n_x, slots):
    passages, rows = kept.shape

    def body(*refs):
        weigh_body(n_y, n_x, slots, *refs)

    return call(
        body,
        [meta, kept, got, weight, info, *counts],
        [struct((passages, rows)), struct((2, rows))],
    )


def slope_body(n_y, n_x, slots, meta, e_ref, sums_ref, info_ref, grad_ref, loss_ref, scale_ref, inv_ref):
    passages, rows = e_ref.shape
    block = passages // n_y
    loss_ref[...] = jnp.sum(sums_ref[...], axis=0)
    for here, there in turned_slots(meta, n_x, rows):
        inv_ref[:, here] = loss_ref[0:1, there]
    for here, there in turned_slots(meta, n_x, rows):
        scale_ref[:, here] = loss_ref[1:2, there]
    sums = inv_ref[...]
    loss_ref[0:1] = jnp.log(sums) - scale_ref[...]
    inv = 1.0 / sums
    base = 2 * INDEX
    scale = (info_ref[base : base + 1] + info_ref[base + 1 : base + 2]) + info_ref[base + 2 : base + 3]
    scale = scale * sharpness
    for line in range(n_y):
        place = positive_place(meta, line, n_y, slots, info_ref)
        for span in spans(block, 32):
            at = slice(line * block + span.start, line * block + span.stop)
            match = (place == row_index(span.stop - span.start, rows, span.start)).astype(f32)
            grad_ref[at] = (scale * (e_ref[at] * inv - match)).astype(bf16)


def slopes(meta, e, sums, info, n_y, n_x, slots):
    passages, rows = e.shape

    def body(*refs):
        slope_body(n_y, n_x, slots, *refs)

    return call(
        body,
        [meta, e, sums, info],
        [struct((passages, rows), bf16), struct((2, rows))],
        [pltpu.VMEM((1, rows), f32), pltpu.VMEM((1, rows), f32)],
    )


def query_part_body(meta, grad_ref, p_ref, out_ref, turned_ref):
    turned_ref[...] = grad_ref[...].T
    for at in spans(p_ref.shape[1], TILE):
        out_ref[:, at] = contract(turned_ref[...], p_ref[:, at], ((1,), (0,))).astype(bf16)


def query_part(meta, grad, p_all):
    (passages, rows), width = grad.shape, p_all.shape[1]
    return call(
        query_part_body,
        [meta, grad, p_all],
        [struct((rows, width), bf16)],
        [pltpu.VMEM((rows, passages), bf16)],
        2 * rows * passages * width,
    )[0]


def ranges_of(shapes, chosen):
    starts = [sum(shapes[:i]) for i in range(len(shapes))]
    return [slice(starts[i], starts[i] + shapes[i]) for i in chosen]


def query_rest_body(ranges, meta, grad_ref, p_ref, first_ref, *refs):
    out_refs, turned_refs = refs[: len(ranges)], refs[len(ranges) :]
    for at, ref, turned_ref in zip(ranges, out_refs, turned_refs):
        rows = slice(at.start // 2, at.stop // 2)
        turned_ref[...] = grad_ref[:, rows].T
        for span in spans(p_ref.shape[1], TILE):
            rest = contract(turned_ref[...], p_ref[:, span], ((1,), (0,))).astype(bf16)
            for i, value in enumerate((first_ref[rows, span], rest)):
                ref[:, i, :, span] = value.reshape(-1, 16, value.shape[1])


def query_rest(meta, grad, p_all, first, shapes, chosen):
    passages, width = p_all.shape
    ranges = ranges_of(shapes, chosen)

    def body(*refs):
        query_rest_body(ranges, *refs)

    parts = call(
        body,
        [meta, grad, p_all, first],
        [struct((shapes[i] // 32, 2, 16, width), bf16) for i in chosen],
        [pltpu.VMEM((shapes[i] // 2, passages), bf16) for i in chosen],
        sum(shapes[i] for i in chosen) * passages * width,
    )
    return [part.reshape(-1, width) for part in parts]


def passage_part_body(ranges, meta, grad_ref, other_ref, own_ref, q_ref, *out_refs):
    for at, ref in zip(ranges, out_refs):
        value = contract(grad_ref[at], own_ref[...], ((1,), (0,)))
        value = value + contract(other_ref[at], q_ref[...], ((1,), (0,)))
        ref[...] = value.astype(bf16)


def passage_part(meta, grad, other, q_own, q_other, shapes, chosen):
    rows, width = q_own.shape
    ranges = ranges_of(shapes, chosen)

    def body(*refs):
        passage_part_body(ranges, *refs)

    return call(
        body,
        [meta, grad, other, q_own, q_other],
        [struct((shapes[i], width), bf16) for i in chosen],
        flops=4 * rows * sum(shapes[i] for i in chosen) * width,
    )


def head_rows_body(meta, w_ref, wo_ref, keep_ref, got_ref, sems):
    half = keep_ref.shape[0]
    copies = []
    for at in spans(half, CHUNK):
        rows = pl.ds(pl.multiple_of(meta[0] * half + at.start, CHUNK), at.stop - at.start)
        to = pl.ds(at.start, at.stop - at.start)
        for from_ref, to_ref in ((w_ref, keep_ref), (wo_ref, got_ref)):
            sem = sems.at[len(copies)]
            copies.append(pltpu.make_async_copy(from_ref.at[rows], to_ref.at[to], sem))
    for copy in copies:
        copy.start()
    for copy in copies:
        copy.wait()


def head_rows(meta, weight, weight_got):
    depth, width = weight.shape
    shape = struct((depth // 2, width), bf16)
    count = 2 * len(spans(depth // 2, CHUNK))
    return call(
        head_rows_body,
        [meta, weight, weight_got],
        [shape, shape],
        [pltpu.SemaphoreType.DMA((count,))],
        hbm=(1, 2),
        vmem=4,
    )


def tangent(grad, other, unit, beyond, inv):
    radial = jnp.sum(unit * grad + beyond * other, axis=1, keepdims=True)
    return (inv * (grad - unit * radial)).astype(bf16), (inv * (other - beyond * radial)).astype(bf16)


def finish_body(
    meta, qg_ref, qgo_ref, pg_ref, pgo_ref, unit_ref, beyond_ref, inv_ref, w_ref, wo_ref,
    q_out, p_out, loss_out, here_ref, there_ref
):
    n_q = q_out.shape[0]
    part = n_q // 2
    first = meta[0] == 0
    turn = lambda rows: jnp.concatenate([rows[part:], rows[:part]], axis=0)
    grad, other = qg_ref[:n_q], qgo_ref[:n_q]
    grad, other = jnp.where(first, grad, turn(grad)), jnp.where(first, turn(other), other)
    here_ref[:n_q], there_ref[:n_q] = tangent(
        grad, other, unit_ref[:n_q], beyond_ref[:n_q], inv_ref[:n_q, :1]
    )
    own, got = qg_ref[n_q : n_q + 1, :128], qgo_ref[n_q : n_q + 1, :128]
    low, high = jnp.where(first, own, got), jnp.where(first, got, own)
    lane = lax.broadcasted_iota(jnp.int32, (1, 128), 1)
    loss_out[...] = jnp.where(lane < part, low, pltpu.roll(high, part, 1))[:, :n_q]
    for at in spans(pg_ref.shape[0], 64):
        to = slice(n_q + at.start, n_q + at.stop)
        here_ref[to], there_ref[to] = tangent(
            pg_ref[at].astype(f32), pgo_ref[at].astype(f32), unit_ref[to], beyond_ref[to], inv_ref[to, :1]
        )
    for at in spans(w_ref.shape[0], CHUNK):
        state = contract(here_ref[...], w_ref[at], ((1,), (1,)))
        state = (state + contract(there_ref[...], wo_ref[at], ((1,), (1,)))).astype(bf16)
        q_out[:, at] = state[:n_q]
        p_out[:, at] = state[n_q:]


def finish(meta, rows_in, weight, weight_got):
    out_width, width = weight.shape
    n, n_p = rows_in[4].shape[0], rows_in[2].shape[0]
    return call(
        finish_body,
        [meta, *rows_in, weight, weight_got],
        [struct((n - n_p, out_width), bf16), struct((n_p, out_width), bf16), struct((1, n - n_p))],
        [
            pltpu.VMEM((n, width), bf16),
            pltpu.VMEM((n, width), bf16),
        ],
        4 * n * out_width * width,
        free=(0, 1, 2),
    )


def per_device(query_states, passage_states, head_weight, positives, negatives, slope):
    n_y, n_x, n_z = (lax.axis_size(a) for a in ("y", "x", "z"))
    y, x, z, core = (lax.axis_index(a) for a in ("y", "x", "z", "mp"))
    q_rows, p_rows = query_states.shape[0], passage_states.shape[0]
    width = head_weight.shape[1]
    half = q_rows // 2
    slots = n_x * n_z
    column = x * n_z + z
    meta = jnp.stack([core, column, x, y, z * half]).astype(jnp.int32)

    q_proj, p_proj, square = project(meta, query_states, passage_states, head_weight)
    square_got = shifted(square, "mp", 1)
    ids = jnp.concatenate([positives[:, None], negatives], axis=1)
    per_query = ids.shape[1]
    padded = ((0, 0), (0, INDEX - per_query))
    aux = jnp.concatenate(
        [jnp.pad((ids // p_rows).astype(f32), padded), jnp.pad((ids % p_rows).astype(f32), padded)]
        + [part[:, None] for part in split_three(slope)],
        axis=1,
    )
    aux = jnp.pad(aux, ((0, 0), (0, AUX - aux.shape[1])))
    message, unit, p_embed, inv = normalize(
        meta, q_proj, p_proj, square, square_got, aux, n_z
    )
    unit_got = shifted(unit, "mp", 1)
    weight_got = shifted(after(head_weight, unit), "mp", 1)
    p_near = ring_near(p_embed, "y")
    q_z = exchanged(message, "z").reshape(n_z * q_rows, width + AUX)
    q_z = after(q_z, unit_got, weight_got)
    q_near = ring_near(q_z, "x")
    q_pieces = ring_far(q_z, q_near, "x")
    p_pieces = ring_far(p_embed, [after(piece, *q_near) for piece in p_near], "y")
    q_shapes = [piece.shape[0] for piece in q_pieces]
    p_shapes = [p_rows, p_rows, p_rows // 2, p_rows // 2, p_rows] if n_y == 4 else [p_rows, p_rows]
    sent, q_other, aux, aux_other = score_sent(meta, q_pieces, p_pieces)
    got = shifted(sent, "mp", 1)
    info, count = count_positives(meta, aux, aux_other, p_rows, slots)
    counts = [count] + [shifted(count, "y", s) for s in range(1, n_y)]
    kept, named, q_own, p_all = score_kept(
        meta, info, q_pieces, p_pieces, n_y, slots, per_query
    )
    e, sums = weigh(meta, kept, got, named, info, counts, n_y, n_x, slots)
    sums = to_all(sums, ("x", "z")).reshape((slots,) + sums.shape)
    grad, loss = slopes(meta, e, sums, info, n_y, n_x, slots)
    grad_got = shifted(grad, "mp", 1)
    q_part = query_part(meta, grad, p_all)
    grad_got = after(grad_got, q_part)
    far, near = ((2, 3), (1, 4)) if len(q_shapes) > 2 else ((1,), ())
    q_parts, p_parts = [None] * len(q_shapes), [None] * len(p_shapes)

    def fill(parts, chosen, values):
        for i, value in zip(chosen, values):
            parts[i] = value

    fill(q_parts, far, query_rest(meta, grad_got, p_all, q_part, q_shapes, far))
    q_far = return_far(q_parts, "x")
    grad_next = after(grad_got, q_parts[far[0]])
    fill(p_parts, far, passage_part(meta, grad, grad_next, q_own, q_other, p_shapes, far))
    p_far = return_far(p_parts, "y")
    grad_last = after(grad_got, p_parts[far[0]])
    if near:
        fill(q_parts, near, query_rest(meta, grad_last, p_all, q_part, q_shapes, near))
    if near:
        fill(p_parts, near, passage_part(meta, grad, grad_last, q_own, q_other, p_shapes, near))
    q_leaving = join(q_parts, q_far)
    p_leaving = join(p_parts, [after(p_far[0], *q_leaving)] + p_far[1:])
    p_coming = near_coming(p_leaving, "y")
    grad_own = after(grad_got, *p_leaving)
    fill(q_parts, (0,), query_rest(meta, grad_own, p_all, q_part, q_shapes, (0,)))
    fill(p_parts, (0,), passage_part(meta, grad, grad_own, q_own, q_other, p_shapes, (0,)))
    q_part = return_near(q_parts, q_leaving, "x")
    weight, weight_got = head_rows(after(meta, *q_leaving), head_weight, weight_got)
    q_part = after(q_part, p_parts[0], *p_coming, weight, weight_got)
    back = exchanged(q_part.reshape(n_z, q_rows, width), "z")
    p_grad = total([after(p_parts[0], back)] + p_coming, bf16)
    p_grad_got = shifted(p_grad, "mp", 1)
    q_grad = total_slots(meta, back, loss, n_z * half)
    q_grad_got = shifted(q_grad, "mp", 1)
    query_grads, passage_grads, losses = finish(
        meta, (q_grad, q_grad_got, p_grad, p_grad_got, unit, unit_got, inv), weight, weight_got
    )
    return losses.reshape(q_rows), query_grads, passage_grads


def solution(mesh):
    n_dp, n_core = mesh.devices.shape
    shape = SHAPES[n_dp] + (n_core,)
    grid = Mesh(mesh.devices.reshape(shape), ("y", "x", "z", "mp"))
    dp = ("y", "x", "z")
    placed = (P(dp, None), P(dp, None), P(None, "mp"), P(dp), P(dp, None), P(dp))
    return jax.shard_map(
        per_device,
        mesh=grid,
        in_specs=placed,
        out_specs=(P(dp), P(dp, "mp"), P(dp, "mp")),
        check_vma=False,
    )
```
